128 devices in a mesh: section: 2 (over core), ctx: 16 (over y, x), expert: 4 (over z).
Axes of the slice: x: 4, y: 4, z: 4, core: 2. Of those that a mesh axis runs over, the one named last changes fastest.
Arguments:
- tokens: bfloat16 [2, 4, 1024, 1024], P(None, 'expert', 'ctx'), may hold values from -6 to 6
- positions: int32 [2, 4, 1024], P(None, 'expert', 'ctx'), may hold values from 0 to 1022, as said below
- expert_ids: int32 [2, 2, 4, 1024, 8], P('section', None, 'expert', 'ctx'), may hold values from 0 to 31, all different within a row; in each aligned block of 64 rows (0 to 63, 64 to 127, ..., all dimensions but the last counted through in order) at most 17 rows name the same one
- cotangent: bfloat16 [2, 4, 1024, 1024], P(None, 'expert', 'ctx'), may hold values from -6 to 6
- first_gain: float32 [2, 1024], P('section'), may hold values from 0.5 to 1.5
- query_weight: bfloat16 [2, 1024, 1024], P('section'), may hold values from -0.1875 to 0.1875
- key_value_matrix: bfloat16 [2, 1024, 1024], P('section'), may hold values from -0.1875 to 0.1875
- output_weight: bfloat16 [2, 1024, 1024], P('section'), may hold values from -4 to 4
- second_gain: float32 [2, 1024], P('section'), may hold values from 0.5 to 1.5
- router_weight: bfloat16 [2, 1024, 32], P('section'), may hold values from -0.09375 to 0.09375
- expert_in: bfloat16 [2, 32, 1024, 1024], P('section', 'expert'), may hold values from -0.1875 to 0.1875
- expert_out: bfloat16 [2, 32, 1024, 512], P('section', 'expert'), may hold values from -0.75 to 0.75
Outputs:
- layer_out: bfloat16 [2, 2, 4, 1024, 1024], P('section', None, 'expert', 'ctx')
- input_grad: float32 [2, 2, 4, 1024, 1024], P('section', None, 'expert', 'ctx')
- grad_first_gain: float32 [2, 1024], P('section', ('ctx', 'expert'))
- grad_query: float32 [2, 1024, 1024], P('section', ('ctx', 'expert'))
- grad_key_value: float32 [2, 1024, 1024], P('section', ('ctx', 'expert'))
- grad_output: float32 [2, 1024, 1024], P('section', ('ctx', 'expert'))
- grad_second_gain: float32 [2, 1024], P('section', ('ctx', 'expert'))
- grad_router: float32 [2, 1024, 32], P('section', ('ctx', 'expert'))
- grad_expert_in: float32 [2, 32, 1024, 1024], P('section', 'expert', 'ctx')
- grad_expert_out: float32 [2, 32, 1024, 512], P('section', 'expert', 'ctx')
The draws below stay inside these ranges and needn't reach their ends.
Inputs may be any that keep to these rules, and one draw needn't show every extreme that they name: positions count 0, 1, 2, ... within each packed document of a sequence: a first document of 1 to 63 tokens, a long middle one, and a last one of at most 63 tokens, possibly absent; in every draw one sequence has a first document of one token and no last one. `expert_ids`: each token names 8 different experts; in the 64 tokens of one sequence on one device (aligned blocks of 64 rows) for one layer and micro-batch no expert is named more than 17 times, a bound that some block reaches.
All inputs are finite; a program needn't handle non-finite values.
Results may differ from the reference program's by a relative error of at most 0.025.
Values may be sent and summed in bfloat16 or wider, within the bound.
No kernel may reach another device: no remote copies, remote signals or barrier semaphores. Data moves between devices by JAX's collectives and lax.ppermute only.
A program may use at most 320 MiB of HBM per device.

```python
import math
import jax
import jax.numpy as jnp
import numpy as np
from jax import lax

MODEL_WIDTH = 1024
QUERY_HEADS = 16
KEY_VALUE_HEADS = 8
HEAD_WIDTH = 64
FFE = 512
TOP = 8
MICRO = 2
LAYER_COUNT = 2
NSEQ = 4
SEQ = 1024
SPAN = 64
EXPERTS = 32
CAP = 17
N_CTX = 16


def draw_positions(key, part):
    key = jax.random.fold_in(key, 7)
    first_key, last_key, pick_key = jax.random.split(key, 3)
    opening = jax.random.randint(first_key, (MICRO, NSEQ, 1), 1, SPAN)
    closing = jax.random.randint(last_key, (MICRO, NSEQ, 1), 0, SPAN)
    special = jax.random.randint(pick_key, (), 0, MICRO * NSEQ)
    flat_at = jnp.arange(MICRO * NSEQ, dtype=jnp.int32).reshape(MICRO, NSEQ, 1)
    opening = jnp.where(flat_at == special, 1, opening)
    closing = jnp.where(flat_at == special, 0, closing)
    token_at = jnp.arange(SEQ, dtype=jnp.int32)[None, None, :]
    tail_start = SEQ - closing
    begins = jnp.where(token_at < opening, 0, jnp.where(token_at < tail_start, opening, tail_start))
    return (token_at - begins).astype(jnp.int32)


def block_levels(stream_key, shape, shards, least, high):
    def one(dim, shards_of):
        draws = jax.random.uniform(jax.random.fold_in(jax.random.fold_in(stream_key, 6), dim), (shards_of,), jnp.float32, least / len(shards), high / len(shards))
        return jnp.repeat(jnp.exp(draws), shape[dim] // shards_of).reshape((-1,) + (1,) * (len(shape) - dim - 1))

    level = one(*shards[0])
    for cut in shards[1:]:
        level = level * one(*cut)
    return level


def shared_out(key, own, number, rows, number_of, top, most, skew):
    order = jax.random.permutation(key, number_of)
    crowded, common = shares(number_of, rows * top, most, skew, True), shares(number_of, rows * top, most, skew, False)
    places = jnp.arange(number_of)

    def named(lengths, turn):
        used = int((lengths > 0).sum())
        fixed = max(1, used // 4)
        moved = fixed + (places - fixed + turn * (used - fixed)) % max(1, number_of - fixed)
        return jnp.zeros((number_of,), jnp.int32).at[order[jnp.where(places < fixed, places, moved)]].set(jnp.asarray(lengths, jnp.int32))

    lengths = jnp.where(number % 4 == 0, named(crowded, number // 4), named(common, number - number // 4 - 1))
    mixed = jax.random.permutation(jax.random.fold_in(own, 3), number_of)
    giver, sink = mixed[0:number_of // 2 * 2:2], mixed[1:number_of // 2 * 2:2]
    margin = jnp.minimum(lengths[giver] - 1, most - lengths[sink]) // 2
    margin = jnp.where((giver == order[0]) | (sink == order[0]) | (lengths[sink] == 0), 0, jnp.maximum(margin, 0))
    moved = jax.random.randint(jax.random.fold_in(own, 4), (number_of // 2,), 0, 1 << 20) % (margin + 1)
    lengths = lengths.at[giver].add(-moved).at[sink].add(moved)
    items = jnp.searchsorted(jnp.cumsum(lengths), jnp.arange(rows * top), side="right").astype(jnp.int32)
    grid = items.reshape(top, rows).T
    grid = grid[jax.random.permutation(jax.random.fold_in(own, 1), rows)]
    turn = jax.random.randint(jax.random.fold_in(own, 2), (rows, 1), 0, top)
    return jnp.take_along_axis(grid, (jnp.arange(top)[None, :] + turn) % top, axis=1)


def shares(amount, total, most, slope, full):
    weights = [(1 << 20) // math.isqrt(rank ** slope) + 1 for rank in range(1, amount + 1)]
    largest = most if full else min(most, max(-(-total // amount), total * weights[0] // sum(weights)))
    least = 1 if total - largest >= amount - 1 else 0
    counts, rest = [largest] + [least] * (amount - 1), total - largest - least * (amount - 1)
    while rest > 0:
        free = [i for i in range(1, amount) if counts[i] < largest] or [i for i in range(1, amount) if counts[i] < most]
        mass, budget = sum([weights[i] for i in free]), rest
        for i in free:
            addition = min(most - counts[i], max(1, budget * weights[i] // mass), rest)
            counts[i] = counts[i] + addition
            rest = rest - addition
    return np.array(counts)


def gaussian(rng, dims, scale, bound, cuts=(), held_as=jnp.bfloat16):
    array = jax.random.normal(rng, dims, jnp.float32) * scale
    if len(cuts) > 0:
        array = block_levels(rng, dims, cuts, -0.22, 0.18) * array
    return jnp.clip(array, min=-bound, max=bound).astype(held_as)


def setup_inputs(seed: int = 0) -> dict:
    key_of = jax.random.split(jax.random.key(seed), 13)
    tokens = gaussian(key_of[0], (MICRO, NSEQ, SEQ, MODEL_WIDTH), 1.0, 6.0, ((1, 4), (2, 16)))
    positions = draw_positions(jax.random.fold_in(key_of[12], 71), 0)
    expert_ids_keys = jax.random.split(jax.random.fold_in(key_of[2], 1), LAYER_COUNT * MICRO * NSEQ * SEQ // SPAN)
    expert_ids_turns = jax.random.permutation(jax.random.fold_in(key_of[2], 3), LAYER_COUNT * MICRO * NSEQ * SEQ // SPAN)
    expert_ids = jax.vmap(lambda own, number: shared_out(jax.random.fold_in(key_of[2], 2), own, number, SPAN, EXPERTS, TOP, CAP, 1))(expert_ids_keys, expert_ids_turns).reshape((LAYER_COUNT, MICRO, NSEQ, SEQ, TOP))
    cotangent = gaussian(key_of[3], (MICRO, NSEQ, SEQ, MODEL_WIDTH), 1.0, 6.0, ((1, 4), (2, 16)))
    first_gain = jnp.clip(1.0 + 0.1 * jax.random.normal(key_of[4], (LAYER_COUNT, MODEL_WIDTH), jnp.float32), 0.5, 1.5)
    query_weight = gaussian(key_of[5], (LAYER_COUNT, MODEL_WIDTH, QUERY_HEADS * HEAD_WIDTH), MODEL_WIDTH ** -0.5, 0.1875, ((0, 2),))
    key_value_matrix = gaussian(key_of[6], (LAYER_COUNT, MODEL_WIDTH, 2 * KEY_VALUE_HEADS * HEAD_WIDTH), MODEL_WIDTH ** -0.5, 0.1875, ((0, 2),))
    output_weight = gaussian(key_of[7], (LAYER_COUNT, QUERY_HEADS * HEAD_WIDTH, MODEL_WIDTH), (max(1, 2 * QUERY_HEADS * HEAD_WIDTH // SEQ)) ** -0.5, 4.0, ((0, 2),))
    second_gain = jnp.clip(1.0 + 0.1 * jax.random.normal(key_of[8], (LAYER_COUNT, MODEL_WIDTH), jnp.float32), 0.5, 1.5)
    router_weight = gaussian(key_of[9], (LAYER_COUNT, MODEL_WIDTH, EXPERTS), (4 * MODEL_WIDTH) ** -0.5, 0.09375, ((0, 2),))
    expert_in = gaussian(key_of[10], (LAYER_COUNT, EXPERTS, MODEL_WIDTH, 2 * FFE), MODEL_WIDTH ** -0.5, 0.1875, ((0, 2), (1, 4)))
    expert_out = gaussian(key_of[11], (LAYER_COUNT, EXPERTS, MODEL_WIDTH, FFE), (max(1, FFE // 8)) ** -0.5, 0.75, ((0, 2), (1, 4)))
    return dict(tokens=tokens, positions=positions, expert_ids=expert_ids, cotangent=cotangent, first_gain=first_gain, query_weight=query_weight, key_value_matrix=key_value_matrix, output_weight=output_weight, second_gain=second_gain, router_weight=router_weight, expert_in=expert_in, expert_out=expert_out)


@jax.custom_vjp
def low(v):
    return lax.optimization_barrier(v.astype(jnp.bfloat16)).astype(jnp.float32)

@jax.custom_vjp
def reduced_backward(v):
    return v

def low_keep(v):
    return (low(v), None)

def low_pass(kept, grad):
    return (grad,)

def back_keep(v):
    return (v, None)

def back_low(kept, grad):
    return (low(grad),)
low.defvjp(low_keep, low_pass)
reduced_backward.defvjp(back_keep, back_low)
epsilon = 1e-06
rope_base = 10000.0
masked = -1e+30

def product_highest(left, right):
    return jnp.dot(left, right, precision=lax.Precision.HIGHEST, preferred_element_type=jnp.float32)

def norm_apply(values, gain_row):
    return values * lax.rsqrt(lax.optimization_barrier(jnp.mean(values * values, axis=-1, keepdims=True)) + epsilon) * gain_row

def softmax_rows(scores):
    largest = lax.optimization_barrier(jnp.max(scores, axis=-1, keepdims=True))
    raised = jnp.exp(scores - largest)
    return raised / lax.optimization_barrier(jnp.sum(raised, axis=-1, keepdims=True))

def swiglu(gate_up):
    half_width = gate_up.shape[-1] // 2
    gate_part = gate_up[..., :half_width]
    return gate_part * jax.nn.sigmoid(gate_part) * gate_up[..., half_width:]

def rotary_apply(values, cosine_table, sine_table):
    half_width = values.shape[-1] // 2
    first_half = values[..., :half_width]
    second_half = values[..., half_width:]
    return jnp.concatenate([first_half * cosine_table - second_half * sine_table, second_half * cosine_table + first_half * sine_table], axis=-1)

def rotary_tables(places):
    frequency = jnp.exp(-math.log(rope_base) * jnp.arange(HEAD_WIDTH // 2, dtype=jnp.float32) * 2.0 / HEAD_WIDTH)
    angles = places.astype(jnp.float32)[..., None] * frequency
    return (jnp.cos(angles)[..., None, :], jnp.sin(angles)[..., None, :])

def attend(pieces):
    query_rows, key_rows, values_in, places = pieces
    sequence_length = query_rows.shape[0]
    grouped_rows = query_rows.reshape(sequence_length, KEY_VALUE_HEADS, QUERY_HEADS // KEY_VALUE_HEADS, HEAD_WIDTH)
    scores = reduced_backward(HEAD_WIDTH ** (-0.5) * jnp.einsum('qhgd,khd->hgqk', grouped_rows, key_rows, precision=lax.Precision.HIGHEST))
    token_at = jnp.arange(sequence_length, dtype=jnp.int32)
    visible = (token_at[None, :] <= token_at[:, None]) & (token_at[None, :] >= (token_at - places)[:, None])
    probs = softmax_rows(jnp.where(visible, scores, masked))
    mixed = jnp.einsum('hgqk,khd->qhgd', low(probs), values_in, precision=lax.Precision.HIGHEST)
    return mixed.reshape(sequence_length, QUERY_HEADS * HEAD_WIDTH)

def one_expert(member):
    arrived, weight_in, weight_out = member
    gate_up = reduced_backward(product_highest(arrived, weight_in))
    hidden = low(swiglu(gate_up))
    return reduced_backward(low(product_highest(hidden, weight_out.T)))

def expert_group(expert_in, expert_out, member):
    routed_rows, gates, flat_ids = member
    rows = routed_rows.shape[0]
    limit = NSEQ * N_CTX * CAP
    ids_line = flat_ids.reshape(-1).astype(jnp.int32)
    one_hot = (ids_line[:, None] == jnp.arange(EXPERTS, dtype=jnp.int32)[None, :]).astype(jnp.int32)
    ranking = lax.optimization_barrier(jnp.sum((jnp.cumsum(one_hot, axis=0, dtype=jnp.int32) - 1) * one_hot, axis=1, dtype=jnp.int32))
    slots = (ids_line * limit + ranking).astype(jnp.int32)
    dispatched = jnp.zeros((EXPERTS * limit, MODEL_WIDTH), routed_rows.dtype).at[slots].set(jnp.repeat(routed_rows, TOP, axis=0))
    arrived = reduced_backward(dispatched).reshape(EXPERTS, limit, MODEL_WIDTH)
    produced = lax.map(jax.checkpoint(one_expert), (arrived, expert_in, expert_out))
    picked = produced.reshape(EXPERTS * limit, MODEL_WIDTH)[slots].reshape(rows, TOP, MODEL_WIDTH)
    return lax.optimization_barrier(jnp.sum(gates[:, :, None] * picked, axis=1))

def layer(current, places, choices_ids, weights):
    first_gain, query_weight, key_value_matrix, output_weight, second_gain, router_weight, expert_in, expert_out = weights
    batch_rows, sequence_length, width = current.shape
    flat = current.reshape(batch_rows * sequence_length, width)
    normalized_rows = low(norm_apply(flat, first_gain))
    query_rows = reduced_backward(product_highest(normalized_rows, query_weight)).reshape(batch_rows, sequence_length, QUERY_HEADS, HEAD_WIDTH)
    key_value_rows = reduced_backward(product_highest(normalized_rows, key_value_matrix)).reshape(batch_rows, sequence_length, 2, KEY_VALUE_HEADS, HEAD_WIDTH)
    cosine_table, sine_table = rotary_tables(places)
    query_rows = low(rotary_apply(query_rows, cosine_table, sine_table))
    key_rows = low(rotary_apply(key_value_rows[:, :, 0], cosine_table, sine_table))
    values_in = low(key_value_rows[:, :, 1])
    mixed = lax.map(jax.checkpoint(attend), (query_rows, key_rows, values_in, places))
    mixed = reduced_backward(low(mixed.reshape(batch_rows * sequence_length, QUERY_HEADS * HEAD_WIDTH)))
    middle = flat + reduced_backward(product_highest(mixed, output_weight))
    routed = low(norm_apply(middle, second_gain))
    logits = reduced_backward(product_highest(routed, router_weight))
    flat_ids = choices_ids.reshape(-1, TOP).astype(jnp.int32)
    picks = (flat_ids[:, :, None] == jnp.arange(EXPERTS, dtype=jnp.int32)[None, None, :]).astype(routed.dtype)
    chosen = lax.optimization_barrier(jnp.sum(logits[:, None, :] * picks, axis=-1))
    gates = softmax_rows(chosen)
    group_rows = NSEQ * sequence_length

    def group_step(member):
        return expert_group(expert_in, expert_out, member)
    mixture = lax.map(jax.checkpoint(group_step), (routed.reshape(MICRO, group_rows, width), gates.reshape(MICRO, group_rows, TOP), flat_ids.reshape(MICRO, group_rows, TOP)))
    return (middle + mixture.reshape(batch_rows * sequence_length, width)).reshape(batch_rows, sequence_length, width)

def reference(tokens, positions, expert_ids, cotangent, first_gain, query_weight, key_value_matrix, output_weight, second_gain, router_weight, expert_in, expert_out):
    batch_rows = MICRO * NSEQ
    start = tokens.astype(jnp.float32).reshape(batch_rows, SEQ, MODEL_WIDTH)
    places = positions.reshape(batch_rows, SEQ).astype(jnp.int32)
    choices_all = expert_ids.reshape(LAYER_COUNT, batch_rows, SEQ, TOP).astype(jnp.int32)
    params = tuple((member.astype(jnp.float32) for member in (first_gain, query_weight, key_value_matrix, output_weight, second_gain, router_weight, expert_in, expert_out)))
    bridges = jnp.zeros((LAYER_COUNT - 1, batch_rows, SEQ, MODEL_WIDTH), jnp.float32)

    def forward(begin, bridge_all, weights_all):
        current = begin
        stacked = []
        for level in range(LAYER_COUNT):
            if level > 0:
                current = reduced_backward(low(current)) + bridge_all[level - 1]
            current = layer(current, places, choices_all[level], tuple((member[level] for member in weights_all)))
            stacked.append(current)
        return (current, jnp.stack(stacked))
    final, back_fn, stacked = jax.vjp(forward, start, bridges, params, has_aux=True)
    d_start, d_bridges, d_params = back_fn(cotangent.astype(jnp.float32).reshape(batch_rows, SEQ, MODEL_WIDTH))
    layer_out = stacked.astype(jnp.bfloat16).reshape(LAYER_COUNT, MICRO, NSEQ, SEQ, MODEL_WIDTH)
    input_grad = jnp.concatenate([d_start[None], d_bridges], axis=0).reshape(LAYER_COUNT, MICRO, NSEQ, SEQ, MODEL_WIDTH)
    return (layer_out, input_grad, d_params[0], d_params[1], d_params[2], d_params[3], d_params[4], d_params[5], d_params[6], d_params[7])
```

```python
import functools
import math

import jax
import jax.numpy as jnp
from jax import lax
from jax.experimental import pallas as pl
from jax.experimental.pallas import tpu as pltpu
from jax.sharding import Mesh
from jax.sharding import PartitionSpec as P

T = 64
D = 1024
HW = 64
NQ = 16
NK = 8
F = 512
E = 32
CAP = 17
MAIN = E * 16
SLOTS = E * CAP
N_CTX = 16
SEQ = N_CTX * T

eps = 1e-06
rope_base = 10000.0
masked = -1e30
f32 = jnp.float32
bf16 = jnp.bfloat16

VMEM = pl.BlockSpec(memory_space=pltpu.VMEM)
SMEM = pl.BlockSpec(memory_space=pltpu.SMEM)
ANY = pl.BlockSpec(memory_space=pl.ANY)
GROUP = ("section", "x", "expert")
CTX = ("y", "x")
ALL = ("y", "x", "expert")


def sds(shape, dtype):
    return jax.ShapeDtypeStruct(shape, dtype)


def call(body, outs, ins, scratch=(), flops=0, limit=56):
    read = sum(a.size * a.dtype.itemsize for k, a in ins if k is VMEM)
    written = sum(math.prod(o.shape) * o.dtype.itemsize for o in outs)
    return pl.pallas_call(
        body,
        out_shape=list(outs),
        in_specs=[k for k, _ in ins],
        out_specs=[VMEM] * len(outs),
        scratch_shapes=list(scratch),
        compiler_params=pltpu.CompilerParams(vmem_limit_bytes=limit * 1024 * 1024),
        cost_estimate=pl.CostEstimate(
            flops=int(flops), bytes_accessed=int(read + written), transcendentals=0
        ),
    )(*[a for _, a in ins])


def dot(a, b):
    return lax.dot_general(a, b, (((1,), (0,)), ((), ())), preferred_element_type=f32)


def dot_nt(a, b):
    return lax.dot_general(a, b, (((1,), (1,)), ((), ())), preferred_element_type=f32)


def dot_tn(a, b):
    return lax.dot_general(a, b, (((0,), (0,)), ((), ())), preferred_element_type=f32)


def split(v):
    high = v.astype(bf16)
    return high, (v - high.astype(f32)).astype(bf16)


def iota(shape, dim):
    return lax.broadcasted_iota(jnp.int32, shape, dim)


def one_hot(cond):
    return jnp.where(cond, 1.0, 0.0).astype(bf16)


def expert_of(d):
    return 8 * (d & 3) + 2 * ((d >> 2) & 3) + (d >> 4)


def slot_table():
    row, col = iota((SLOTS, E), 0), iota((SLOTS, E), 1)
    d = jnp.where(row < MAIN, row >> 4, row - MAIN)
    return one_hot(expert_of(d) == col)


def shuffle(count, inverse):
    n = count * E
    row, col = iota((n, n), 0), iota((n, n), 1)
    bits = count.bit_length() - 1
    if inverse:
        return one_hot(row == (col & (count - 1)) * E + (col >> bits))
    return one_hot(col == (row & (count - 1)) * E + (row >> bits))


def pack(buf_ref, parts):
    n = len(parts)
    extra = []
    for k, rows in enumerate(parts):
        for c in range(8):
            piece = rows[:, c * 128 : (c + 1) * 128]
            buf_ref[:, k * 128 + c * 16 : k * 128 + (c + 1) * 16, :] = piece[:MAIN].reshape(
                E, 16, 128
            )
            extra.append(piece[MAIN:])
    moved = dot(shuffle(8 * n, False), jnp.concatenate(extra, axis=0)).astype(bf16)
    buf_ref[:, 128 * n :, :] = moved.reshape(E, 8 * n, 128)


def unpack(buf_ref, n):
    moved = dot(shuffle(8 * n, True), buf_ref[:, 128 * n :, :].reshape(E * 8 * n, 128)).astype(bf16)
    parts = []
    for k in range(n):
        pieces = []
        for c in range(8):
            head = buf_ref[:, k * 128 + c * 16 : k * 128 + (c + 1) * 16, :].reshape(MAIN, 128)
            at = (k * 8 + c) * E
            pieces.append(jnp.concatenate([head, moved[at : at + E]], axis=0))
        parts.append(jnp.concatenate(pieces, axis=1))
    return parts


def norm_parts(v):
    r = lax.rsqrt(jnp.mean(v * v, axis=-1, keepdims=True) + eps)
    return r, v * r


def norm_back(v, gain, dh):
    r, n = norm_parts(v)
    a = gain * dh
    return r * (a - n * jnp.mean(n * a, axis=-1, keepdims=True)), dh * n


def rotate(chunk, cos, sin):
    lane = iota(chunk.shape, 1) & 63
    other = jnp.where(lane < 32, pltpu.roll(chunk, 96, 1), pltpu.roll(chunk, 32, 1))
    return chunk * cos + other * sin


class Chosen:
    def __init__(self, scal, layer, own, sent, place, sem):
        self.args = (own, place, sem)
        mine = scal[0] == layer

        @pl.when(mine)
        def _():
            pltpu.make_async_copy(own, place, sem).start()

        @pl.when(jnp.logical_not(mine))
        def _():
            pltpu.make_async_copy(sent, place, sem).start()

    def wait(self):
        own, place, sem = self.args
        pltpu.make_async_copy(own, place, sem).wait()


def either(scal, layer, own, sent):
    return jnp.where(scal[0] == layer, own, sent)


def prep_kernel(scal, ids_own, ids_sent, s0, st0, m0, s1, st1, m1):
    rep = slot_table()
    own = ids_own[0, scal[0], 0]
    sent = ids_sent[...]
    for layer, (s_ref, st_ref, m_ref) in enumerate(((s0, st0, m0), (s1, st1, m1))):
        ids = either(scal, layer, own, sent)
        col = iota((T, E), 1)
        member = jnp.zeros((T, E), f32)
        for k in range(8):
            member = member + jnp.where(ids[:, k : k + 1] == col, 1.0, 0.0)
        m_ref[...] = member
        low = member.astype(bf16)
        row64, col64 = iota((T, T), 0), iota((T, T), 1)
        rank = dot(one_hot(col64 < row64), low)
        rank = jnp.where(member > 0.5, rank, -1.0).astype(bf16)
        at = dot_nt(rank, rep)
        slot = iota((T, SLOTS), 1)
        place = jnp.where(slot < MAIN, slot & 15, 16).astype(f32)
        st_ref[...] = one_hot(at == place)
        eye = one_hot(iota((E, E), 0) == iota((E, E), 1))
        member_t = dot_nt(eye, low)
        rank_t = dot(member_t.astype(bf16), one_hot(row64 < col64))
        rank_t = jnp.where(member_t > 0.5, rank_t, -1.0).astype(bf16)
        at_t = dot(rep, rank_t)
        slot_t = iota((SLOTS, T), 0)
        place_t = jnp.where(slot_t < MAIN, slot_t & 15, 16).astype(f32)
        s_ref[...] = one_hot(at_t == place_t)


def qkv_body(h1, q_w, kv_w, cos, sin, pos, buf_ref):
    q = dot(h1, q_w)
    kv = dot(h1, kv_w)
    hi, lo = (pos >> 5).astype(f32), (pos & 31).astype(f32)
    lane = iota((T, 64), 1)
    where_am_i = jnp.where(lane == 0, hi, jnp.where(lane == 1, lo, 0.0)).astype(bf16)
    for pair in range(4):
        k_two = rotate(kv[:, pair * 128 : (pair + 1) * 128], cos, sin).astype(bf16)
        v_two = kv[:, 512 + pair * 128 : 512 + (pair + 1) * 128].astype(bf16)
        for g in range(2):
            k_one = k_two[:, g * 64 : (g + 1) * 64]
            v_one = v_two[:, g * 64 : (g + 1) * 64]
            group = pair * 2 + g
            q_two = rotate(q[:, group * 128 : (group + 1) * 128], cos, sin).astype(bf16)
            low_half = jnp.concatenate([v_one, where_am_i], axis=1)
            for j in range(2):
                top = jnp.concatenate([q_two[:, j * 64 : (j + 1) * 64], k_one], axis=1)
                buf_ref[2 * group + j, 0:T, :] = top
                buf_ref[2 * group + j, T : 2 * T, :] = low_half


def first_kernel(
    scal, tok, pos, cos, sin, g_own, g_sent, q_own, q_sent, kv_own, kv_sent, h1_ref, buf_ref,
    q_w, kv_w, sems,
):
    q_copy = Chosen(scal, 0, q_own.at[0], q_sent.at[0], q_w, sems.at[0])
    kv_copy = Chosen(scal, 0, kv_own.at[0], kv_sent.at[0], kv_w, sems.at[1])
    x = tok[scal[0], 0].astype(f32)
    h1 = (norm_parts(x)[1] * either(scal, 0, g_own[...], g_sent[...])).astype(bf16)
    h1_ref[...] = h1
    q_copy.wait()
    kv_copy.wait()
    qkv_body(h1, q_w[...], kv_w[...], cos[...], sin[...], pos[...], buf_ref)


def attention_parts(buf):
    q = buf[:, 0:T, 0:HW].reshape(SEQ, HW)
    k = buf[:, 0:T, HW : 2 * HW].reshape(SEQ, HW)
    v = buf[:, T : 2 * T, 0:HW].reshape(SEQ, HW)
    hi = buf[:, T : 2 * T, HW : HW + 1].reshape(SEQ, 1).astype(f32)
    lo = buf[:, T : 2 * T, HW + 1 : HW + 2].reshape(SEQ, 1).astype(f32)
    return q, k, v, hi * 32.0 + lo


def block_probs(q, k, pos, start, rows):
    keys = start + rows
    scores = dot_nt(q[start : start + rows], k[:keys]) * (HW**-0.5)
    at = (iota((rows, keys), 0) + start).astype(f32)
    key = iota((rows, keys), 1).astype(f32)
    begin = at[:, 0:1] - pos[start : start + rows]
    scores = jnp.where((key <= at) & (key >= begin), scores, masked)
    raised = jnp.exp(scores - jnp.max(scores, axis=-1, keepdims=True))
    return raised / jnp.sum(raised, axis=-1, keepdims=True)


ROWS = 256


def attend_kernel(buf_ref, out_ref):
    q, k, v, pos = attention_parts(buf_ref[...])
    for start in range(0, SEQ, ROWS):
        probs = block_probs(q, k, pos, start, ROWS)
        o = dot(probs.astype(bf16), v[: start + ROWS]).astype(bf16)
        for b in range(ROWS // T):
            piece = o[b * T : (b + 1) * T]
            out_ref[start // T + b] = jnp.concatenate([piece[: T // 2], piece[T // 2 :]], axis=1)


def heads_in(buf_ref, o_ref):
    for g in range(8):
        a, b = buf_ref[2 * g], buf_ref[2 * g + 1]
        o_ref[0 : T // 2, g * 128 : (g + 1) * 128] = jnp.concatenate([a[:, :64], b[:, :64]], axis=1)
        o_ref[T // 2 : T, g * 128 : (g + 1) * 128] = jnp.concatenate([a[:, 64:], b[:, 64:]], axis=1)


def heads_out(do, buf_ref):
    for g in range(8):
        two = do[:, g * 128 : (g + 1) * 128]
        for j in range(2):
            one = two[:, j * 64 : (j + 1) * 64]
            buf_ref[2 * g + j] = jnp.concatenate([one[: T // 2], one[T // 2 :]], axis=1)


def gates_from(logits, member):
    chosen = member > 0.5
    largest = jnp.max(jnp.where(chosen, logits, masked), axis=-1, keepdims=True)
    raised = jnp.where(chosen, jnp.exp(jnp.minimum(logits - largest, 0.0)), 0.0)
    return raised / jnp.sum(raised, axis=-1, keepdims=True)


def gated_rows(gates, s, rep, g_low):
    high, low = split(gates)
    up = (s * dot_nt(rep, high).astype(bf16)).astype(bf16)
    down = (s * dot_nt(rep, low).astype(bf16)).astype(bf16)
    return (dot(up, g_low) + dot(down, g_low)).astype(bf16)


def mid_kernel(layer, *refs):
    refs = list(refs)
    scal, ob, x_ref, wo_own, wo_sent, g_own, g_sent, r_own, r_sent, s_ref, m_ref = refs[:11]
    refs = refs[11:]
    cot = refs.pop(0) if layer == 1 else None
    o_ref, mid_ref, h2_ref, gates_ref, buf_ref, wo, sems = refs
    copy = Chosen(scal, layer, wo_own.at[0], wo_sent.at[0], wo, sems.at[0])
    heads_in(ob, o_ref)
    x = (tok_row(x_ref, scal) if layer == 0 else x_ref[...]).astype(f32)
    copy.wait()
    middle = x + dot(o_ref[...], wo[...])
    mid_ref[...] = middle
    h2 = (norm_parts(middle)[1] * either(scal, layer, g_own[...], g_sent[...])).astype(bf16)
    h2_ref[...] = h2
    logits = dot(h2, either(scal, layer, r_own[0], r_sent[0]))
    gates = gates_from(logits, m_ref[...])
    gates_ref[...] = gates
    s = s_ref[...]
    parts = [dot(s, h2).astype(bf16)]
    if layer == 1:
        parts.append(gated_rows(gates, s, slot_table(), tok_row(cot, scal)))
    pack(buf_ref, parts)


def tok_row(ref, scal):
    return ref[scal[0], 0]


def hidden_of(gu):
    gate, up = gu[:, :F], gu[:, F:]
    sg = jax.nn.sigmoid(gate)
    return gate, up, sg, (gate * sg * up).astype(bf16)


def expert_forward_kernel(
    scal, buf, in_own, in_sent, out_own, out_sent, ybuf, gu_ref, w_in, w_out, sems
):
    at = scal[1]
    copy_in = Chosen(scal, 0, in_own.at[0, at], in_sent, w_in, sems.at[0])
    copy_out = Chosen(scal, 0, out_own.at[0, at], out_sent, w_out, sems.at[1])
    (x,) = unpack(buf, 1)
    copy_in.wait()
    gu = dot(x, w_in[...])
    gu_ref[...] = gu
    z = hidden_of(gu)[3]
    copy_out.wait()
    pack(ybuf, [dot_nt(z, w_out[...]).astype(bf16)])


def expert_back(dy, gu, w_in, w_out):
    gate, up, sg, z = hidden_of(gu)
    dz = dot(dy, w_out)
    dgate = dz * up * (sg + gate * sg * (1.0 - sg))
    dup = dz * gate * sg
    dgu = jnp.concatenate([dgate, dup], axis=1).astype(bf16)
    return z, dgu, dot_nt(dgu, w_in).astype(bf16)


def expert_both_kernel(
    scal, buf, in_own, in_sent, out_own, out_sent, back, dgu_ref, z_ref, w_in, w_out, sems
):
    at = scal[1]
    copy_in = Chosen(scal, 1, in_own.at[0, at], in_sent, w_in, sems.at[0])
    copy_out = Chosen(scal, 1, out_own.at[0, at], out_sent, w_out, sems.at[1])
    x, dy = unpack(buf, 2)
    copy_in.wait()
    gu = dot(x, w_in[...])
    copy_out.wait()
    z, dgu, dx = expert_back(dy, gu, w_in[...], w_out[...])
    dgu_ref[...] = dgu
    z_ref[...] = z
    y = dot_nt(z, w_out[...]).astype(bf16)
    pack(back, [y, dx])


def expert_back_kernel(
    scal, buf, gu_ref, in_own, in_sent, out_own, out_sent, back, dgu_ref, z_ref, w_in, w_out, sems
):
    at = scal[1]
    copy_out = Chosen(scal, 0, out_own.at[0, at], out_sent, w_out, sems.at[1])
    copy_in = Chosen(scal, 0, in_own.at[0, at], in_sent, w_in, sems.at[0])
    (dy,) = unpack(buf, 1)
    copy_out.wait()
    copy_in.wait()
    z, dgu, dx = expert_back(dy, gu_ref[...], w_in[...], w_out[...])
    dgu_ref[...] = dgu
    z_ref[...] = z
    pack(back, [dx])


def expert_grad_kernel(layer, *refs):
    if layer == 1:
        buf, dgu, z, out = refs
        x, dy = unpack(buf, 2)
    else:
        xbuf, dybuf, dgu, z, out = refs
        (x,), (dy,) = unpack(xbuf, 1), unpack(dybuf, 1)
    out[:, :D] = dot_tn(x, dgu[...]).astype(bf16)
    out[:, D:] = dot_tn(dy, z[...]).astype(bf16)


def combine(middle, gates, st, rep, y):
    high, low = split(gates)
    up = (st * dot_nt(high, rep).astype(bf16)).astype(bf16)
    down = (st * dot_nt(low, rep).astype(bf16)).astype(bf16)
    return middle + (dot(up, y) + dot(down, y))


def next_kernel(
    scal, yb, mid, gates, st, pos, cos, sin, g_own, g_sent, q_own, q_sent, kv_own, kv_sent,
    out_ref, h1_ref, buf_ref, q_w, kv_w, sems,
):
    q_copy = Chosen(scal, 1, q_own.at[0], q_sent.at[0], q_w, sems.at[0])
    kv_copy = Chosen(scal, 1, kv_own.at[0], kv_sent.at[0], kv_w, sems.at[1])
    (y,) = unpack(yb, 1)
    out = combine(mid[...], gates[...], st[...], slot_table(), y).astype(bf16)
    out_ref[...] = out
    h1 = (norm_parts(out.astype(f32))[1] * either(scal, 1, g_own[...], g_sent[...])).astype(bf16)
    h1_ref[...] = h1
    q_copy.wait()
    kv_copy.wait()
    qkv_body(h1, q_w[...], kv_w[...], cos[...], sin[...], pos[...], buf_ref)


def turn_kernel(layer, *refs):
    refs = list(refs)
    scal, mid, gates_ref, st_ref, g_own, g_sent, r_own, r_sent, wo_own, wo_sent = refs[:10]
    refs = refs[10:]
    if layer == 1:
        ret, cot = refs[:2]
        out_ref, dlog_ref, dmid_ref, dhn_ref, da_ref, dobuf, wo, sems = refs[2:]
    else:
        yb, dxb, g_ref = refs[:3]
        dlog_ref, dmid_ref, dhn_ref, da_ref, dobuf, wo, sems = refs[3:]
    copy = Chosen(scal, layer, wo_own.at[0], wo_sent.at[0], wo, sems.at[0])
    rep, st, gates = slot_table(), st_ref[...], gates_ref[...]
    middle = mid[...]
    if layer == 1:
        y, dx = unpack(ret, 2)
        g_low = tok_row(cot, scal)
        out_ref[...] = combine(middle, gates, st, rep, y).astype(bf16)
    else:
        (y,), (dx,) = unpack(yb, 1), unpack(dxb, 1)
        g_low = g_ref[...]
    d_slot = dot_nt(g_low, y) * st.astype(f32)
    high, low = split(d_slot)
    d_gates = dot(high, rep) + dot(low, rep)
    d_chosen = gates * (d_gates - jnp.sum(gates * d_gates, axis=-1, keepdims=True))
    d_log = d_chosen.astype(bf16)
    dlog_ref[...] = d_log
    d_h2 = dot(st, dx) + dot_nt(d_log, either(scal, layer, r_own[0], r_sent[0]))
    d_v, d_hn = norm_back(middle, either(scal, layer, g_own[...], g_sent[...]), d_h2)
    d_mid = g_low.astype(f32) + d_v
    dmid_ref[...] = d_mid
    dhn_ref[...] = d_hn.astype(bf16)
    d_a = d_mid.astype(bf16)
    da_ref[...] = d_a
    copy.wait()
    heads_out(dot_nt(d_a, wo[...]).astype(bf16), dobuf)


def attend_back_kernel(buf_ref, dobuf, out_ref, dk_ref, dv_ref):
    q, k, v, pos = attention_parts(buf_ref[...])
    packed = dobuf[...]
    do = jnp.concatenate([packed[:, :, :HW], packed[:, :, HW:]], axis=1).reshape(SEQ, HW)
    scale = HW**-0.5
    dq = []
    for start in reversed(range(0, SEQ, ROWS)):
        keys = start + ROWS
        probs = block_probs(q, k, pos, start, ROWS)
        do_rows = do[start:keys]
        d_probs = dot_nt(do_rows, v[:keys])
        inner = jnp.sum(probs * d_probs, axis=-1, keepdims=True)
        d_scores = (probs * (d_probs - inner)).astype(bf16)
        dq.append((dot(d_scores, k[:keys]) * scale).astype(bf16))
        d_k = dot_tn(d_scores, q[start:keys]) * scale
        d_v = dot_tn(probs.astype(bf16), do_rows)
        if keys == SEQ:
            dk_ref[...] = d_k
            dv_ref[...] = d_v
        else:
            dk_ref[0:keys] = dk_ref[0:keys] + d_k
            dv_ref[0:keys] = dv_ref[0:keys] + d_v
    d_q = jnp.concatenate(dq[::-1], axis=0)
    d_k = dk_ref[...].astype(bf16)
    d_v = dv_ref[...].astype(bf16)
    out_ref[:, 0:T, :] = jnp.concatenate([d_q, d_k], axis=1).reshape(N_CTX, T, 128)
    d_v = d_v.reshape(N_CTX, T, HW)
    out_ref[:, T:, :] = jnp.concatenate([d_v[:, : T // 2], d_v[:, T // 2 :]], axis=2)


def back_kernel(layer, *refs):
    refs = list(refs)
    scal, buf, x_ref, dmid, cos_ref, sin_ref, g_own, g_sent, q_own, q_sent, kv_own, kv_sent = refs[:12]
    refs = refs[12:]
    if layer == 1:
        s_ref, gates_ref = refs[:2]
        refs = refs[2:]
    grad_ref, dq_ref, dkv_ref, dhn_ref = refs[:4]
    refs = refs[4:]
    if layer == 1:
        g_ref, dybuf = refs[:2]
        refs = refs[2:]
    q_w, kv_w, sems = refs
    q_copy = Chosen(scal, layer, q_own.at[0], q_sent.at[0], q_w, sems.at[0])
    kv_copy = Chosen(scal, layer, kv_own.at[0], kv_sent.at[0], kv_w, sems.at[1])
    cos, sin = cos_ref[...], -sin_ref[...]
    half = T // 2
    k_parts, v_parts = [], []
    for g in range(8):
        a, b = buf[2 * g], buf[2 * g + 1]
        q_two = jnp.concatenate([a[:T, :64], b[:T, :64]], axis=1).astype(f32)
        dq_ref[:, g * 128 : (g + 1) * 128] = rotate(q_two, cos, sin).astype(bf16)
        k_parts.append(a[:T, 64:].astype(f32) + b[:T, 64:].astype(f32))
        v_sum = a[T:].astype(f32) + b[T:].astype(f32)
        v_parts.append(jnp.concatenate([v_sum[:, :64], v_sum[:, 64:]], axis=0))
    for p in range(4):
        k_two = jnp.concatenate([k_parts[2 * p], k_parts[2 * p + 1]], axis=1)
        v_two = jnp.concatenate([v_parts[2 * p], v_parts[2 * p + 1]], axis=1)
        dkv_ref[:, p * 128 : (p + 1) * 128] = rotate(k_two, cos, sin).astype(bf16)
        dkv_ref[:, 512 + p * 128 : 512 + (p + 1) * 128] = v_two.astype(bf16)
    q_copy.wait()
    kv_copy.wait()
    d_h1 = dot_nt(dq_ref[...], q_w[...]) + dot_nt(dkv_ref[...], kv_w[...])
    x = (tok_row(x_ref, scal) if layer == 0 else x_ref[...]).astype(f32)
    d_x, d_hn = norm_back(x, either(scal, layer, g_own[...], g_sent[...]), d_h1)
    dhn_ref[...] = d_hn.astype(bf16)
    grad = dmid[...] + d_x
    grad_ref[...] = grad
    if layer == 1:
        g_low = grad.astype(bf16)
        g_ref[...] = g_low
        pack(dybuf, [gated_rows(gates_ref[...], s_ref[...], slot_table(), g_low)])


def dense_grad_kernel(
    scal, h1, dq, dkv, o, da, h1_s, dq_s, dkv_s, o_s, da_s, h2, dlog, dhn1, dhn2, out
):
    half = D // 2
    cols = pl.ds(pl.multiple_of(scal[0] * half, half), half)
    for k, (a, a_s, b, b_s) in enumerate(
        ((h1, h1_s, dq, dq_s), (h1, h1_s, dkv, dkv_s), (o, o_s, da, da_s))
    ):
        both = jnp.concatenate([a[...], a_s[...]], axis=0)
        right = jnp.concatenate([b[:, cols], b_s[:, cols]], axis=0)
        out[:, k * half : (k + 1) * half] = dot_tn(both, right).astype(bf16)
    lane = iota((T, 128), 1)
    logs = jnp.concatenate([dlog[...], jnp.zeros((T, 128 - E), bf16)], axis=1)
    extra = dot_tn(h2[...], logs)
    extra = extra + dot_tn(dhn1[...], one_hot(lane == E)) + dot_tn(dhn2[...], one_hot(lane == E + 1))
    out[:, 3 * half :] = extra.astype(bf16)


def swap(v):
    return lax.ppermute(v, "section", [(0, 1), (1, 0)])


def all_to_all(v, axes):
    return lax.all_to_all(v, axes, 0, 0, tiled=True)


def rotary_tables(places):
    frequency = jnp.exp(-math.log(rope_base) * jnp.arange(HW // 2, dtype=f32) * 2.0 / HW)
    angles = places.astype(f32)[:, None] * frequency
    cos, sin = jnp.cos(angles), jnp.sin(angles)
    return jnp.concatenate([cos] * 4, axis=1), jnp.concatenate([-sin, sin] * 2, axis=1)


def local(
    tokens, positions, expert_ids, cotangent, first_gain, query_weight, key_value_matrix,
    output_weight, second_gain, router_weight, expert_in, expert_out,
):
    s = lax.axis_index("section")
    x_at = lax.axis_index("x")
    scal = jnp.stack([s, 2 * x_at + s]).astype(jnp.int32)
    sc = (SMEM, scal)
    vm = lambda *arrays: [(VMEM, a) for a in arrays]
    sems = lambda n: pltpu.SemaphoreType.DMA((n,))

    q_sent, kv_sent = swap(query_weight), swap(key_value_matrix)
    g1_sent = swap(first_gain)
    ids_sent = swap(lax.dynamic_slice(expert_ids, (0, 1 - s, 0, 0, 0), (1, 1, 1, T, 8)))
    ids_sent = ids_sent.reshape(T, 8)
    wo_sent = swap(output_weight)
    g2_sent, r_sent = swap(second_gain), swap(router_weight)
    theirs = 2 * x_at + 1 - s
    in_sent = swap(lax.dynamic_slice(expert_in, (0, theirs, 0, 0), (1, 1, D, 2 * F)).reshape(D, 2 * F))
    out_sent = swap(lax.dynamic_slice(expert_out, (0, theirs, 0, 0), (1, 1, D, F)).reshape(D, F))

    places = lax.dynamic_index_in_dim(positions, s, 0, keepdims=False).reshape(T)
    cos, sin = rotary_tables(places)
    pos = places.reshape(T, 1)

    g1 = vm(first_gain, g1_sent)
    g2 = vm(second_gain, g2_sent)
    router = vm(router_weight, r_sent)
    qkv_w = [(ANY, a) for a in (query_weight, q_sent, key_value_matrix, kv_sent)]
    wo_w = [(ANY, a) for a in (output_weight, wo_sent)]
    ex_w = [(ANY, a) for a in (expert_in, in_sent, expert_out, out_sent)]
    w_dd = pltpu.VMEM((D, D), bf16)
    ex_scratch = [pltpu.VMEM((D, 2 * F), bf16), pltpu.VMEM((D, F), bf16), sems(2)]

    route = [sds((SLOTS, T), bf16), sds((T, SLOTS), bf16), sds((T, E), f32)]
    s0, st0, m0, s1, st1, m1 = call(
        prep_kernel, route + route, [sc] + vm(expert_ids, ids_sent), flops=1e7
    )
    qkv_shape = sds((N_CTX, 2 * T, 128), bf16)
    o_shape = sds((N_CTX, T // 2, 128), bf16)
    row_low, row_full = sds((T, D), bf16), sds((T, D), f32)
    gates_shape = sds((T, E), f32)
    one, two = sds((E, 136, 128), bf16), sds((E, 272, 128), bf16)

    h1_0, buf = call(
        first_kernel, [row_low, qkv_shape], [sc] + vm(tokens, pos, cos, sin) + g1 + qkv_w,
        [w_dd, w_dd, sems(2)], flops=3e8,
    )
    qkv_0 = all_to_all(buf, CTX)
    (buf,) = call(attend_kernel, [o_shape], vm(qkv_0), flops=4e8)
    o_in = all_to_all(buf, CTX)
    o_0, mid_0, h2_0, gates_0, buf = call(
        functools.partial(mid_kernel, 0), [row_low, row_full, row_low, gates_shape, one],
        [sc] + vm(o_in, tokens) + wo_w + g2 + router + vm(s0, m0), [w_dd, sems(1)], flops=2e8,
    )
    x_rows_0 = all_to_all(buf, GROUP)
    buf, gu_0 = call(
        expert_forward_kernel, [one, sds((SLOTS, 2 * F), f32)], [sc] + vm(x_rows_0) + ex_w,
        ex_scratch, flops=2e9,
    )
    y_0 = all_to_all(buf, GROUP)

    out_0, h1_1, buf = call(
        next_kernel, [row_low, row_low, qkv_shape],
        [sc] + vm(y_0, mid_0, gates_0, st0, pos, cos, sin) + g1 + qkv_w,
        [w_dd, w_dd, sems(2)], flops=5e8,
    )
    qkv_1 = all_to_all(buf, CTX)
    (buf,) = call(attend_kernel, [o_shape], vm(qkv_1), flops=4e8)
    o_in = all_to_all(buf, CTX)
    o_1, mid_1, h2_1, gates_1, buf = call(
        functools.partial(mid_kernel, 1), [row_low, row_full, row_low, gates_shape, two],
        [sc] + vm(o_in, out_0) + wo_w + g2 + router + vm(s1, m1, cotangent), [w_dd, sems(1)], flops=4e8,
    )
    rows_1 = all_to_all(buf, GROUP)

    buf, dgu_1, z_1 = call(
        expert_both_kernel, [two, sds((SLOTS, 2 * F), bf16), sds((SLOTS, F), bf16)],
        [sc] + vm(rows_1) + ex_w, ex_scratch, flops=4e9,
    )
    ret_1 = all_to_all(buf, GROUP)
    (ex_part_1,) = call(
        functools.partial(expert_grad_kernel, 1), [sds((D, 3 * F), bf16)], vm(rows_1, dgu_1, z_1), flops=2e9
    )

    log_shape = sds((T, E), bf16)
    out_1, dlog_1, dmid_1, dhn2_1, da_1, buf = call(
        functools.partial(turn_kernel, 1),
        [row_low, log_shape, row_full, row_low, row_low, o_shape],
        [sc] + vm(mid_1, gates_1, st1) + g2 + router + wo_w + vm(ret_1, cotangent), [w_dd, sems(1)], flops=5e8,
    )
    do_in = all_to_all(buf, CTX)
    back_shape = sds((N_CTX, T + T // 2, 128), bf16)
    kv_scratch = [pltpu.VMEM((SEQ, HW), f32), pltpu.VMEM((SEQ, HW), f32)]
    (buf,) = call(attend_back_kernel, [back_shape], vm(qkv_1, do_in), kv_scratch, flops=1e9)
    dqkv = all_to_all(buf, CTX)
    grad_1, dq_1, dkv_1, dhn1_1, g_0, buf = call(
        functools.partial(back_kernel, 1), [row_full, row_low, row_low, row_low, row_low, one],
        [sc] + vm(dqkv, out_0, dmid_1, cos, sin) + g1 + qkv_w + vm(s0, gates_0),
        [w_dd, w_dd, sems(2)], flops=4e8,
    )

    dy_rows_0 = all_to_all(buf, GROUP)
    buf, dgu_0, z_0 = call(
        expert_back_kernel, [one, sds((SLOTS, 2 * F), bf16), sds((SLOTS, F), bf16)],
        [sc] + vm(dy_rows_0, gu_0) + ex_w, ex_scratch, flops=2e9,
    )
    dx_0 = all_to_all(buf, GROUP)
    (ex_part_0,) = call(
        functools.partial(expert_grad_kernel, 0), [sds((D, 3 * F), bf16)],
        vm(x_rows_0, dy_rows_0, dgu_0, z_0), flops=2e9,
    )
    dlog_0, dmid_0, dhn2_0, da_0, buf = call(
        functools.partial(turn_kernel, 0), [log_shape, row_full, row_low, row_low, o_shape],
        [sc] + vm(mid_0, gates_0, st0) + g2 + router + wo_w + vm(y_0, dx_0, g_0), [w_dd, sems(1)], flops=5e8,
    )
    do_in = all_to_all(buf, CTX)
    (buf,) = call(attend_back_kernel, [back_shape], vm(qkv_0, do_in), kv_scratch, flops=1e9)
    dqkv = all_to_all(buf, CTX)
    grad_0, dq_0, dkv_0, dhn1_0 = call(
        functools.partial(back_kernel, 0), [row_full, row_low, row_low, row_low],
        [sc] + vm(dqkv, tokens, dmid_0, cos, sin) + g1 + qkv_w, [w_dd, w_dd, sems(2)], flops=3e8,
    )

    def dense(h1, dq, dkv, o, da, h2, dlog, dhn1, dhn2):
        mine = (h1, dq, dkv, o, da)
        (part,) = call(
            dense_grad_kernel, [sds((D, 3 * D // 2 + 128), bf16)],
            [sc] + vm(*mine) + vm(*[swap(v) for v in mine]) + vm(h2, dlog, dhn1, dhn2), flops=5e8,
        )
        full = all_to_all(part.reshape(64, 16, 3 * D // 2 + 128), ALL)
        return jnp.sum(full.astype(f32), axis=0)

    def expert(part):
        full = all_to_all(part.reshape(N_CTX, T, 3 * F), CTX)
        return jnp.sum(full.reshape(4, 4, T, 3 * F).astype(f32), axis=0)

    dense_1 = dense(h1_1, dq_1, dkv_1, o_1, da_1, h2_1, dlog_1, dhn1_1, dhn2_1)
    dense_0 = dense(h1_0, dq_0, dkv_0, o_0, da_0, h2_0, dlog_0, dhn1_0, dhn2_0)
    ex_1, ex_0 = expert(ex_part_1), expert(ex_part_0)

    first = s == 0

    def exchange(v_0, v_1):
        return jnp.where(first, v_0, v_1), swap(jnp.where(first, v_1, v_0))

    def ordered(mine, other):
        return jnp.where(first, mine, other), jnp.where(first, other, mine)

    mine, other = exchange(dense_0, dense_1)
    a, b = ordered(mine, other)
    half = D // 2
    mats = [
        jnp.concatenate([a[:, k * half : (k + 1) * half], b[:, k * half : (k + 1) * half]], axis=1)[None]
        for k in range(3)
    ]
    extra = mine[:, 3 * half :] + other[:, 3 * half :]
    router_grad = extra[None, :, :E]
    first_grad = extra[:, E].reshape(1, 16)
    second_grad = extra[:, E + 1].reshape(1, 16)
    a, b = ordered(*exchange(ex_0, ex_1))
    ex = jnp.stack([a, b], axis=1).reshape(8, T, 3 * F)
    layer_out = jnp.stack(ordered(*exchange(out_0, out_1)))[None, :, None]
    input_grad = jnp.stack(ordered(*exchange(grad_0, grad_1)))[None, :, None]
    return (
        layer_out, input_grad, first_grad, *mats, second_grad, router_grad,
        ex[None, :, :, : 2 * F], ex[None, :, :, 2 * F :],
    )


def solution(mesh):
    grid = Mesh(mesh.devices.reshape(2, 4, 4, 4), ("section", "y", "x", "expert"))
    ctx = ("y", "x")
    every = ("y", "x", "expert")
    placed = (
        P(None, "expert", ctx, None),
        P(None, "expert", ctx),
        P("section", None, "expert", ctx, None),
        P(None, "expert", ctx, None),
        P("section", None),
        P("section", None, None),
        P("section", None, None),
        P("section", None, None),
        P("section", None),
        P("section", None, None),
        P("section", "expert", None, None),
        P("section", "expert", None, None),
    )
    return jax.shard_map(
        local,
        mesh=grid,
        in_specs=placed,
        out_specs=(
            P("section", None, "expert", ctx, None),
            P("section", None, "expert", ctx, None),
            P("section", every),
            P("section", every, None),
            P("section", every, None),
            P("section", every, None),
            P("section", every),
            P("section", every, None),
            P("section", "expert", ctx, None),
            P("section", "expert", ctx, None),
        ),
        check_vma=False,
    )
```

```python
import functools
import math

import jax
import jax.numpy as jnp
from jax import lax
from jax.experimental import pallas as pl
from jax.experimental.pallas import tpu as pltpu
from jax.sharding import Mesh
from jax.sharding import PartitionSpec as P

T = 64
D = 1024
HW = 64
NQ = 16
NK = 8
F = 512
E = 32
CAP = 17
MAIN = E * 16
SLOTS = E * CAP
GROUP_SIZE = 16
ROWS_OF = GROUP_SIZE * CAP
N_CTX = 16
SEQ = N_CTX * T

eps = 1e-06
rope_base = 10000.0
masked = -1e30
f32 = jnp.float32
bf16 = jnp.bfloat16

VMEM = pl.BlockSpec(memory_space=pltpu.VMEM)
SMEM = pl.BlockSpec(memory_space=pltpu.SMEM)
ANY = pl.BlockSpec(memory_space=pl.ANY)
GROUP = ("x", "expert")
CTX = ("y", "x")
ALL = ("y", "x", "expert")


def sds(shape, dtype):
    return jax.ShapeDtypeStruct(shape, dtype)


def call(body, outs, ins, scratch=(), flops=0, limit=56):
    read = sum(a.size * a.dtype.itemsize for k, a in ins if k is VMEM)
    written = sum(math.prod(o.shape) * o.dtype.itemsize for o in outs)
    return pl.pallas_call(
        body,
        out_shape=list(outs),
        in_specs=[k for k, _ in ins],
        out_specs=[VMEM] * len(outs),
        scratch_shapes=list(scratch),
        compiler_params=pltpu.CompilerParams(vmem_limit_bytes=limit * 1024 * 1024),
        cost_estimate=pl.CostEstimate(
            flops=int(flops), bytes_accessed=int(read + written), transcendentals=0
        ),
    )(*[a for _, a in ins])


def dot(a, b):
    return lax.dot_general(a, b, (((1,), (0,)), ((), ())), preferred_element_type=f32)


def dot_nt(a, b):
    return lax.dot_general(a, b, (((1,), (1,)), ((), ())), preferred_element_type=f32)


def dot_tn(a, b):
    return lax.dot_general(a, b, (((0,), (0,)), ((), ())), preferred_element_type=f32)


def split(v):
    high = v.astype(bf16)
    return high, (v - high.astype(f32)).astype(bf16)


def iota(shape, dim):
    return lax.broadcasted_iota(jnp.int32, shape, dim)


def one_hot(cond):
    return jnp.where(cond, 1.0, 0.0).astype(bf16)


def expert_of(k):
    return 8 * ((k >> 1) & 3) + 2 * (k >> 3) + (k & 1)


def slot_table():
    row, col = iota((SLOTS, E), 0), iota((SLOTS, E), 1)
    return one_hot(expert_of(jnp.where(row < MAIN, row >> 4, row - MAIN)) == col)


def moved_rows(index, q, order):
    bits = q.bit_length() - 1
    if order == "block":
        return index >> (bits + 1), (index >> 1) & (q - 1), index & 1
    if order == "token":
        return (index >> 1) & 15, index >> 5, index & 1
    return index & 15, (index >> 4) & (q - 1), index >> (bits + 4)


def shuffle(q, to, order):
    n = 32 * q
    d, p, i = moved_rows(iota((n, n), 0), q, to)
    at = iota((n, n), 1)
    if order == "block":
        return one_hot(at == d * (2 * q) + p * 2 + i)
    if order == "token":
        return one_hot(at == p * 32 + d * 2 + i)
    return one_hot(at == (i * q + p) * 16 + d)


def pack(buf_ref, parts):
    n = len(parts)
    extra = []
    for k, rows in enumerate(parts):
        for c in range(8):
            piece = rows[:, c * 128 : (c + 1) * 128]
            buf_ref[:, k * 256 + c * 32 : k * 256 + (c + 1) * 32, :] = piece[:MAIN].reshape(16, 32, 128)
            extra.append(piece[MAIN:])
    moved = dot(shuffle(8 * n, "block", "token"), jnp.concatenate(extra, axis=0)).astype(bf16)
    buf_ref[:, 256 * n :, :] = moved.reshape(16, 16 * n, 128)


def unpack(buf_ref, n):
    rest = buf_ref[:, 256 * n :, :].reshape(256 * n, 128)
    moved = dot(shuffle(8 * n, "token", "block"), rest).astype(bf16)
    parts = []
    for k in range(n):
        pieces = []
        for c in range(8):
            head = buf_ref[:, k * 256 + c * 32 : k * 256 + (c + 1) * 32, :].reshape(MAIN, 128)
            at = (k * 8 + c) * E
            pieces.append(jnp.concatenate([head, moved[at : at + E]], axis=0))
        parts.append(jnp.concatenate(pieces, axis=1))
    return parts


def pack_experts(buf_ref, parts):
    n = len(parts)
    extra = []
    for i in range(2):
        for k in range(n):
            for c in range(8):
                piece = parts[k][i][:, c * 128 : (c + 1) * 128]
                at = k * 256 + c * 32 + i * 16
                buf_ref[:, at : at + 16, :] = piece[:256].reshape(16, 16, 128)
                extra.append(piece[256:])
    moved = dot(shuffle(8 * n, "block", "expert"), jnp.concatenate(extra, axis=0)).astype(bf16)
    buf_ref[:, 256 * n :, :] = moved.reshape(16, 16 * n, 128)


def unpack_experts(buf_ref, n):
    rest = buf_ref[:, 256 * n :, :].reshape(256 * n, 128)
    moved = dot(shuffle(8 * n, "expert", "block"), rest).astype(bf16)
    parts = []
    for k in range(n):
        both = []
        for i in range(2):
            pieces = []
            for c in range(8):
                at = k * 256 + c * 32 + i * 16
                head = buf_ref[:, at : at + 16, :].reshape(256, 128)
                at = (i * 8 * n + k * 8 + c) * 16
                pieces.append(jnp.concatenate([head, moved[at : at + 16]], axis=0))
            both.append(jnp.concatenate(pieces, axis=1))
        parts.append(both)
    return parts


def norm_parts(v):
    r = lax.rsqrt(jnp.mean(v * v, axis=-1, keepdims=True) + eps)
    return r, v * r


def norm_back(v, gain, dh):
    r, n = norm_parts(v)
    a = gain * dh
    return r * (a - n * jnp.mean(n * a, axis=-1, keepdims=True)), dh * n


def rotate(chunk, cos, sin):
    lane = iota(chunk.shape, 1) & 63
    other = jnp.where(lane < 32, pltpu.roll(chunk, 96, 1), pltpu.roll(chunk, 32, 1))
    return chunk * cos + other * sin


class Chosen:
    def __init__(self, scal, layer, own, sent, place, sem):
        self.args = (own, place, sem)
        mine = scal[0] == layer

        @pl.when(mine)
        def _():
            pltpu.make_async_copy(own, place, sem).start()

        @pl.when(jnp.logical_not(mine))
        def _():
            pltpu.make_async_copy(sent, place, sem).start()

    def wait(self):
        own, place, sem = self.args
        pltpu.make_async_copy(own, place, sem).wait()


def either(scal, layer, own, sent):
    return jnp.where(scal[0] == layer, own, sent)


def prep_kernel(scal, ids_own, ids_sent, s0, st0, m0, s1, st1, m1):
    rep = slot_table()
    own = ids_own[0, scal[0], 0]
    sent = ids_sent[...]
    for layer, (s_ref, st_ref, m_ref) in enumerate(((s0, st0, m0), (s1, st1, m1))):
        ids = either(scal, layer, own, sent)
        col = iota((T, E), 1)
        member = jnp.zeros((T, E), f32)
        for k in range(8):
            member = member + jnp.where(ids[:, k : k + 1] == col, 1.0, 0.0)
        m_ref[...] = member
        low = member.astype(bf16)
        row64, col64 = iota((T, T), 0), iota((T, T), 1)
        rank = dot(one_hot(col64 < row64), low)
        rank = jnp.where(member > 0.5, rank, -1.0).astype(bf16)
        at = dot_nt(rank, rep)
        slot = iota((T, SLOTS), 1)
        place = jnp.where(slot < MAIN, slot & 15, 16).astype(f32)
        st_ref[...] = one_hot(at == place)
        eye = one_hot(iota((E, E), 0) == iota((E, E), 1))
        member_t = dot_nt(eye, low)
        rank_t = dot(member_t.astype(bf16), one_hot(row64 < col64))
        rank_t = jnp.where(member_t > 0.5, rank_t, -1.0).astype(bf16)
        at_t = dot(rep, rank_t)
        slot_t = iota((SLOTS, T), 0)
        place_t = jnp.where(slot_t < MAIN, slot_t & 15, 16).astype(f32)
        s_ref[...] = one_hot(at_t == place_t)


def qkv_pack(q, kv, cos, sin, pos, buf_ref):
    hi = jnp.floor(pos * (1.0 / 32.0))
    lo = pos - hi * 32.0
    lane = iota((T, 64), 1)
    where_am_i = jnp.where(lane == 0, hi, jnp.where(lane == 1, lo, 0.0)).astype(bf16)
    for pair in range(4):
        k_two = rotate(kv[:, pair * 128 : (pair + 1) * 128], cos, sin).astype(bf16)
        v_two = kv[:, 512 + pair * 128 : 512 + (pair + 1) * 128].astype(bf16)
        for g in range(2):
            k_one = k_two[:, g * 64 : (g + 1) * 64]
            v_one = v_two[:, g * 64 : (g + 1) * 64]
            group = pair * 2 + g
            q_two = rotate(q[:, group * 128 : (group + 1) * 128], cos, sin).astype(bf16)
            low_half = jnp.concatenate([v_one, where_am_i], axis=1)
            for j in range(2):
                top = jnp.concatenate([q_two[:, j * 64 : (j + 1) * 64], k_one], axis=1)
                buf_ref[2 * group + j, 0:T, :] = top
                buf_ref[2 * group + j, T : 2 * T, :] = low_half


def rotary(pos):
    rows = pos.shape[0]
    lane = iota((rows, 128), 1)
    frequency = jnp.exp((lane & 31).astype(f32) * (-2.0 * math.log(rope_base) / HW))
    angles = pos * frequency
    sin = jnp.sin(angles)
    return jnp.cos(angles), jnp.where((lane & 63) < 32, -sin, sin)


def table_kernel(pos, cos, sin):
    for start in range(0, SEQ, 256):
        at = slice(start, start + 256)
        cos[at], sin[at] = rotary(pos[at])


def first_kernel(tok, places, gain, q_own, kv_own, h1_a, h1_b, buf_a, buf_b, cos_ref, sin_ref, q_w, kv_w, sems):
    q_copy = pltpu.make_async_copy(q_own.at[0], q_w, sems.at[0])
    kv_copy = pltpu.make_async_copy(kv_own.at[0], kv_w, sems.at[1])
    q_copy.start()
    kv_copy.start()
    x = jnp.concatenate([tok[0, 0], tok[1, 0]], axis=0).astype(f32)
    h1 = (norm_parts(x)[1] * gain[...]).astype(bf16)
    h1_a[...] = h1[:T]
    h1_b[...] = h1[T:]
    eye = iota((T, T), 0) == iota((T, T), 1)
    columns = [
        jnp.sum(jnp.where(eye, places[m].astype(f32), 0.0), axis=1, keepdims=True) for m in range(2)
    ]
    pos = jnp.concatenate(columns, axis=0)
    cos, sin = rotary(pos)
    cos_ref[...] = cos
    sin_ref[...] = sin
    q_copy.wait()
    q = dot(h1, q_w[...])
    kv_copy.wait()
    kv = dot(h1, kv_w[...])
    for m, buf_ref in enumerate((buf_a, buf_b)):
        at = slice(m * T, (m + 1) * T)
        qkv_pack(q[at], kv[at], cos[at], sin[at], pos[at], buf_ref)


def attention_parts(buf):
    q = buf[:, 0:T, 0:HW].reshape(SEQ, HW)
    k = buf[:, 0:T, HW : 2 * HW].reshape(SEQ, HW)
    v = buf[:, T : 2 * T, 0:HW].reshape(SEQ, HW)
    return q, k, v


def sent_positions(buf):
    hi = buf[:, T : 2 * T, HW : HW + 1].reshape(SEQ, 1).astype(f32)
    lo = buf[:, T : 2 * T, HW + 1 : HW + 2].reshape(SEQ, 1).astype(f32)
    return hi * 32.0 + lo


def block_probs(q, k, pos, start, rows):
    keys = start + rows
    scores = dot_nt(q[start : start + rows], k[:keys]) * (HW**-0.5)
    at = (iota((rows, keys), 0) + start).astype(f32)
    key = iota((rows, keys), 1).astype(f32)
    begin = at[:, 0:1] - pos[start : start + rows]
    scores = jnp.where((key <= at) & (key >= begin), scores, masked)
    raised = jnp.exp(scores - jnp.max(scores, axis=-1, keepdims=True))
    return raised / jnp.sum(raised, axis=-1, keepdims=True)


ROWS = 256


def attend_kernel(layer, buf_ref, *refs):
    q, k, v = attention_parts(buf_ref[...])
    if layer == 0:
        out_ref, pos_ref = refs
        pos = sent_positions(buf_ref[...])
        pos_ref[...] = pos
    else:
        pos_ref, out_ref = refs
        pos = pos_ref[...]
    for start in range(0, SEQ, ROWS):
        probs = block_probs(q, k, pos, start, ROWS)
        o = dot(probs.astype(bf16), v[: start + ROWS]).astype(bf16)
        for b in range(ROWS // T):
            piece = o[b * T : (b + 1) * T]
            out_ref[start // T + b] = jnp.concatenate([piece[: T // 2], piece[T // 2 :]], axis=1)


def heads_in(buf_ref, o_ref):
    for g in range(8):
        a, b = buf_ref[2 * g], buf_ref[2 * g + 1]
        o_ref[0 : T // 2, g * 128 : (g + 1) * 128] = jnp.concatenate([a[:, :64], b[:, :64]], axis=1)
        o_ref[T // 2 : T, g * 128 : (g + 1) * 128] = jnp.concatenate([a[:, 64:], b[:, 64:]], axis=1)


def heads_out(do, buf_ref):
    for g in range(8):
        two = do[:, g * 128 : (g + 1) * 128]
        for j in range(2):
            one = two[:, j * 64 : (j + 1) * 64]
            buf_ref[2 * g + j] = jnp.concatenate([one[: T // 2], one[T // 2 :]], axis=1)


def gates_from(logits, member):
    chosen = member > 0.5
    largest = jnp.max(jnp.where(chosen, logits, masked), axis=-1, keepdims=True)
    raised = jnp.where(chosen, jnp.exp(jnp.minimum(logits - largest, 0.0)), 0.0)
    return raised / jnp.sum(raised, axis=-1, keepdims=True)


def gated_rows(gates, s, rep, g_low):
    high, low = split(gates)
    up = (s * dot_nt(rep, high).astype(bf16)).astype(bf16)
    down = (s * dot_nt(rep, low).astype(bf16)).astype(bf16)
    return (dot(up, g_low) + dot(down, g_low)).astype(bf16)


def mid_kernel(layer, *refs):
    refs = list(refs)
    scal, ob, x_ref, wo_own, wo_sent, g_own, g_sent, r_own, r_sent, s_ref, m_ref = refs[:11]
    refs = refs[11:]
    cot = refs.pop(0) if layer == 1 else None
    o_ref, mid_ref, h2_ref, gates_ref, buf_ref, wo, sems = refs
    copy = Chosen(scal, layer, wo_own.at[0], wo_sent.at[0], wo, sems.at[0])
    heads_in(ob, o_ref)
    x = (tok_row(x_ref, scal) if layer == 0 else x_ref[...]).astype(f32)
    copy.wait()
    middle = x + dot(o_ref[...], wo[...])
    mid_ref[...] = middle
    h2 = (norm_parts(middle)[1] * either(scal, layer, g_own[...], g_sent[...])).astype(bf16)
    h2_ref[...] = h2
    logits = dot(h2, either(scal, layer, r_own[0], r_sent[0]))
    gates = gates_from(logits, m_ref[...])
    gates_ref[...] = gates
    s = s_ref[...]
    parts = [dot(s, h2).astype(bf16)]
    if layer == 1:
        parts.append(gated_rows(gates, s, slot_table(), tok_row(cot, scal)))
    pack(buf_ref, parts)


def tok_row(ref, scal):
    return ref[scal[0], 0]


def hidden_of(gu):
    gate, up = gu[:, :F], gu[:, F:]
    sg = jax.nn.sigmoid(gate)
    return gate, up, sg, (gate * sg * up).astype(bf16)


def sorted_out(scal, i, keep, send, at, value):
    cols = slice(at, at + value.shape[1])

    @pl.when(scal[0] == i)
    def _():
        keep[:, cols] = value

    @pl.when(scal[0] != i)
    def _():
        send[:, cols] = value


class ExpertWeights:
    def __init__(self, scal, layer, own_sent, w_in, w_out, sems):
        in_own, in_sent, out_own, out_sent = own_sent
        pair = pl.ds(scal[1], 2)
        self.copies = (
            Chosen(scal, layer, in_own.at[0, pair], in_sent, w_in, sems.at[0]),
            Chosen(scal, layer, out_own.at[0, pair], out_sent, w_out, sems.at[1]),
        )

    def wait(self):
        for copy in self.copies:
            copy.wait()


def expert_forward_kernel(
    scal, buf, in_own, in_sent, out_own, out_sent, ybuf, gu_ref, keep, send, w_in, w_out, sems
):
    weights = ExpertWeights(scal, 0, (in_own, in_sent, out_own, out_sent), w_in, w_out, sems)
    (x,) = unpack_experts(buf, 1)
    weights.wait()
    y = []
    for i in range(2):
        gu = dot(x[i], w_in[i])
        gu_ref[i] = gu
        y.append(dot_nt(hidden_of(gu)[3], w_out[i]).astype(bf16))
        sorted_out(scal, i, keep, send, 0, x[i])
    pack_experts(ybuf, [y])


def expert_back(dy, gu, w_in, w_out):
    gate, up, sg, z = hidden_of(gu)
    dz = dot(dy, w_out)
    dgate = dz * up * (sg + gate * sg * (1.0 - sg))
    dup = dz * gate * sg
    dgu = jnp.concatenate([dgate, dup], axis=1).astype(bf16)
    return z, dgu, dot_nt(dgu, w_in).astype(bf16)


def expert_both_kernel(
    scal, buf, in_own, in_sent, out_own, out_sent, back, keep, send, w_in, w_out, sems
):
    weights = ExpertWeights(scal, 1, (in_own, in_sent, out_own, out_sent), w_in, w_out, sems)
    x, dy = unpack_experts(buf, 2)
    weights.wait()
    y, dx = [], []
    for i in range(2):
        z, dgu, dx_i = expert_back(dy[i], dot(x[i], w_in[i]), w_in[i], w_out[i])
        y.append(dot_nt(z, w_out[i]).astype(bf16))
        dx.append(dx_i)
        for at, value in ((0, dy[i]), (D, dgu), (D + 2 * F, z), (D + 3 * F, x[i])):
            sorted_out(scal, i, keep, send, at, value)
    pack_experts(back, [y, dx])


def expert_back_kernel(
    scal, buf, gu_ref, in_own, in_sent, out_own, out_sent, back, keep, send, w_in, w_out, sems
):
    weights = ExpertWeights(scal, 0, (in_own, in_sent, out_own, out_sent), w_in, w_out, sems)
    (dy,) = unpack_experts(buf, 1)
    weights.wait()
    dx = []
    for i in range(2):
        z, dgu, dx_i = expert_back(dy[i], gu_ref[i], w_in[i], w_out[i])
        dx.append(dx_i)
        for at, value in ((0, dy[i]), (D, dgu), (D + 2 * F, z)):
            sorted_out(scal, i, keep, send, at, value)
    pack_experts(back, [dx])


def expert_grad_kernel(layer, *refs):
    if layer == 1:
        keep, got, out = refs
        x = jnp.concatenate([keep[:, D + 3 * F :], got[:, D + 3 * F :]], axis=0)
    else:
        x_keep, x_got, keep, got, out = refs
        x = jnp.concatenate([x_keep[...], x_got[...]], axis=0)
    dy = jnp.concatenate([keep[:, :D], got[:, :D]], axis=0)
    dgu = jnp.concatenate([keep[:, D : D + 2 * F], got[:, D : D + 2 * F]], axis=0)
    z = jnp.concatenate([keep[:, D + 2 * F : D + 3 * F], got[:, D + 2 * F : D + 3 * F]], axis=0)
    out[:, : 2 * F] = dot_tn(x, dgu).astype(bf16)
    out[:, 2 * F :] = dot_tn(dy, z).astype(bf16)


def expert_rows_kernel(scal, rows, b0, b1, b2, b3):
    for k, b in enumerate((b0, b1, b2, b3)):
        at = pl.multiple_of(((scal[2] + k) & 3) * T, T)
        b[...] = rows[pl.ds(at, T), :]


def expert_sort_kernel(scal, *refs):
    keep, send = refs[8:]
    for layer in range(2):
        for k in range(4):
            block = refs[4 * layer + k]
            place = (scal[2] - k) & 3

            @pl.when(scal[0] == layer)
            def _():
                keep[place] = block[...]

            @pl.when(scal[0] != layer)
            def _():
                send[place] = block[...]


def expert_final_kernel(scal, keep, got, out_in, out_out):
    for x in range(4):
        for ref, j in ((keep, scal[0]), (got, 1 - scal[0])):
            out_in[0, 2 * x + j] = ref[x, :, : 2 * F].astype(f32)
            out_out[0, 2 * x + j] = ref[x, :, 2 * F :].astype(f32)


def place_kernel(scal, keep, got, out):
    out[0, scal[0], 0] = keep[...]
    out[0, 1 - scal[0], 0] = got[...]


def by_section(scal, v_0, v_1, keep, send):
    keep[...] = jnp.where(scal[0] == 0, v_0, v_1)
    send[...] = jnp.where(scal[0] == 0, v_1, v_0)


def combine(middle, gates, st, rep, y):
    high, low = split(gates)
    up = (st * dot_nt(high, rep).astype(bf16)).astype(bf16)
    down = (st * dot_nt(low, rep).astype(bf16)).astype(bf16)
    return middle + (dot(up, y) + dot(down, y))


def micro_rows(ref, scal):
    return ref[pl.ds(pl.multiple_of(scal[0] * T, T), T), :]


def next_kernel(
    scal, yb, mid, gates, st, cos, sin, h1_a, h1_b, g_own, g_sent, q_own, q_sent, kv_own, kv_sent,
    out_ref, h1_ref, buf_ref, q_w, kv_w, sems,
):
    q_copy = Chosen(scal, 1, q_own.at[0], q_sent.at[0], q_w, sems.at[0])
    kv_copy = Chosen(scal, 1, kv_own.at[0], kv_sent.at[0], kv_w, sems.at[1])
    (y,) = unpack(yb, 1)
    out = combine(mid[...], gates[...], st[...], slot_table(), y).astype(bf16)
    out_ref[...] = out
    h1 = (norm_parts(out.astype(f32))[1] * either(scal, 1, g_own[...], g_sent[...])).astype(bf16)
    h1_ref[:, :D] = jnp.where(scal[0] == 0, h1_a[...], h1_b[...])
    h1_ref[:, D:] = h1
    q_copy.wait()
    q = dot(h1, q_w[...])
    kv_copy.wait()
    kv = dot(h1, kv_w[...])
    qkv_pack(q, kv, micro_rows(cos, scal), micro_rows(sin, scal), jnp.zeros((T, 1), f32), buf_ref)


def turn_kernel(layer, *refs):
    refs = list(refs)
    scal, mid, gates_ref, st_ref, g_own, g_sent, r_own, r_sent, wo_own, wo_sent = refs[:10]
    refs = refs[10:]
    if layer == 1:
        ret, cot, out_0 = refs[:3]
        refs = refs[1:]
        keep, send, dlog_ref, dmid_ref, dhn_ref, da_ref, dobuf, wo, sems = refs[2:]
    else:
        yb, dxb, g_ref = refs[:3]
        dlog_ref, dmid_ref, dhn_ref, da_ref, dobuf, wo, sems = refs[3:]
    copy = Chosen(scal, layer, wo_own.at[0], wo_sent.at[0], wo, sems.at[0])
    rep, st, gates = slot_table(), st_ref[...], gates_ref[...]
    middle = mid[...]
    if layer == 1:
        y, dx = unpack(ret, 2)
        g_low = tok_row(cot, scal)
        by_section(scal, out_0[...], combine(middle, gates, st, rep, y).astype(bf16), keep, send)
    else:
        (y,), (dx,) = unpack(yb, 1), unpack(dxb, 1)
        g_low = g_ref[...]
    d_slot = dot_nt(g_low, y) * st.astype(f32)
    high, low = split(d_slot)
    d_gates = dot(high, rep) + dot(low, rep)
    d_chosen = gates * (d_gates - jnp.sum(gates * d_gates, axis=-1, keepdims=True))
    d_log = d_chosen.astype(bf16)
    dlog_ref[...] = d_log
    d_h2 = dot(st, dx) + dot_nt(d_log, either(scal, layer, r_own[0], r_sent[0]))
    d_v, d_hn = norm_back(middle, either(scal, layer, g_own[...], g_sent[...]), d_h2)
    d_mid = g_low.astype(f32) + d_v
    dmid_ref[...] = d_mid
    dhn_ref[...] = d_hn.astype(bf16)
    d_a = d_mid.astype(bf16)
    da_ref[...] = d_a
    copy.wait()
    heads_out(dot_nt(d_a, wo[...]).astype(bf16), dobuf)


def attend_back_kernel(buf_ref, dobuf, pos_ref, out_ref, dk_ref, dv_ref):
    q, k, v = attention_parts(buf_ref[...])
    pos = pos_ref[...]
    packed = dobuf[...]
    do = jnp.concatenate([packed[:, :, :HW], packed[:, :, HW:]], axis=1).reshape(SEQ, HW)
    scale = HW**-0.5
    dq = []
    for start in reversed(range(0, SEQ, ROWS)):
        keys = start + ROWS
        probs = block_probs(q, k, pos, start, ROWS)
        do_rows = do[start:keys]
        d_probs = dot_nt(do_rows, v[:keys])
        inner = jnp.sum(probs * d_probs, axis=-1, keepdims=True)
        d_scores = (probs * (d_probs - inner)).astype(bf16)
        dq.append((dot(d_scores, k[:keys]) * scale).astype(bf16))
        d_k = dot_tn(d_scores, q[start:keys]) * scale
        d_v = dot_tn(probs.astype(bf16), do_rows)
        if keys == SEQ:
            dk_ref[...] = d_k
            dv_ref[...] = d_v
        else:
            dk_ref[0:keys] = dk_ref[0:keys] + d_k
            dv_ref[0:keys] = dv_ref[0:keys] + d_v
    d_q = jnp.concatenate(dq[::-1], axis=0)
    d_k = dk_ref[...].astype(bf16)
    d_v = dv_ref[...].astype(bf16)
    out_ref[:, 0:T, :] = jnp.concatenate([d_q, d_k], axis=1).reshape(N_CTX, T, 128)
    d_v = d_v.reshape(N_CTX, T, HW)
    out_ref[:, T:, :] = jnp.concatenate([d_v[:, : T // 2], d_v[:, T // 2 :]], axis=2)


def back_kernel(layer, *refs):
    refs = list(refs)
    scal, buf, x_ref, dmid, cos_ref, sin_ref, g_own, g_sent, q_own, q_sent, kv_own, kv_sent = refs[:12]
    refs = refs[12:]
    if layer == 1:
        s_ref, gates_ref = refs[:2]
        refs = refs[2:]
    if layer == 0:
        grad_1 = refs.pop(0)
        keep, send = refs[:2]
        refs = refs[2:]
    else:
        grad_ref = refs.pop(0)
    if layer == 1:
        g_ref, dybuf = refs[:2]
        refs = refs[2:]
    q_w, kv_w, dq_ref, dkv_ref, sems = refs
    q_copy = Chosen(scal, layer, q_own.at[0], q_sent.at[0], q_w, sems.at[0])
    kv_copy = Chosen(scal, layer, kv_own.at[0], kv_sent.at[0], kv_w, sems.at[1])
    cos, sin = micro_rows(cos_ref, scal), -micro_rows(sin_ref, scal)
    half = T // 2
    k_parts, v_parts = [], []
    for g in range(8):
        a, b = buf[2 * g], buf[2 * g + 1]
        q_two = jnp.concatenate([a[:T, :64], b[:T, :64]], axis=1).astype(f32)
        dq_ref[:, g * 128 : (g + 1) * 128] = rotate(q_two, cos, sin).astype(bf16)
        k_parts.append(a[:T, 64:].astype(f32) + b[:T, 64:].astype(f32))
        v_sum = a[T:].astype(f32) + b[T:].astype(f32)
        v_parts.append(jnp.concatenate([v_sum[:, :64], v_sum[:, 64:]], axis=0))
    for p in range(4):
        k_two = jnp.concatenate([k_parts[2 * p], k_parts[2 * p + 1]], axis=1)
        v_two = jnp.concatenate([v_parts[2 * p], v_parts[2 * p + 1]], axis=1)
        dkv_ref[:, p * 128 : (p + 1) * 128] = rotate(k_two, cos, sin).astype(bf16)
        dkv_ref[:, 512 + p * 128 : 512 + (p + 1) * 128] = v_two.astype(bf16)
    q_copy.wait()
    kv_copy.wait()
    d_h1 = dot_nt(dq_ref[...], q_w[...]) + dot_nt(dkv_ref[...], kv_w[...])
    x = (tok_row(x_ref, scal) if layer == 0 else x_ref[...]).astype(f32)
    d_x, _ = norm_back(x, either(scal, layer, g_own[...], g_sent[...]), d_h1)
    grad = dmid[...] + d_x
    if layer == 0:
        by_section(scal, grad, grad_1[...], keep, send)
    else:
        grad_ref[...] = grad
        g_low = grad.astype(bf16)
        g_ref[...] = g_low
        pack(dybuf, [gated_rows(gates_ref[...], s_ref[...], slot_table(), g_low)])


def head_grad_kernel(layer, back, cos_ref, sin_ref, h1_ref, h2, dlog, dhn2, *refs):
    cos, sin = cos_ref[...], -sin_ref[...]
    out = refs[-1]
    if layer == 0:
        out[:, 256:] = refs[0][...]
    h1_all = h1_ref[:, layer * D : (layer + 1) * D]
    both = rotate(back[:, :T, :].reshape(SEQ, 2 * HW).astype(f32), cos, sin).astype(bf16)
    d_v = back[:, T:, :]
    d_v = jnp.concatenate([d_v[:, :, :HW], d_v[:, :, HW:]], axis=1).reshape(SEQ, HW)
    lane = iota((T, HW), 1)
    logs = jnp.concatenate([dlog[...], jnp.zeros((T, HW - E), bf16)], axis=1)
    extra = dot_tn(logs, h2[...]) + dot_tn(one_hot(lane == E), dhn2[...])
    out[:, : 2 * HW] = dot_tn(both, h1_all).T.astype(bf16)
    rest = jnp.concatenate([dot_tn(d_v, h1_all), extra], axis=0)
    out[:, 2 * HW : 4 * HW] = rest.T.astype(bf16)


def output_grad_kernel(scal, o_buf, da_all, b0, b1, b2, b3, rows):
    packed = o_buf[...]
    o = jnp.concatenate([packed[:, :, :HW], packed[:, :, HW:]], axis=1).reshape(SEQ, HW)
    rows[...] = dot_tn(o, da_all[...])
    for k, b in enumerate((b0, b1, b2, b3)):
        at = pl.multiple_of(((scal[3] + k) & 3) * 16, 16)
        b[...] = rows[pl.ds(at, 16), :].astype(bf16)


def head_sums(got, layer):
    v = []
    cols = slice(256 * layer, 256 * (layer + 1))
    for c in range(N_CTX):
        v.append(sum(got[4 * c + k, :, cols].astype(f32) for k in range(1, 4)) + got[4 * c, :, cols].astype(f32))
    parts = []
    for g in range(NK):
        a, b = v[2 * g], v[2 * g + 1]
        parts.append(jnp.concatenate([a[:, :HW], b[:, :HW]], axis=1))
    pair = [v[2 * g] + v[2 * g + 1] for g in range(NK)]
    for at in (HW, 2 * HW):
        for p in range(NK // 2):
            a, b = pair[2 * p], pair[2 * p + 1]
            parts.append(jnp.concatenate([a[:, at : at + HW], b[:, at : at + HW]], axis=1))
    total = sum(pair[1:]) + pair[0]
    parts.append(total[:, 2 * HW :])
    return jnp.concatenate(parts, axis=1)


def halves_kernel(scal, got, *refs):
    keep, send = refs[8:]
    go = [sum(b[...].astype(f32) for b in refs[4 * k + 1 : 4 * k + 4]) + refs[4 * k][...].astype(f32) for k in range(2)]
    by_section(scal, head_sums(got, 0), head_sums(got, 1), keep.at[:, D:], send.at[:, D:])
    by_section(scal, go[0], go[1], keep.at[:, :D], send.at[:, :D])


def final_kernel(scal, keep, got, q_rows, kv_rows, gain, gq, gkv, go, gr, g1, g2):
    mine = keep[...] + got[...]
    grad_q, grad_kv, rest = mine[:, D : 2 * D], mine[:, 2 * D : 3 * D], mine[:, 3 * D :]
    go[0] = mine[:, :D]
    gq[0] = grad_q
    gkv[0] = grad_kv
    gr[0] = rest[:, HW : HW + E]
    g2[...] = rest[:, HW + E : HW + E + 1]
    both = grad_q * q_rows[...].astype(f32) + grad_kv * kv_rows[...].astype(f32)
    g1[...] = jnp.sum(both, axis=-1, keepdims=True) / gain[...]


def swap(v):
    return lax.ppermute(v, "section", [(0, 1), (1, 0)])


def all_to_all(v, axes):
    return lax.all_to_all(v, axes, 0, 0, tiled=True)


def local(
    tokens, positions, expert_ids, cotangent, first_gain, query_weight, key_value_matrix,
    output_weight, second_gain, router_weight, expert_in, expert_out,
):
    s, y_at, x_at, z_at = (lax.axis_index(a) for a in ("section", "y", "x", "expert"))
    first = s == 0
    scal = jnp.stack([s, 2 * x_at, x_at, z_at, y_at]).astype(jnp.int32)
    sc = (SMEM, scal)
    vm = lambda *arrays: [(VMEM, a) for a in arrays]
    sems = lambda n: pltpu.SemaphoreType.DMA((n,))
    tied = lambda v, *after: lax.optimization_barrier((v,) + after)[0]

    w_dd = pltpu.VMEM((D, D), bf16)
    w_in, w_out = pltpu.VMEM((2, D, 2 * F), bf16), pltpu.VMEM((2, D, F), bf16)
    ex_scratch = [w_in, w_out, sems(2)]
    qkv_shape = sds((N_CTX, 2 * T, 128), bf16)
    o_shape = sds((N_CTX, T // 2, 128), bf16)
    row_low, row_full = sds((T, D), bf16), sds((T, D), f32)
    gates_shape = sds((T, E), f32)
    one, two = sds((GROUP_SIZE, 272, 128), bf16), sds((GROUP_SIZE, 544, 128), bf16)

    table = sds((2 * T, 128), f32)
    h1_a, h1_b, buf_a, buf_b, cos, sin = call(
        first_kernel, [row_low, row_low, qkv_shape, qkv_shape, table, table],
        vm(tokens, positions, first_gain) + [(ANY, query_weight), (ANY, key_value_matrix)],
        [w_dd, w_dd, sems(2)], flops=6e8,
    )
    down = lambda v: lax.ppermute(v, "section", [(0, 1)])
    buf = jnp.where(first, buf_a, down(buf_b))
    qkv_0 = all_to_all(buf, CTX)
    h1_b = down(h1_b)

    late = lambda v: swap(tied(v, buf_a))
    g1_sent, g2_sent, r_sent = late(first_gain), late(second_gain), late(router_weight)
    ids_sent = late(lax.dynamic_slice(expert_ids, (0, 1 - s, 0, 0, 0), (1, 1, 1, T, 8))).reshape(T, 8)
    wo_sent = late(output_weight)

    g1 = vm(first_gain, g1_sent)
    g2 = vm(second_gain, g2_sent)
    router = vm(router_weight, r_sent)
    wo_w = [(ANY, a) for a in (output_weight, wo_sent)]

    route = [sds((SLOTS, T), bf16), sds((T, SLOTS), bf16), sds((T, E), f32)]
    s0, st0, m0, s1, st1, m1 = call(
        prep_kernel, route + route, [sc] + vm(expert_ids, ids_sent), flops=1e7
    )

    def gather(v):
        return lax.all_gather(v, CTX, axis=0, tiled=True)

    def round_trip(blocks, axis):
        route = lambda k: [(i, (i + k) % 4) for i in range(4)]
        return [blocks[0]] + [lax.ppermute(blocks[k], axis, route(k)) for k in range(1, 4)]

    def heads(layer, back, h2, dlog, dhn2, *other):
        return call(
            functools.partial(head_grad_kernel, layer), [sds((D, 512 - 256 * layer), bf16)],
            vm(back, cos_all, sin_all, h1_all, h2, dlog, dhn2, *other), flops=6e8,
        )[0]

    def output(head, da_all):
        block = sds((16, D), bf16)
        return call(
            output_grad_kernel, [block] * 4, [sc] + vm(head, da_all), [pltpu.VMEM((HW, D), f32)], flops=2e8
        )

    def sum_y(part):
        return lax.psum_scatter(part, "y", scatter_dimension=0, tiled=True)

    def expert_rows(rows):
        return call(expert_rows_kernel, [sds((T, 3 * F), bf16)] * 4, [sc] + vm(rows))

    def placed(keep, send):
        return call(place_kernel, [sds((1, 2, 1, T, D), keep.dtype)], [sc] + vm(keep, swap(send)))[0]

    def with_(v, others):
        v, *others = lax.optimization_barrier((v, *others))
        return v, others

    head_0, pos_all = call(
        functools.partial(attend_kernel, 0), [o_shape, sds((SEQ, 1), f32)], vm(qkv_0), flops=4e8
    )
    pair_in = lax.dynamic_slice(tied(expert_in, head_0), (0, 2 * x_at, 0, 0), (1, 2, D, 2 * F))[0]
    pair_out = lax.dynamic_slice(tied(expert_out, head_0), (0, 2 * x_at, 0, 0), (1, 2, D, F))[0]
    o_in, (pair_in, pair_out) = with_(all_to_all(head_0, CTX), (pair_in, pair_out))
    in_sent, out_sent = swap(pair_in), swap(pair_out)
    q_sent, kv_sent = swap(tied(query_weight, o_in)), swap(tied(key_value_matrix, o_in))
    qkv_w = [(ANY, a) for a in (query_weight, q_sent, key_value_matrix, kv_sent)]
    ex_w = [(ANY, a) for a in (expert_in, in_sent, expert_out, out_sent)]
    cos_all, sin_all = call(table_kernel, [sds((SEQ, 128), f32)] * 2, vm(pos_all))
    o_0, mid_0, h2_0, gates_0, buf = call(
        functools.partial(mid_kernel, 0), [row_low, row_full, row_low, gates_shape, one],
        [sc] + vm(o_in, tokens) + wo_w + g2 + router + vm(s0, m0), [w_dd, sems(1)], flops=2e8,
    )
    x_rows_0 = all_to_all(buf, GROUP)
    x_rows_0, cos_all, sin_all = lax.optimization_barrier((x_rows_0, cos_all, sin_all))
    row_block = sds((ROWS_OF, D), bf16)
    buf, gu_0, x_keep, x_send = call(
        expert_forward_kernel, [one, sds((2, ROWS_OF, 2 * F), f32), row_block, row_block],
        [sc] + vm(x_rows_0) + ex_w, ex_scratch, flops=2e9,
    )
    y_0 = all_to_all(buf, GROUP)
    x_got = swap(x_send)

    out_0, h1_both, buf = call(
        next_kernel, [row_low, sds((T, 2 * D), bf16), qkv_shape],
        [sc] + vm(y_0, mid_0, gates_0, st0, cos, sin, h1_a, h1_b) + g1 + qkv_w,
        [w_dd, w_dd, sems(2)], flops=5e8,
    )
    h1_all = gather(h1_both)
    qkv_1 = all_to_all(buf, CTX)
    (head_1,) = call(functools.partial(attend_kernel, 1), [o_shape], vm(qkv_1, pos_all), flops=4e8)
    o_in = all_to_all(head_1, CTX)
    o_1, mid_1, h2_1, gates_1, buf = call(
        functools.partial(mid_kernel, 1), [row_low, row_full, row_low, gates_shape, two],
        [sc] + vm(o_in, out_0) + wo_w + g2 + router + vm(s1, m1, cotangent), [w_dd, sems(1)], flops=4e8,
    )
    rows_1 = all_to_all(buf, GROUP)

    wide = sds((ROWS_OF, 2 * D + 3 * F), bf16)
    buf, keep_1, send_1 = call(
        expert_both_kernel, [two, wide, wide], [sc] + vm(rows_1) + ex_w, ex_scratch, flops=4e9,
    )
    ret_1 = all_to_all(buf, GROUP)
    ex_shape = [sds((D, 3 * F), bf16)]
    (part,) = call(functools.partial(expert_grad_kernel, 1), ex_shape, vm(keep_1, swap(send_1)), flops=2e9)
    ret_1, (part,) = with_(ret_1, [part])
    ex_1 = sum_y(part)

    log_shape = sds((T, E), bf16)
    out_keep, out_send, dlog_1, dmid_1, dhn2_1, da_1, buf = call(
        functools.partial(turn_kernel, 1),
        [row_low, row_low, log_shape, row_full, row_low, row_low, o_shape],
        [sc] + vm(mid_1, gates_1, st1) + g2 + router + wo_w + vm(ret_1, cotangent, out_0),
        [w_dd, sems(1)], flops=5e8,
    )
    da_all_1 = gather(da_1)
    do_in = all_to_all(buf, CTX)
    back_shape = sds((N_CTX, T + T // 2, 128), bf16)
    kv_scratch = [pltpu.VMEM((SEQ, HW), f32), pltpu.VMEM((SEQ, HW), f32)]
    (back_1,) = call(attend_back_kernel, [back_shape], vm(qkv_1, do_in, pos_all), kv_scratch, flops=1e9)
    dqkv = all_to_all(back_1, CTX)
    head_part_1 = heads(1, back_1, h2_1, dlog_1, dhn2_1)
    layer_out = placed(out_keep, out_send)
    dqkv_scratch = [w_dd, w_dd, pltpu.VMEM((T, D), bf16), pltpu.VMEM((T, D), bf16), sems(2)]
    grad_1, g_0, buf = call(
        functools.partial(back_kernel, 1), [row_full, row_low, one],
        [sc] + vm(dqkv, out_0, dmid_1, cos, sin) + g1 + qkv_w + vm(s0, gates_0),
        dqkv_scratch, flops=4e8,
    )

    ex_1 = expert_rows(ex_1)
    ex_1_sent = round_trip(ex_1, "x")
    dy_rows_0, (head_part_1, layer_out, *_) = with_(all_to_all(buf, GROUP), (head_part_1, layer_out, *ex_1))
    narrow = sds((ROWS_OF, D + 3 * F), bf16)
    buf, keep_0, send_0 = call(
        expert_back_kernel, [one, narrow, narrow], [sc] + vm(dy_rows_0, gu_0) + ex_w, ex_scratch, flops=2e9,
    )
    dx_0 = all_to_all(buf, GROUP)
    (part,) = call(
        functools.partial(expert_grad_kernel, 0), ex_shape, vm(x_keep, x_got, keep_0, swap(send_0)), flops=2e9
    )
    dx_0, (part,) = with_(dx_0, [part])
    ex_0 = sum_y(part)
    go_1 = output(head_1, da_all_1)
    dlog_0, dmid_0, dhn2_0, da_0, buf = call(
        functools.partial(turn_kernel, 0), [log_shape, row_full, row_low, row_low, o_shape],
        [sc] + vm(mid_0, gates_0, st0) + g2 + router + wo_w + vm(y_0, dx_0, g_0), [w_dd, sems(1)], flops=5e8,
    )
    da_all_0 = gather(da_0)
    go_1_sent = round_trip(go_1, "expert")
    do_in, (*_, e0, e1, e2, e3) = with_(all_to_all(buf, CTX), (*go_1, *ex_1_sent))
    ex_1 = [e0, e1, e2, e3]
    (back_0,) = call(attend_back_kernel, [back_shape], vm(qkv_0, do_in, pos_all), kv_scratch, flops=1e9)
    dqkv, go_1 = with_(all_to_all(back_0, CTX), go_1_sent)
    head_part = heads(0, back_0, h2_0, dlog_0, dhn2_0, head_part_1)
    full = all_to_all(head_part.reshape(64, 16, 512), ALL)
    grad_keep, grad_send = call(
        functools.partial(back_kernel, 0), [row_full, row_full],
        [sc] + vm(dqkv, tokens, dmid_0, cos, sin) + g1 + qkv_w + vm(grad_1), dqkv_scratch, flops=3e8,
    )

    row_at = 16 * lax.axis_index(ALL)
    q_rows = lax.dynamic_slice(query_weight, (0, row_at, 0), (1, 16, D))[0]
    kv_rows = lax.dynamic_slice(key_value_matrix, (0, row_at, 0), (1, 16, D))[0]
    gain_rows = lax.dynamic_slice(first_gain, (0, row_at), (1, 16)).reshape(16, 1)
    ex_0 = round_trip(expert_rows(ex_0), "x")
    go_0 = round_trip(output(head_0, da_all_0), "expert")
    ex_0, (grad_keep, q_rows, kv_rows, gain_rows) = with_(ex_0, (grad_keep, q_rows, kv_rows, gain_rows))
    four = sds((4, T, 3 * F), bf16)
    keep, send = call(expert_sort_kernel, [four, four], [sc] + vm(*ex_0, *ex_1))
    input_grad = placed(grad_keep, grad_send)
    ex_in, ex_out = call(
        expert_final_kernel, [sds((1, 8, T, 2 * F), f32), sds((1, 8, T, F), f32)], [sc] + vm(keep, swap(send))
    )
    full, (ex_in, ex_out, input_grad, *go_0) = with_(full, (ex_in, ex_out, input_grad, *go_0))

    sums = sds((16, 3 * D + 128), f32)
    keep, send = call(halves_kernel, [sums, sums], [sc] + vm(full, *go_0, *go_1))
    mat = sds((1, 16, D), f32)
    column = sds((16, 1), f32)
    grad_q, grad_kv, grad_o, router_grad, first_grad, second_grad = call(
        final_kernel, [mat, mat, mat, sds((1, 16, E), f32), column, column],
        [sc] + vm(keep, swap(send), q_rows, kv_rows, gain_rows),
    )
    return (
        layer_out, input_grad, first_grad.reshape(1, 16), grad_q, grad_kv, grad_o,
        second_grad.reshape(1, 16), router_grad, ex_in, ex_out,
    )


def solution(mesh):
    grid = Mesh(mesh.devices.reshape(2, 4, 4, 4), ("section", "y", "x", "expert"))
    ctx = ("y", "x")
    every = ("y", "x", "expert")
    placed = (
        P(None, "expert", ctx, None),
        P(None, "expert", ctx),
        P("section", None, "expert", ctx, None),
        P(None, "expert", ctx, None),
        P("section", None),
        P("section", None, None),
        P("section", None, None),
        P("section", None, None),
        P("section", None),
        P("section", None, None),
        P("section", "expert", None, None),
        P("section", "expert", None, None),
    )
    return jax.shard_map(
        local,
        mesh=grid,
        in_specs=placed,
        out_specs=(
            P("section", None, "expert", ctx, None),
            P("section", None, "expert", ctx, None),
            P("section", every),
            P("section", every, None),
            P("section", every, None),
            P("section", every, None),
            P("section", every),
            P("section", every, None),
            P("section", "expert", ctx, None),
            P("section", "expert", ctx, None),
        ),
        check_vma=False,
    )
```

```python
import functools
import math

import jax
import jax.numpy as jnp
from jax import lax
from jax.experimental import pallas as pl
from jax.experimental.pallas import tpu as pltpu
from jax.sharding import Mesh
from jax.sharding import PartitionSpec as P

T = 64
D = 1024
HW = 64
WIDE = 5 * HW
NQ = 16
NK = 8
F = 512
E = 32
CAP = 17
MAIN = E * 16
SLOTS = E * CAP
GROUP_SIZE = 16
ROWS_OF = GROUP_SIZE * CAP
N_CTX = 16
SEQ = N_CTX * T

eps = 1e-06
rope_base = 10000.0
masked = -1e30
f32 = jnp.float32
bf16 = jnp.bfloat16

VMEM = pl.BlockSpec(memory_space=pltpu.VMEM)
SMEM = pl.BlockSpec(memory_space=pltpu.SMEM)
ANY = pl.BlockSpec(memory_space=pl.ANY)
PIN = "pinned"
GROUP = ("x", "expert")
CTX = ("y", "x")
ALL = ("y", "x", "expert")


def sds(shape, dtype):
    return jax.ShapeDtypeStruct(shape, dtype)


def pinned(shape, dtype):
    return pltpu.VMEM(shape, dtype)


def call(body, outs, ins, scratch=(), flops=0, limit=36, out_spec=VMEM):
    place = lambda k, a: a if k is SMEM else pltpu.with_memory_space_constraint(a, pltpu.VMEM if k is PIN else pltpu.HBM)
    outs = [o if isinstance(o, jax.ShapeDtypeStruct) is False else pltpu.HBM(o.shape, o.dtype) for o in outs]
    read = sum(a.size * a.dtype.itemsize for k, a in ins if k is VMEM)
    written = sum(math.prod(o.shape) * jnp.dtype(o.dtype).itemsize for o in outs)
    return pl.pallas_call(
        body,
        out_shape=list(outs),
        in_specs=[VMEM if k is PIN else k for k, _ in ins],
        out_specs=[out_spec] * len(outs),
        scratch_shapes=list(scratch),
        compiler_params=pltpu.CompilerParams(vmem_limit_bytes=limit * 1024 * 1024),
        cost_estimate=pl.CostEstimate(
            flops=int(flops), bytes_accessed=int(read + written), transcendentals=0
        ),
    )(*[place(k, a) for k, a in ins])


def dot(a, b):
    return lax.dot_general(a, b, (((1,), (0,)), ((), ())), preferred_element_type=f32)


def dot_nt(a, b):
    return lax.dot_general(a, b, (((1,), (1,)), ((), ())), preferred_element_type=f32)


def dot_tn(a, b):
    return lax.dot_general(a, b, (((0,), (0,)), ((), ())), preferred_element_type=f32)


def split(v):
    high = v.astype(bf16)
    return high, (v - high.astype(f32)).astype(bf16)


def iota(shape, dim):
    return lax.broadcasted_iota(jnp.int32, shape, dim)


def one_hot(cond):
    return jnp.where(cond, 1.0, 0.0).astype(bf16)


def expert_of(k):
    return 8 * ((k >> 1) & 3) + 2 * (k >> 3) + (k & 1)


def slot_table():
    row, col = iota((SLOTS, E), 0), iota((SLOTS, E), 1)
    return one_hot(expert_of(jnp.where(row < MAIN, row >> 4, row - MAIN)) == col)


def moved_rows(index, q, order):
    bits = q.bit_length() - 1
    if order == "block":
        return index >> (bits + 1), (index >> 1) & (q - 1), index & 1
    if order == "token":
        return (index >> 1) & 15, index >> 5, index & 1
    return index & 15, (index >> 4) & (q - 1), index >> (bits + 4)


def shuffle(q, to, order):
    n = 32 * q
    d, p, i = moved_rows(iota((n, n), 0), q, to)
    at = iota((n, n), 1)
    if order == "block":
        return one_hot(at == d * (2 * q) + p * 2 + i)
    if order == "token":
        return one_hot(at == p * 32 + d * 2 + i)
    return one_hot(at == (i * q + p) * 16 + d)


def pack(buf_ref, parts):
    n = len(parts)
    extra = []
    for k, rows in enumerate(parts):
        for c in range(8):
            piece = rows[:, c * 128 : (c + 1) * 128]
            buf_ref[:, k * 256 + c * 32 : k * 256 + (c + 1) * 32, :] = piece[:MAIN].reshape(16, 32, 128)
            extra.append(piece[MAIN:])
    moved = dot(shuffle(8 * n, "block", "token"), jnp.concatenate(extra, axis=0)).astype(bf16)
    buf_ref[:, 256 * n :, :] = moved.reshape(16, 16 * n, 128)


def unpack(buf_ref, n):
    rest = buf_ref[:, 256 * n :, :].reshape(256 * n, 128)
    moved = dot(shuffle(8 * n, "token", "block"), rest).astype(bf16)
    parts = []
    for k in range(n):
        pieces = []
        for c in range(8):
            head = buf_ref[:, k * 256 + c * 32 : k * 256 + (c + 1) * 32, :].reshape(MAIN, 128)
            at = (k * 8 + c) * E
            pieces.append(jnp.concatenate([head, moved[at : at + E]], axis=0))
        parts.append(jnp.concatenate(pieces, axis=1))
    return parts


def pack_experts(buf_ref, parts):
    n = len(parts)
    extra = []
    for i in range(2):
        for k in range(n):
            for c in range(8):
                piece = parts[k][i][:, c * 128 : (c + 1) * 128]
                at = k * 256 + c * 32 + i * 16
                buf_ref[:, at : at + 16, :] = piece[:256].reshape(16, 16, 128)
                extra.append(piece[256:])
    moved = dot(shuffle(8 * n, "block", "expert"), jnp.concatenate(extra, axis=0)).astype(bf16)
    buf_ref[:, 256 * n :, :] = moved.reshape(16, 16 * n, 128)


def unpack_experts(buf_ref, n):
    rest = buf_ref[:, 256 * n :, :].reshape(256 * n, 128)
    moved = dot(shuffle(8 * n, "expert", "block"), rest).astype(bf16)
    parts = []
    for k in range(n):
        both = []
        for i in range(2):
            pieces = []
            for c in range(8):
                at = k * 256 + c * 32 + i * 16
                head = buf_ref[:, at : at + 16, :].reshape(256, 128)
                at = (i * 8 * n + k * 8 + c) * 16
                pieces.append(jnp.concatenate([head, moved[at : at + 16]], axis=0))
            both.append(jnp.concatenate(pieces, axis=1))
        parts.append(both)
    return parts


def norm_parts(v):
    r = lax.rsqrt(jnp.mean(v * v, axis=-1, keepdims=True) + eps)
    return r, v * r


def norm_back(v, gain, dh):
    r, n = norm_parts(v)
    a = gain * dh
    return r * (a - n * jnp.mean(n * a, axis=-1, keepdims=True)), dh * n


def rotate(chunk, cos, sin):
    lane = iota(chunk.shape, 1) & 63
    other = jnp.where(lane < 32, pltpu.roll(chunk, 96, 1), pltpu.roll(chunk, 32, 1))
    return chunk * cos + other * sin


class Copy:
    def __init__(self, ref, place, sem):
        self.copy = pltpu.make_async_copy(ref, place, sem)
        self.copy.start()

    def wait(self):
        self.copy.wait()


def at_axis(axis):
    return lax.axis_index(axis)


class Chosen(Copy):
    def __init__(self, layer, own, sent, place, sem):
        self.copy = pltpu.make_async_copy(own, place, sem)
        mine = at_axis("section") == layer

        @pl.when(mine)
        def _():
            self.copy.start()

        @pl.when(jnp.logical_not(mine))
        def _():
            pltpu.make_async_copy(sent, place, sem).start()


def either(layer, own, sent):
    return jnp.where(at_axis("section") == layer, own, sent)


def prep_kernel(ids_own, ids_sent, s0, st0, m0, s1, st1, m1):
    rep = slot_table()
    own = ids_own[0, at_axis("section"), 0]
    sent = ids_sent[...]
    for layer, (s_ref, st_ref, m_ref) in enumerate(((s0, st0, m0), (s1, st1, m1))):
        ids = either(layer, own, sent)
        col = iota((T, E), 1)
        member = jnp.zeros((T, E), f32)
        for k in range(8):
            member = member + jnp.where(ids[:, k : k + 1] == col, 1.0, 0.0)
        m_ref[...] = member
        low = member.astype(bf16)
        row64, col64 = iota((T, T), 0), iota((T, T), 1)
        rank = dot(one_hot(col64 < row64), low)
        rank = jnp.where(member > 0.5, rank, -1.0).astype(bf16)
        at = dot_nt(rank, rep)
        slot = iota((T, SLOTS), 1)
        place = jnp.where(slot < MAIN, slot & 15, 16).astype(f32)
        st_ref[...] = one_hot(at == place)
        eye = one_hot(iota((E, E), 0) == iota((E, E), 1))
        member_t = dot_nt(eye, low)
        rank_t = dot(member_t.astype(bf16), one_hot(row64 < col64))
        rank_t = jnp.where(member_t > 0.5, rank_t, -1.0).astype(bf16)
        at_t = dot(rep, rank_t)
        slot_t = iota((SLOTS, T), 0)
        place_t = jnp.where(slot_t < MAIN, slot_t & 15, 16).astype(f32)
        s_ref[...] = one_hot(at_t == place_t)


def pair_kernel(in_own, out_own, experts, at, sems):
    moves = []

    def move(source, place, target):
        n = len(moves)
        first = pltpu.make_async_copy(source, place, sems.at[2 * n])
        moves.append((first, pltpu.make_async_copy(place, target, sems.at[2 * n + 1])))
        first.start()

    for i in range(2):
        e = 2 * at_axis("x") + i
        move(in_own.at[0, e], at.at[i, :, : 2 * F], experts.at[0, i, :, : 2 * F])
        move(out_own.at[0, e], at.at[i, :, 2 * F :], experts.at[0, i, :, 2 * F :])
    for first, second in moves:
        first.wait()
        second.start()
    for _, second in moves:
        second.wait()


def qkv_pack(q, kv, cos, sin, pos, buf_ref):
    hi = jnp.floor(pos * (1.0 / 32.0))
    lo = pos - hi * 32.0
    lane = iota((T, 64), 1)
    where_am_i = jnp.where(lane == 0, hi, jnp.where(lane == 1, lo, 0.0)).astype(bf16)
    for pair in range(4):
        k_two = rotate(kv[:, pair * 128 : (pair + 1) * 128], cos, sin).astype(bf16)
        v_two = kv[:, 512 + pair * 128 : 512 + (pair + 1) * 128].astype(bf16)
        for g in range(2):
            k_one = k_two[:, g * 64 : (g + 1) * 64]
            v_one = v_two[:, g * 64 : (g + 1) * 64]
            group = pair * 2 + g
            q_two = rotate(q[:, group * 128 : (group + 1) * 128], cos, sin).astype(bf16)
            low_half = jnp.concatenate([v_one, where_am_i], axis=1)
            for j in range(2):
                top = jnp.concatenate([q_two[:, j * 64 : (j + 1) * 64], k_one], axis=1)
                buf_ref[2 * group + j, 0:T, :] = top
                buf_ref[2 * group + j, T : 2 * T, :] = low_half


def rotary(pos):
    rows = pos.shape[0]
    lane = iota((rows, 128), 1)
    frequency = jnp.exp((lane & 31).astype(f32) * (-2.0 * math.log(rope_base) / HW))
    angles = pos * frequency
    sin = jnp.sin(angles)
    return jnp.cos(angles), jnp.where((lane & 63) < 32, -sin, sin)


def table_kernel(pos, cos, sin):
    for start in range(0, SEQ, 256):
        at = slice(start, start + 256)
        cos[at], sin[at] = rotary(pos[at])


def first_kernel(tok, places, gain, q_own, kv_own, h1_a, h1_b, buf_a, buf_b, cos_ref, sin_ref, q_w, kv_w, sems):
    q_copy = pltpu.make_async_copy(q_own.at[0], q_w, sems.at[0])
    kv_copy = pltpu.make_async_copy(kv_own.at[0], kv_w, sems.at[1])
    q_copy.start()
    kv_copy.start()
    x = jnp.concatenate([tok[0, 0], tok[1, 0]], axis=0).astype(f32)
    h1 = (norm_parts(x)[1] * gain[...]).astype(bf16)
    h1_a[...] = h1[:T]
    h1_b[...] = h1[T:]
    eye = iota((T, T), 0) == iota((T, T), 1)
    columns = [
        jnp.sum(jnp.where(eye, places[m].astype(f32), 0.0), axis=1, keepdims=True) for m in range(2)
    ]
    pos = jnp.concatenate(columns, axis=0)
    cos, sin = rotary(pos)
    cos_ref[...] = cos
    sin_ref[...] = sin
    q_copy.wait()
    q = dot(h1, q_w[...])
    kv_copy.wait()
    kv = dot(h1, kv_w[...])
    for m, buf_ref in enumerate((buf_a, buf_b)):
        at = slice(m * T, (m + 1) * T)
        qkv_pack(q[at], kv[at], cos[at], sin[at], pos[at], buf_ref)


def attention_parts(buf):
    q = buf[:, 0:T, 0:HW].reshape(SEQ, HW)
    k = buf[:, 0:T, HW : 2 * HW].reshape(SEQ, HW)
    v = buf[:, T : 2 * T, 0:HW].reshape(SEQ, HW)
    return q, k, v


def sent_positions(buf):
    hi = buf[:, T : 2 * T, HW : HW + 1].reshape(SEQ, 1).astype(f32)
    lo = buf[:, T : 2 * T, HW + 1 : HW + 2].reshape(SEQ, 1).astype(f32)
    return hi * 32.0 + lo


def block_probs(q, k, pos, start, rows):
    keys = start + rows
    scores = dot_nt(q[start : start + rows], k[:keys]) * (HW**-0.5)
    at = (iota((rows, keys), 0) + start).astype(f32)
    key = iota((rows, keys), 1).astype(f32)
    begin = at[:, 0:1] - pos[start : start + rows]
    scores = jnp.where((key <= at) & (key >= begin), scores, masked)
    raised = jnp.exp(scores - jnp.max(scores, axis=-1, keepdims=True))
    return raised / jnp.sum(raised, axis=-1, keepdims=True)


ROWS = 256


def attend_kernel(layer, buf_ref, *refs):
    q, k, v = attention_parts(buf_ref[...])
    if layer == 0:
        out_ref, kept, pos_ref = refs
        pos = sent_positions(buf_ref[...])
        pos_ref[...] = pos
    else:
        pos_ref, out_ref, kept = refs
        pos = pos_ref[...]
    kept[...] = buf_ref[...]
    for start in range(0, SEQ, ROWS):
        probs = block_probs(q, k, pos, start, ROWS)
        o = dot(probs.astype(bf16), v[: start + ROWS]).astype(bf16)
        for b in range(ROWS // T):
            piece = o[b * T : (b + 1) * T]
            out_ref[start // T + b] = jnp.concatenate([piece[: T // 2], piece[T // 2 :]], axis=1)


def heads_in(buf_ref, o_ref):
    for g in range(8):
        a, b = buf_ref[2 * g], buf_ref[2 * g + 1]
        o_ref[0 : T // 2, g * 128 : (g + 1) * 128] = jnp.concatenate([a[:, :64], b[:, :64]], axis=1)
        o_ref[T // 2 : T, g * 128 : (g + 1) * 128] = jnp.concatenate([a[:, 64:], b[:, 64:]], axis=1)


def heads_out(do, buf_ref, start):
    for g in range(8):
        two = do[:, g * 128 : (g + 1) * 128]
        for j in range(2):
            one = two[:, j * 64 : (j + 1) * 64]
            block = jnp.concatenate([one[: T // 2], one[T // 2 :]], axis=1)
            buf_ref[2 * g + j, start : start + T // 2, :] = block


def gates_from(logits, member):
    chosen = member > 0.5
    largest = jnp.max(jnp.where(chosen, logits, masked), axis=-1, keepdims=True)
    raised = jnp.where(chosen, jnp.exp(jnp.minimum(logits - largest, 0.0)), 0.0)
    return raised / jnp.sum(raised, axis=-1, keepdims=True)


def gated_rows(gates, s, rep, g_low):
    high, low = split(gates)
    up = (s * dot_nt(rep, high).astype(bf16)).astype(bf16)
    down = (s * dot_nt(rep, low).astype(bf16)).astype(bf16)
    return (dot(up, g_low) + dot(down, g_low)).astype(bf16)


def mid_kernel(layer, *refs):
    ob, x_ref, wo_all, gain, r_ref, s_ref, m_ref = refs[:7]
    h1_refs, (mid_ref, h2_ref, gates_ref, pair_ref, buf_ref, wo, sems) = refs[7:-7], refs[-7:]
    copy = Copy(wo_all.at[layer], wo, sems.at[0])
    o_ref = pair_ref.at[:, D:]
    heads_in(ob, o_ref)
    if layer == 0:
        pair_ref[:, :D] = jnp.where(at_axis("section") == 0, h1_refs[0][...], h1_refs[1][...])
    else:
        pair_ref[:, :D] = h1_refs[0][...]
    x = (tok_row(x_ref) if layer == 0 else x_ref[...]).astype(f32)
    copy.wait()
    middle = x + dot(o_ref[...], wo[...])
    mid_ref[...] = middle
    h2 = (norm_parts(middle)[1] * gain[layer]).astype(bf16)
    h2_ref[...] = h2
    pack(buf_ref, [dot(s_ref[...], h2).astype(bf16)])
    gates_ref[...] = gates_from(dot(h2, r_ref[layer]), m_ref[...])


def send_back_kernel(gates, s_ref, cot, buf_ref):
    pack(buf_ref, [gated_rows(gates[...], s_ref[...], slot_table(), tok_row(cot))])


def tok_row(ref):
    return ref[at_axis("section"), 0]


def hidden_of(gu):
    gate, up = gu[:, :F], gu[:, F:]
    sg = jax.nn.sigmoid(gate)
    return gate, up, sg, (gate * sg * up).astype(bf16)


def sorted_out(i, keep, send, at, value):
    cols = slice(at, at + value.shape[1])

    @pl.when(at_axis("section") == i)
    def _():
        keep[:, cols] = value

    @pl.when(at_axis("section") != i)
    def _():
        send[:, cols] = value


def expert_forward_kernel(layer, buf, w_all, ybuf, gu_ref, keep, send, w, sems):
    copies = [Copy(w_all.at[layer, i], w.at[i], sems.at[i]) for i in range(2)]
    (x,) = unpack_experts(buf, 1)
    y = []
    for i in range(2):
        copies[i].wait()
        gu = dot(x[i], w[i, :, : 2 * F])
        gu_ref[i] = gu
        y.append(dot_nt(hidden_of(gu)[3], w[i, :, 2 * F :]).astype(bf16))
        sorted_out(i, keep, send, 0, x[i])
    pack_experts(ybuf, [y])


def expert_back(dy, gu, w_in, w_out):
    gate, up, sg, z = hidden_of(gu)
    dz = dot(dy, w_out)
    dgate = dz * up * (sg + gate * sg * (1.0 - sg))
    dup = dz * gate * sg
    dgu = jnp.concatenate([dgate, dup], axis=1).astype(bf16)
    return z, dgu, dot_nt(dgu, w_in).astype(bf16)


def expert_back_kernel(layer, buf, gu_all, w_all, back, keep, send, w, gu, sems):
    copies = []
    for i in range(2):
        copies.append(Copy(w_all.at[layer, i], w.at[i], sems.at[i]))
        copies.append(Copy(gu_all.at[i], gu.at[i], sems.at[2 + i]))
    (dy,) = unpack_experts(buf, 1)
    dx = []
    for i in range(2):
        copies[2 * i].wait()
        copies[2 * i + 1].wait()
        z, dgu, dx_i = expert_back(dy[i], gu[i], w[i, :, : 2 * F], w[i, :, 2 * F :])
        dx.append(dx_i)
        for at, value in ((0, dy[i]), (D, dgu), (D + 2 * F, z)):
            sorted_out(i, keep, send, at, value)
    pack_experts(back, [dx])


def expert_grad_kernel(x_keep, x_got, keep, got, out):
    x = jnp.concatenate([x_keep[...], x_got[...]], axis=0)
    dy = jnp.concatenate([keep[:, :D], got[:, :D]], axis=0)
    dgu = jnp.concatenate([keep[:, D : D + 2 * F], got[:, D : D + 2 * F]], axis=0)
    z = jnp.concatenate([keep[:, D + 2 * F : D + 3 * F], got[:, D + 2 * F : D + 3 * F]], axis=0)
    out[:, : 2 * F] = dot_tn(x, dgu).astype(bf16)
    out[:, 2 * F :] = dot_tn(dy, z).astype(bf16)


def expert_rows_kernel(rows, b0, b1, b2, b3):
    for k, b in enumerate((b0, b1, b2, b3)):
        at = pl.multiple_of(((at_axis("x") + k) & 3) * T, T)
        b[...] = rows[pl.ds(at, T), :]


def expert_sort_kernel(*refs):
    keep, send = refs[8:]
    for layer in range(2):
        for k in range(4):
            block = refs[4 * layer + k]
            place = (at_axis("x") - k) & 3

            @pl.when(at_axis("section") == layer)
            def _():
                keep[place] = block[...]

            @pl.when(at_axis("section") != layer)
            def _():
                send[place] = block[...]


def expert_final_kernel(keep, got, out_in, out_out):
    for x in range(4):
        for ref, j in ((keep, at_axis("section")), (got, 1 - at_axis("section"))):
            out_in[0, 2 * x + j] = ref[x, :, : 2 * F].astype(f32)
            out_out[0, 2 * x + j] = ref[x, :, 2 * F :].astype(f32)


def place_kernel(keep, got, out):
    out[0, at_axis("section"), 0] = keep[...]
    out[0, 1 - at_axis("section"), 0] = got[...]


def by_section(v_0, v_1, keep, send):
    keep[...] = jnp.where(at_axis("section") == 0, v_0, v_1)
    send[...] = jnp.where(at_axis("section") == 0, v_1, v_0)


def combine(middle, gates, st, rep, y):
    high, low = split(gates)
    up = (st * dot_nt(high, rep).astype(bf16)).astype(bf16)
    down = (st * dot_nt(low, rep).astype(bf16)).astype(bf16)
    return middle + (dot(up, y) + dot(down, y))


def micro_rows(ref):
    return ref[pl.ds(pl.multiple_of(at_axis("section") * T, T), T), :]


def next_kernel(
    yb, mid, gates, st, cos, sin, gain, q_own, q_sent, kv_own, kv_sent, out_ref, h1_ref, saved, buf_ref, q_w, kv_w, sems,
):
    saved[...] = yb[...]
    q_copy = Chosen(1, q_own.at[0], q_sent.at[0], q_w, sems.at[0])
    kv_copy = Chosen(1, kv_own.at[0], kv_sent.at[0], kv_w, sems.at[1])
    (y,) = unpack(yb, 1)
    out = combine(mid[...], gates[...], st[...], slot_table(), y).astype(bf16)
    out_ref[...] = out
    h1 = (norm_parts(out.astype(f32))[1] * gain[1]).astype(bf16)
    h1_ref[...] = h1
    q_copy.wait()
    q = dot(h1, q_w[...])
    kv_copy.wait()
    kv = dot(h1, kv_w[...])
    qkv_pack(q, kv, micro_rows(cos), micro_rows(sin), jnp.zeros((T, 1), f32), buf_ref)


def route_back_kernel(layer, *refs):
    yb, gates_ref, st_ref, r_ref, g_ref = refs[:5]
    dlog_ref, dh2_ref = refs[-2:]
    rep, st, gates = slot_table(), st_ref[...], gates_ref[...]
    (y,) = unpack(yb, 1)
    if layer == 1:
        mid, out_0, keep, send = refs[5:9]
        g_low = tok_row(g_ref)
        by_section(out_0[...], combine(mid[...], gates, st, rep, y).astype(bf16), keep, send)
    else:
        g_low = g_ref[...]
    d_slot = dot_nt(g_low, y) * st.astype(f32)
    high, low = split(d_slot)
    d_gates = dot(high, rep) + dot(low, rep)
    d_chosen = gates * (d_gates - jnp.sum(gates * d_gates, axis=-1, keepdims=True))
    d_log = d_chosen.astype(bf16)
    dlog_ref[...] = d_log
    dh2_ref[...] = dot_nt(d_log, r_ref[layer])


def turn_kernel(layer, *refs):
    dxb, st, dh2, mid, gain, g_ref, wo_all, dmid_ref, dhn_ref, dobuf, wo, sems = refs
    copy = Copy(wo_all.at[layer], wo, sems.at[0])
    (dx,) = unpack(dxb, 1)
    g_low = tok_row(g_ref) if layer == 1 else g_ref[...]
    d_h2 = dot(st[...], dx) + dh2[...]
    d_v, d_hn = norm_back(mid[...], gain[layer], d_h2)
    d_mid = g_low.astype(f32) + d_v
    d_a = d_mid.astype(bf16)
    heads_out(d_a, dobuf, T // 2)
    copy.wait()
    heads_out(dot_nt(d_a, wo[...]).astype(bf16), dobuf, 0)
    dmid_ref[...] = d_mid
    dhn_ref[...] = d_hn.astype(bf16)


def attend_back_kernel(buf_ref, dobuf, pos_ref, out_ref, saved, da_saved, dk_ref, dv_ref):
    q, k, v = attention_parts(buf_ref[...])
    pos = pos_ref[...]
    da_saved[...] = dobuf[:, T // 2 :, :]
    packed = dobuf[:, : T // 2, :]
    do = halves(packed)
    scale = HW**-0.5
    dq = []
    for start in reversed(range(0, SEQ, ROWS)):
        keys = start + ROWS
        probs = block_probs(q, k, pos, start, ROWS)
        do_rows = do[start:keys]
        d_probs = dot_nt(do_rows, v[:keys])
        inner = jnp.sum(probs * d_probs, axis=-1, keepdims=True)
        d_scores = (probs * (d_probs - inner)).astype(bf16)
        dq.append((dot(d_scores, k[:keys]) * scale).astype(bf16))
        d_k = dot_tn(d_scores, q[start:keys]) * scale
        d_v = dot_tn(probs.astype(bf16), do_rows)
        if keys == SEQ:
            dk_ref[...] = d_k
            dv_ref[...] = d_v
        else:
            dk_ref[0:keys] = dk_ref[0:keys] + d_k
            dv_ref[0:keys] = dv_ref[0:keys] + d_v
    d_q = jnp.concatenate(dq[::-1], axis=0)
    d_k = dk_ref[...].astype(bf16)
    d_v = dv_ref[...].astype(bf16)
    out_ref[:, 0:T, :] = jnp.concatenate([d_q, d_k], axis=1).reshape(N_CTX, T, 128)
    d_v = d_v.reshape(N_CTX, T, HW)
    out_ref[:, T:, :] = jnp.concatenate([d_v[:, : T // 2], d_v[:, T // 2 :]], axis=2)
    saved[...] = out_ref[...]


def back_kernel(layer, *refs):
    refs = list(refs)
    buf, x_ref, dmid, cos_ref, sin_ref, gain, q_own, q_sent, kv_own, kv_sent = refs[:10]
    refs = refs[10:]
    if layer == 1:
        s_ref, gates_ref = refs[:2]
        refs = refs[2:]
    if layer == 0:
        grad_1 = refs.pop(0)
        keep, send = refs[:2]
        refs = refs[2:]
    else:
        grad_ref = refs.pop(0)
    if layer == 1:
        g_ref, dybuf = refs[:2]
        refs = refs[2:]
    q_w, kv_w, dq_ref, dkv_ref, sems = refs
    q_copy = Chosen(layer, q_own.at[0], q_sent.at[0], q_w, sems.at[0])
    kv_copy = Chosen(layer, kv_own.at[0], kv_sent.at[0], kv_w, sems.at[1])
    cos, sin = micro_rows(cos_ref), -micro_rows(sin_ref)
    half = T // 2
    k_parts, v_parts = [], []
    for g in range(8):
        a, b = buf[2 * g], buf[2 * g + 1]
        q_two = jnp.concatenate([a[:T, :64], b[:T, :64]], axis=1).astype(f32)
        dq_ref[:, g * 128 : (g + 1) * 128] = rotate(q_two, cos, sin).astype(bf16)
        k_parts.append(a[:T, 64:].astype(f32) + b[:T, 64:].astype(f32))
        v_sum = a[T:].astype(f32) + b[T:].astype(f32)
        v_parts.append(jnp.concatenate([v_sum[:, :64], v_sum[:, 64:]], axis=0))
    for p in range(4):
        k_two = jnp.concatenate([k_parts[2 * p], k_parts[2 * p + 1]], axis=1)
        v_two = jnp.concatenate([v_parts[2 * p], v_parts[2 * p + 1]], axis=1)
        dkv_ref[:, p * 128 : (p + 1) * 128] = rotate(k_two, cos, sin).astype(bf16)
        dkv_ref[:, 512 + p * 128 : 512 + (p + 1) * 128] = v_two.astype(bf16)
    q_copy.wait()
    kv_copy.wait()
    d_h1 = dot_nt(dq_ref[...], q_w[...]) + dot_nt(dkv_ref[...], kv_w[...])
    x = (tok_row(x_ref) if layer == 0 else x_ref[...]).astype(f32)
    d_x, _ = norm_back(x, gain[layer], d_h1)
    grad = dmid[...] + d_x
    if layer == 0:
        by_section(grad, grad_1[...], keep, send)
    else:
        grad_ref[...] = grad
        g_low = grad.astype(bf16)
        g_ref[...] = g_low
        pack(dybuf, [gated_rows(gates_ref[...], s_ref[...], slot_table(), g_low)])


def head_grad_kernel(layer, back, da, cos_ref, sin_ref, pairs, h2, dlog, dhn2, *refs):
    out = refs[-1]
    if layer == 0:
        out[:, WIDE:] = refs[0][...]
    cos, sin = cos_ref[...], -sin_ref[...]
    both = rotate(back[:, :T, :].reshape(SEQ, 2 * HW).astype(f32), cos, sin).astype(bf16)
    lane = iota((T, HW), 1)
    logs = jnp.concatenate([dlog[...], jnp.zeros((T, HW - E), bf16)], axis=1)
    extra = dot_tn(logs, h2[...]) + dot_tn(one_hot(lane == E), dhn2[...])
    h1_all = pairs[:, :D]
    out[:, : 2 * HW] = dot_tn(both, h1_all).T.astype(bf16)
    rest = [dot_tn(halves(back[:, T:, :]), h1_all), dot_tn(halves(da[...]), pairs[:, D:]), extra]
    out[:, 2 * HW : WIDE] = jnp.concatenate(rest, axis=0).T.astype(bf16)


def halves(packed):
    return jnp.concatenate([packed[:, :, :HW], packed[:, :, HW:]], axis=1).reshape(SEQ, HW)


def head_sums(got, layer):
    v = []
    cols = slice(WIDE * layer, WIDE * (layer + 1))
    for c in range(N_CTX):
        v.append(sum(got[4 * c + k, :, cols].astype(f32) for k in range(1, 4)) + got[4 * c, :, cols].astype(f32))
    pair = [v[2 * g] + v[2 * g + 1] for g in range(NK)]
    parts = []
    for blocks, at in ((v, 3 * HW), (v, 0), (pair, HW), (pair, 2 * HW)):
        for a, b in zip(blocks[::2], blocks[1::2]):
            parts.append(jnp.concatenate([a[:, at : at + HW], b[:, at : at + HW]], axis=1))
    total = sum(pair[1:]) + pair[0]
    parts.append(total[:, 3 * HW :])
    return jnp.concatenate(parts, axis=1)


def halves_kernel(got, keep, send):
    by_section(head_sums(got, 0), head_sums(got, 1), keep, send)


def final_kernel(keep, got, q_own, kv_own, gain, gq, gkv, go, gr, g1, g2, q_rows, kv_rows, sems):
    first = 16 * at_axis(ALL)
    rows = pl.ds(pl.multiple_of(first, 16), 16)
    copies = [Copy(q_own.at[0, rows], q_rows, sems.at[0]), Copy(kv_own.at[0, rows], kv_rows, sems.at[1])]
    mine = keep[...] + got[...]
    grad_q, grad_kv, rest = mine[:, D : 2 * D], mine[:, 2 * D : 3 * D], mine[:, 3 * D :]
    go[0] = mine[:, :D]
    gq[0] = grad_q
    gkv[0] = grad_kv
    gr[0] = rest[:, HW : HW + E]
    eye = iota((16, 16), 0) == iota((16, 16), 1)
    as_row = lambda column: jnp.sum(jnp.where(eye, column, 0.0), axis=0, keepdims=True)
    g2[...] = as_row(rest[:, HW + E : HW + E + 1])
    here = iota((16, D), 1) == iota((16, D), 0) + first
    gains = jnp.sum(jnp.where(here, gain[...], 0.0), axis=1, keepdims=True)
    for copy in copies:
        copy.wait()
    both = grad_q * q_rows[...].astype(f32) + grad_kv * kv_rows[...].astype(f32)
    g1[...] = as_row(jnp.sum(both, axis=-1, keepdims=True) / gains)


def swap(v):
    return lax.ppermute(v, "section", [(0, 1), (1, 0)])


def either_order(first, mine, other):
    return jnp.where(first, mine, other), jnp.where(first, other, mine)


def all_to_all(v, axes):
    return lax.all_to_all(v, axes, 0, 0, tiled=True)


def local(
    tokens, positions, expert_ids, cotangent, first_gain, query_weight, key_value_matrix,
    output_weight, second_gain, router_weight, expert_in, expert_out,
):
    s, y_at, x_at, z_at = (lax.axis_index(a) for a in ("section", "y", "x", "expert"))
    first = s == 0
    vm = lambda *arrays: [(VMEM, a) for a in arrays]
    pin = lambda *arrays: [(PIN, a) for a in arrays]
    sems = lambda n: pltpu.SemaphoreType.DMA((n,))
    tied = lambda v, *after: lax.optimization_barrier((v,) + after)[0]

    def with_(v, others):
        v, *others = lax.optimization_barrier((v, *others))
        return v, others

    def gather(v, axis):
        return lax.all_gather(v, axis, axis=0, tiled=True)

    def both(v):
        return lax.all_gather(v, "section", axis=0, tiled=True)

    def round_trip(blocks, axis):
        route = lambda k: [(i, (i + k) % 4) for i in range(4)]
        return [blocks[0]] + [lax.ppermute(blocks[k], axis, route(k)) for k in range(1, 4)]

    w_dd = pltpu.VMEM((D, D), bf16)
    ex_scratch = [pltpu.VMEM((2, D, 3 * F), bf16), sems(2)]
    qkv_shape = pinned((N_CTX, 2 * T, 128), bf16)
    o_shape = pinned((N_CTX, T // 2, 128), bf16)
    qkv_half = pinned((N_CTX, T, 128), bf16)
    back_shape = pinned((N_CTX, T + T // 2, 128), bf16)
    rows_shape = pinned((GROUP_SIZE, 272, 128), bf16)
    row_low, row_full = sds((T, D), bf16), sds((T, D), f32)
    gates_shape, log_shape = sds((T, E), f32), sds((T, E), bf16)
    o_saved, back_saved = sds(o_shape.shape, bf16), sds(back_shape.shape, bf16)
    qkv_saved, rows_saved = sds(qkv_shape.shape, bf16), sds(rows_shape.shape, bf16)
    kv_scratch = [pltpu.VMEM((SEQ, HW), f32), pltpu.VMEM((SEQ, HW), f32)]
    dqkv_scratch = [w_dd, w_dd, pltpu.VMEM((T, D), bf16), pltpu.VMEM((T, D), bf16), sems(2)]

    table = sds((2 * T, 128), f32)
    h1_a, h1_b, buf_a, buf_b, cos, sin = call(
        first_kernel, [row_low, row_low, qkv_shape, qkv_shape, table, table],
        vm(tokens, positions, first_gain) + [(ANY, query_weight), (ANY, key_value_matrix)],
        [w_dd, w_dd, sems(2)], flops=6e8,
    )
    down = lambda v: lax.ppermute(v, "section", [(0, 1)])
    buf = jnp.where(first, buf_a, down(buf_b))
    h1_b = down(h1_b)

    late = lambda v: tied(v, buf_a)
    wo_all = both(late(output_weight))
    g1, g2 = (jnp.stack(either_order(first, v, swap(late(v)))) for v in (first_gain, second_gain))
    router = jnp.concatenate(either_order(first, router_weight, swap(late(router_weight))), axis=0)
    ids_sent = swap(late(lax.dynamic_slice(expert_ids, (0, 1 - s, 0, 0, 0), (1, 1, 1, T, 8)))).reshape(T, 8)
    (pair,) = call(
        pair_kernel, [sds((1, 2, D, 3 * F), bf16)], [(ANY, tied(v, buf)) for v in (expert_in, expert_out)],
        [pltpu.VMEM((2, D, 3 * F), bf16), sems(8)], out_spec=ANY,
    )
    route = [sds((SLOTS, T), bf16), sds((T, SLOTS), bf16), sds((T, E), f32)]

    qkv_0, (pair, g1, g2, router, ids_sent) = with_(all_to_all(buf, CTX), (pair, g1, g2, router, ids_sent))
    ex_w = [(ANY, both(pair))]
    s0, st0, m0, s1, st1, m1 = call(
        prep_kernel, route + route, vm(expert_ids, ids_sent), flops=1e7
    )
    buf, qkv_0, pos_all = call(
        functools.partial(attend_kernel, 0), [o_shape, qkv_saved, sds((SEQ, 1), f32)], pin(qkv_0), flops=4e8
    )
    o_in = all_to_all(buf, CTX)
    q_sent, kv_sent = swap(tied(query_weight, o_in)), swap(tied(key_value_matrix, o_in))
    cos_all, sin_all = call(table_kernel, [sds((SEQ, 128), f32)] * 2, vm(pos_all))

    def middle(layer, o_in, x, s_l, m_l, *h1):
        return call(
            functools.partial(mid_kernel, layer),
            [row_full, row_low, gates_shape, sds((T, 2 * D), bf16), rows_shape],
            pin(o_in) + vm(x) + [(ANY, wo_all)] + vm(g2, router, s_l, m_l, *h1), [w_dd, sems(1)], flops=2e8,
        )

    row_block = sds((ROWS_OF, D), bf16)
    narrow = sds((ROWS_OF, D + 3 * F), bf16)

    def experts_forward(layer, rows):
        return call(
            functools.partial(expert_forward_kernel, layer),
            [rows_shape, sds((2, ROWS_OF, 2 * F), f32), row_block, row_block],
            pin(rows) + ex_w, ex_scratch, flops=2e9,
        )

    def experts_back(layer, rows, gu):
        return call(
            functools.partial(expert_back_kernel, layer), [rows_shape, narrow, narrow],
            pin(rows) + [(ANY, gu)] + ex_w,
            [ex_scratch[0], pltpu.VMEM((2, ROWS_OF, 2 * F), f32), sems(4)], flops=2e9,
        )

    def expert_grad(x_keep, x_got, keep, send):
        return call(
            expert_grad_kernel, [sds((D, 3 * F), bf16)], vm(x_keep) + pin(x_got) + vm(keep) + pin(swap(send)), flops=2e9
        )[0]

    mid_0, h2_0, gates_0, pair_0, buf = middle(0, o_in, tokens, s0, m0, h1_a, h1_b)
    x_rows, (cos_all, sin_all, q_sent, kv_sent) = with_(
        all_to_all(buf, GROUP), (cos_all, sin_all, q_sent, kv_sent)
    )
    qkv_w = [(ANY, v) for v in (query_weight, q_sent, key_value_matrix, kv_sent)]
    buf, gu_0, x_keep_0, x_send = experts_forward(0, x_rows)
    row_0 = gather(pair_0, "x")
    y_0, (row_0,) = with_(all_to_all(buf, GROUP), (row_0,))
    all_0 = gather(row_0, "y")
    x_got_0 = swap(x_send)

    out_0, h1_1, y_0, buf = call(
        next_kernel, [row_low, row_low, rows_saved, qkv_shape],
        pin(y_0) + vm(mid_0, gates_0, st0, cos, sin, g1) + qkv_w,
        [w_dd, w_dd, sems(2)], flops=5e8,
    )
    qkv_1 = all_to_all(buf, CTX)
    buf, qkv_1 = call(
        functools.partial(attend_kernel, 1), [o_shape, qkv_saved], pin(qkv_1) + vm(pos_all), flops=4e8
    )
    mid_1, h2_1, gates_1, pair_1, buf = middle(1, all_to_all(buf, CTX), out_0, s1, m1, h1_1)

    (dy_buf,) = call(send_back_kernel, [rows_shape], vm(gates_1, s1, cotangent), flops=2e8)
    x_rows, (dy_buf, pair_1, all_0) = with_(all_to_all(buf, GROUP), (dy_buf, pair_1, all_0))
    row_1 = gather(pair_1, "x")
    dy_rows = all_to_all(dy_buf, GROUP)
    buf, gu_1, x_keep, x_send = experts_forward(1, x_rows)
    dy_rows, (buf, gu_1) = with_(dy_rows, (buf, gu_1))
    y_1 = all_to_all(buf, GROUP)
    x_got = swap(x_send)
    buf, keep, send = experts_back(1, dy_rows, gu_1)
    y_1, (buf, row_1) = with_(y_1, (buf, row_1))
    all_1 = gather(row_1, "y")
    dx_1 = all_to_all(buf, GROUP)
    out_keep, out_send, dlog_1, dh2 = call(
        functools.partial(route_back_kernel, 1), [row_low, row_low, log_shape, row_full],
        pin(y_1) + vm(gates_1, st1, router, cotangent, mid_1, out_0), flops=5e8,
    )
    part = expert_grad(x_keep, x_got, keep, send)
    dx_1, (part, dh2) = with_(dx_1, (part, dh2))

    def sum_y(part):
        return lax.psum_scatter(part, "y", scatter_dimension=0, tiled=True)

    def turn(layer, dx, st, dh2, mid, g):
        return call(
            functools.partial(turn_kernel, layer), [row_full, row_low, qkv_half],
            pin(dx) + vm(st, dh2, mid, g2, g) + [(ANY, wo_all)], [w_dd, sems(1)], flops=5e8,
        )

    def attend_back(qkv, do):
        return call(
            attend_back_kernel, [back_shape, back_saved, o_saved], vm(qkv) + pin(do) + vm(pos_all), kv_scratch, flops=1e9
        )

    def heads(layer, back, da, pairs, h2, dlog, dhn2, *other):
        return call(
            functools.partial(head_grad_kernel, layer),
            [sds((D, WIDE), bf16) if layer else pinned((D, 2 * WIDE), bf16)],
            vm(back, da, cos_all, sin_all, pairs, h2, dlog, dhn2, *other), flops=8e8,
        )[0]

    def expert_rows(rows):
        return call(expert_rows_kernel, [sds((T, 3 * F), bf16)] * 4, vm(rows))

    def placed(keep, send):
        return call(place_kernel, [sds((1, 2, 1, T, D), keep.dtype)], vm(keep) + pin(swap(send)))[0]

    dmid_1, dhn2_1, buf = turn(1, dx_1, st1, dh2, mid_1, cotangent)
    buf, back_1, da_1 = attend_back(qkv_1, all_to_all(buf, CTX))
    dqkv, (part, all_1) = with_(all_to_all(buf, CTX), (part, all_1))
    ex_1 = sum_y(part)
    head_part_1 = heads(1, back_1, da_1, all_1, h2_1, dlog_1, dhn2_1)
    layer_out = placed(out_keep, out_send)
    grad_1, g_0, buf = call(
        functools.partial(back_kernel, 1), [row_full, row_low, rows_shape],
        pin(dqkv) + vm(out_0, dmid_1, cos, sin, g1) + qkv_w + vm(s0, gates_0),
        dqkv_scratch, flops=4e8,
    )

    dy_rows, (layer_out,) = with_(all_to_all(buf, GROUP), (layer_out,))
    buf, keep, send = experts_back(0, dy_rows, gu_0)
    dx_0 = all_to_all(buf, GROUP)
    dlog_0, dh2 = call(
        functools.partial(route_back_kernel, 0), [log_shape, row_full],
        vm(y_0, gates_0, st0, router, g_0), flops=3e8,
    )
    part = expert_grad(x_keep_0, x_got_0, keep, send)
    dx_0, (part, dh2, ex_1) = with_(dx_0, (part, dh2, ex_1))
    ex_0 = sum_y(part)
    ex_1_sent = round_trip(expert_rows(ex_1), "x")
    dmid_0, dhn2_0, buf = turn(0, dx_0, st0, dh2, mid_0, g_0)
    do_in, (head_part_1,) = with_(all_to_all(buf, CTX), (head_part_1,))
    buf, back_0, da_0 = attend_back(qkv_0, do_in)
    buf, ex_1 = with_(buf, ex_1_sent)
    dqkv = all_to_all(buf, CTX)
    rows_0 = expert_rows(ex_0)
    head_part = heads(0, back_0, da_0, all_0, h2_0, dlog_0, dhn2_0, head_part_1)
    full = all_to_all(head_part.reshape(64, 16, 2 * WIDE), ALL)
    grad_keep, grad_send = call(
        functools.partial(back_kernel, 0), [row_full, row_full],
        pin(tied(dqkv, *rows_0)) + vm(tokens, dmid_0, cos, sin, g1) + qkv_w + vm(grad_1), dqkv_scratch, flops=3e8,
    )

    ex_0 = round_trip(rows_0, "x")
    input_grad = placed(grad_keep, grad_send)
    (*ex_0, input_grad) = lax.optimization_barrier((*ex_0, input_grad))
    four = sds((4, T, 3 * F), bf16)
    keep, send = call(expert_sort_kernel, [four, four], vm(ex_0[0]) + pin(*ex_0[1:]) + vm(*ex_1))
    ex_in, ex_out = call(
        expert_final_kernel, [sds((1, 8, T, 2 * F), f32), sds((1, 8, T, F), f32)], vm(keep) + pin(swap(send))
    )
    full, (ex_in, ex_out, input_grad) = with_(full, (ex_in, ex_out, input_grad))
    sums = sds((16, 3 * D + 128), f32)
    keep, send = call(halves_kernel, [sums, sums], pin(full))
    mat = sds((1, 16, D), f32)
    row = sds((1, 16), f32)
    grad_q, grad_kv, grad_o, router_grad, first_grad, second_grad = call(
        final_kernel, [mat, mat, mat, sds((1, 16, E), f32), row, row],
        vm(keep) + pin(swap(send)) + [(ANY, query_weight), (ANY, key_value_matrix)] + vm(first_gain),
        [pltpu.VMEM((16, D), bf16), pltpu.VMEM((16, D), bf16), sems(2)],
    )
    return (
        layer_out, input_grad, first_grad, grad_q, grad_kv, grad_o, second_grad, router_grad, ex_in, ex_out,
    )


def solution(mesh):
    grid = Mesh(mesh.devices.reshape(2, 4, 4, 4), ("section", "y", "x", "expert"))
    ctx = ("y", "x")
    every = ("y", "x", "expert")
    placed = (
        P(None, "expert", ctx, None),
        P(None, "expert", ctx),
        P("section", None, "expert", ctx, None),
        P(None, "expert", ctx, None),
        P("section", None),
        P("section", None, None),
        P("section", None, None),
        P("section", None, None),
        P("section", None),
        P("section", None, None),
        P("section", "expert", None, None),
        P("section", "expert", None, None),
    )
    return jax.shard_map(
        local,
        mesh=grid,
        in_specs=placed,
        out_specs=(
            P("section", None, "expert", ctx, None),
            P("section", None, "expert", ctx, None),
            P("section", every),
            P("section", every, None),
            P("section", every, None),
            P("section", every, None),
            P("section", every),
            P("section", every, None),
            P("section", "expert", ctx, None),
            P("section", "expert", ctx, None),
        ),
        check_vma=False,
    )
```

```python
import functools
import math

import jax
import jax.numpy as jnp
from jax import lax
from jax.experimental import pallas as pl
from jax.experimental.pallas import tpu as pltpu
from jax.sharding import Mesh
from jax.sharding import PartitionSpec as P

T = 64
D = 1024
HW = 64
WIDE = 5 * HW
NQ = 16
NK = 8
F = 512
E = 32
CAP = 17
MAIN = E * 16
SLOTS = E * CAP
GROUP_SIZE = 16
ROWS_OF = GROUP_SIZE * CAP
N_CTX = 16
SEQ = N_CTX * T

eps = 1e-06
rope_base = 10000.0
masked = -1e30
f32 = jnp.float32
bf16 = jnp.bfloat16

VMEM = pl.BlockSpec(memory_space=pltpu.VMEM)
SMEM = pl.BlockSpec(memory_space=pltpu.SMEM)
ANY = pl.BlockSpec(memory_space=pl.ANY)
PIN = "pinned"
GROUP = ("x", "expert")
CTX = ("y", "x")
ALL = ("y", "x", "expert")


def sds(shape, dtype):
    return jax.ShapeDtypeStruct(shape, dtype)


def pinned(shape, dtype):
    return pltpu.VMEM(shape, dtype)


def call(body, outs, ins, scratch=(), flops=0, limit=36, out_spec=VMEM):
    place = lambda k, a: a if k is SMEM else pltpu.with_memory_space_constraint(a, pltpu.VMEM if k is PIN else pltpu.HBM)
    outs = [o if isinstance(o, jax.ShapeDtypeStruct) is False else pltpu.HBM(o.shape, o.dtype) for o in outs]
    read = sum(a.size * a.dtype.itemsize for k, a in ins if k is VMEM)
    written = sum(math.prod(o.shape) * jnp.dtype(o.dtype).itemsize for o in outs)
    return pl.pallas_call(
        body,
        out_shape=list(outs),
        in_specs=[VMEM if k is PIN else k for k, _ in ins],
        out_specs=[out_spec] * len(outs),
        scratch_shapes=list(scratch),
        compiler_params=pltpu.CompilerParams(vmem_limit_bytes=limit * 1024 * 1024),
        cost_estimate=pl.CostEstimate(
            flops=int(flops), bytes_accessed=int(read + written), transcendentals=0
        ),
    )(*[place(k, a) for k, a in ins])


def dot(a, b):
    return lax.dot_general(a, b, (((1,), (0,)), ((), ())), preferred_element_type=f32)


def dot_nt(a, b):
    return lax.dot_general(a, b, (((1,), (1,)), ((), ())), preferred_element_type=f32)


def dot_tn(a, b):
    return lax.dot_general(a, b, (((0,), (0,)), ((), ())), preferred_element_type=f32)


def split(v):
    high = v.astype(bf16)
    return high, (v - high.astype(f32)).astype(bf16)


def iota(shape, dim):
    return lax.broadcasted_iota(jnp.int32, shape, dim)


def one_hot(cond):
    return jnp.where(cond, 1.0, 0.0).astype(bf16)


def expert_of(k):
    return 8 * ((k >> 1) & 3) + 2 * (k >> 3) + (k & 1)


def slot_table():
    row, col = iota((SLOTS, E), 0), iota((SLOTS, E), 1)
    return one_hot(expert_of(jnp.where(row < MAIN, row >> 4, row - MAIN)) == col)


def moved_rows(index, q, order):
    bits = q.bit_length() - 1
    if order == "block":
        return index >> (bits + 1), (index >> 1) & (q - 1), index & 1
    if order == "token":
        return (index >> 1) & 15, index >> 5, index & 1
    return index & 15, (index >> 4) & (q - 1), index >> (bits + 4)


def shuffle(q, to, order):
    n = 32 * q
    d, p, i = moved_rows(iota((n, n), 0), q, to)
    at = iota((n, n), 1)
    if order == "block":
        return one_hot(at == d * (2 * q) + p * 2 + i)
    if order == "token":
        return one_hot(at == p * 32 + d * 2 + i)
    return one_hot(at == (i * q + p) * 16 + d)


def pack(buf_ref, parts):
    n = len(parts)
    extra = []
    for k, rows in enumerate(parts):
        for c in range(8):
            piece = rows[:, c * 128 : (c + 1) * 128]
            buf_ref[:, k * 256 + c * 32 : k * 256 + (c + 1) * 32, :] = piece[:MAIN].reshape(16, 32, 128)
            extra.append(piece[MAIN:])
    moved = dot(shuffle(8 * n, "block", "token"), jnp.concatenate(extra, axis=0)).astype(bf16)
    buf_ref[:, 256 * n :, :] = moved.reshape(16, 16 * n, 128)


def unpack(buf_ref, n):
    rest = buf_ref[:, 256 * n :, :].reshape(256 * n, 128)
    moved = dot(shuffle(8 * n, "token", "block"), rest).astype(bf16)
    parts = []
    for k in range(n):
        pieces = []
        for c in range(8):
            head = buf_ref[:, k * 256 + c * 32 : k * 256 + (c + 1) * 32, :].reshape(MAIN, 128)
            at = (k * 8 + c) * E
            pieces.append(jnp.concatenate([head, moved[at : at + E]], axis=0))
        parts.append(jnp.concatenate(pieces, axis=1))
    return parts


def pack_experts(buf_ref, parts):
    n = len(parts)
    extra = []
    for i in range(2):
        for k in range(n):
            for c in range(8):
                piece = parts[k][i][:, c * 128 : (c + 1) * 128]
                at = k * 256 + c * 32 + i * 16
                buf_ref[:, at : at + 16, :] = piece[:256].reshape(16, 16, 128)
                extra.append(piece[256:])
    moved = dot(shuffle(8 * n, "block", "expert"), jnp.concatenate(extra, axis=0)).astype(bf16)
    buf_ref[:, 256 * n :, :] = moved.reshape(16, 16 * n, 128)


def unpack_experts(buf_ref, n):
    rest = buf_ref[:, 256 * n :, :].reshape(256 * n, 128)
    moved = dot(shuffle(8 * n, "expert", "block"), rest).astype(bf16)
    parts = []
    for k in range(n):
        both = []
        for i in range(2):
            pieces = []
            for c in range(8):
                at = k * 256 + c * 32 + i * 16
                head = buf_ref[:, at : at + 16, :].reshape(256, 128)
                at = (i * 8 * n + k * 8 + c) * 16
                pieces.append(jnp.concatenate([head, moved[at : at + 16]], axis=0))
            both.append(jnp.concatenate(pieces, axis=1))
        parts.append(both)
    return parts


def norm_parts(v):
    r = lax.rsqrt(jnp.mean(v * v, axis=-1, keepdims=True) + eps)
    return r, v * r


def norm_back(v, gain, dh):
    r, n = norm_parts(v)
    a = gain * dh
    return r * (a - n * jnp.mean(n * a, axis=-1, keepdims=True)), dh * n


def rotate(chunk, cos, sin):
    lane = iota(chunk.shape, 1) & 63
    other = jnp.where(lane < 32, pltpu.roll(chunk, 96, 1), pltpu.roll(chunk, 32, 1))
    return chunk * cos + other * sin


class Copy:
    def __init__(self, ref, place, sem):
        self.copy = pltpu.make_async_copy(ref, place, sem)
        self.copy.start()

    def wait(self):
        self.copy.wait()


def at_axis(axis):
    return lax.axis_index(axis)


class Chosen(Copy):
    def __init__(self, layer, own, sent, place, sem):
        self.copy = pltpu.make_async_copy(own, place, sem)
        mine = at_axis("section") == layer

        @pl.when(mine)
        def _():
            self.copy.start()

        @pl.when(jnp.logical_not(mine))
        def _():
            pltpu.make_async_copy(sent, place, sem).start()


def either(layer, own, sent):
    return jnp.where(at_axis("section") == layer, own, sent)


def prep_kernel(ids_own, ids_sent, s0, st0, m0, s1, st1, m1):
    rep = slot_table()
    own = ids_own[0, at_axis("section"), 0]
    sent = ids_sent[...]
    for layer, (s_ref, st_ref, m_ref) in enumerate(((s0, st0, m0), (s1, st1, m1))):
        ids = either(layer, own, sent)
        col = iota((T, E), 1)
        member = jnp.zeros((T, E), f32)
        for k in range(8):
            member = member + jnp.where(ids[:, k : k + 1] == col, 1.0, 0.0)
        m_ref[...] = member
        low = member.astype(bf16)
        row64, col64 = iota((T, T), 0), iota((T, T), 1)
        rank = dot(one_hot(col64 < row64), low)
        rank = jnp.where(member > 0.5, rank, -1.0).astype(bf16)
        at = dot_nt(rank, rep)
        slot = iota((T, SLOTS), 1)
        place = jnp.where(slot < MAIN, slot & 15, 16).astype(f32)
        st_ref[...] = one_hot(at == place)
        eye = one_hot(iota((E, E), 0) == iota((E, E), 1))
        member_t = dot_nt(eye, low)
        rank_t = dot(member_t.astype(bf16), one_hot(row64 < col64))
        rank_t = jnp.where(member_t > 0.5, rank_t, -1.0).astype(bf16)
        at_t = dot(rep, rank_t)
        slot_t = iota((SLOTS, T), 0)
        place_t = jnp.where(slot_t < MAIN, slot_t & 15, 16).astype(f32)
        s_ref[...] = one_hot(at_t == place_t)


def pair_kernel(in_own, out_own, experts, at, sems):
    moves = []

    def move(source, place, target):
        n = len(moves)
        first = pltpu.make_async_copy(source, place, sems.at[2 * n])
        moves.append((first, pltpu.make_async_copy(place, target, sems.at[2 * n + 1])))
        first.start()

    for i in range(2):
        e = 2 * at_axis("x") + i
        move(in_own.at[0, e], at.at[i, :, : 2 * F], experts.at[0, i, :, : 2 * F])
        move(out_own.at[0, e], at.at[i, :, 2 * F :], experts.at[0, i, :, 2 * F :])
    for first, second in moves:
        first.wait()
        second.start()
    for _, second in moves:
        second.wait()


def qkv_pack(q, kv, cos, sin, pos, buf_ref):
    hi = jnp.floor(pos * (1.0 / 32.0))
    lo = pos - hi * 32.0
    lane = iota((T, 64), 1)
    where_am_i = jnp.where(lane == 0, hi, jnp.where(lane == 1, lo, 0.0)).astype(bf16)
    for pair in range(4):
        k_two = rotate(kv[:, pair * 128 : (pair + 1) * 128], cos, sin).astype(bf16)
        v_two = kv[:, 512 + pair * 128 : 512 + (pair + 1) * 128].astype(bf16)
        for g in range(2):
            k_one = k_two[:, g * 64 : (g + 1) * 64]
            v_one = v_two[:, g * 64 : (g + 1) * 64]
            group = pair * 2 + g
            q_two = rotate(q[:, group * 128 : (group + 1) * 128], cos, sin).astype(bf16)
            low_half = jnp.concatenate([v_one, where_am_i], axis=1)
            for j in range(2):
                top = jnp.concatenate([q_two[:, j * 64 : (j + 1) * 64], k_one], axis=1)
                buf_ref[2 * group + j, 0:T, :] = top
                buf_ref[2 * group + j, T : 2 * T, :] = low_half


def rotary(pos):
    rows = pos.shape[0]
    lane = iota((rows, 128), 1)
    frequency = jnp.exp((lane & 31).astype(f32) * (-2.0 * math.log(rope_base) / HW))
    angles = pos * frequency
    sin = jnp.sin(angles)
    return jnp.cos(angles), jnp.where((lane & 63) < 32, -sin, sin)


def table_kernel(pos, cos, sin):
    for start in range(0, SEQ, 256):
        at = slice(start, start + 256)
        cos[at], sin[at] = rotary(pos[at])


def first_kernel(tok, places, gain, q_own, kv_own, h1_a, h1_b, buf_a, buf_b, cos_ref, sin_ref, q_w, kv_w, sems):
    q_copy = pltpu.make_async_copy(q_own.at[0], q_w, sems.at[0])
    kv_copy = pltpu.make_async_copy(kv_own.at[0], kv_w, sems.at[1])
    q_copy.start()
    kv_copy.start()
    x = jnp.concatenate([tok[0, 0], tok[1, 0]], axis=0).astype(f32)
    h1 = (norm_parts(x)[1] * gain[...]).astype(bf16)
    h1_a[...] = h1[:T]
    h1_b[...] = h1[T:]
    eye = iota((T, T), 0) == iota((T, T), 1)
    columns = [
        jnp.sum(jnp.where(eye, places[m].astype(f32), 0.0), axis=1, keepdims=True) for m in range(2)
    ]
    pos = jnp.concatenate(columns, axis=0)
    cos, sin = rotary(pos)
    cos_ref[...] = cos
    sin_ref[...] = sin
    q_copy.wait()
    q = dot(h1, q_w[...])
    kv_copy.wait()
    kv = dot(h1, kv_w[...])
    for m, buf_ref in enumerate((buf_a, buf_b)):
        at = slice(m * T, (m + 1) * T)
        qkv_pack(q[at], kv[at], cos[at], sin[at], pos[at], buf_ref)


def attention_parts(buf):
    q = buf[:, 0:T, 0:HW].reshape(SEQ, HW)
    k = buf[:, 0:T, HW : 2 * HW].reshape(SEQ, HW)
    v = buf[:, T : 2 * T, 0:HW].reshape(SEQ, HW)
    return q, k, v


def sent_positions(buf):
    hi = buf[:, T : 2 * T, HW : HW + 1].reshape(SEQ, 1).astype(f32)
    lo = buf[:, T : 2 * T, HW + 1 : HW + 2].reshape(SEQ, 1).astype(f32)
    return hi * 32.0 + lo


def block_probs(q, k, pos, start, rows):
    keys = start + rows
    scores = dot_nt(q[start : start + rows], k[:keys]) * (HW**-0.5)
    at = (iota((rows, keys), 0) + start).astype(f32)
    key = iota((rows, keys), 1).astype(f32)
    begin = at[:, 0:1] - pos[start : start + rows]
    scores = jnp.where((key <= at) & (key >= begin), scores, masked)
    raised = jnp.exp(scores - jnp.max(scores, axis=-1, keepdims=True))
    return raised / jnp.sum(raised, axis=-1, keepdims=True)


ROWS = 256


def attend_kernel(layer, buf_ref, *refs):
    q, k, v = attention_parts(buf_ref[...])
    if layer == 0:
        out_ref, kept, pos_ref = refs
        pos = sent_positions(buf_ref[...])
        pos_ref[...] = pos
    else:
        pos_ref, out_ref, kept = refs
        pos = pos_ref[...]
    kept[...] = buf_ref[...]
    for start in range(0, SEQ, ROWS):
        probs = block_probs(q, k, pos, start, ROWS)
        o = dot(probs.astype(bf16), v[: start + ROWS]).astype(bf16)
        for b in range(ROWS // T):
            piece = o[b * T : (b + 1) * T]
            out_ref[start // T + b] = jnp.concatenate([piece[: T // 2], piece[T // 2 :]], axis=1)


def heads_in(buf_ref, o_ref):
    for g in range(8):
        a, b = buf_ref[2 * g], buf_ref[2 * g + 1]
        o_ref[0 : T // 2, g * 128 : (g + 1) * 128] = jnp.concatenate([a[:, :64], b[:, :64]], axis=1)
        o_ref[T // 2 : T, g * 128 : (g + 1) * 128] = jnp.concatenate([a[:, 64:], b[:, 64:]], axis=1)


def heads_out(do, buf_ref, start):
    for g in range(8):
        two = do[:, g * 128 : (g + 1) * 128]
        for j in range(2):
            one = two[:, j * 64 : (j + 1) * 64]
            block = jnp.concatenate([one[: T // 2], one[T // 2 :]], axis=1)
            buf_ref[2 * g + j, start : start + T // 2, :] = block


def gates_from(logits, member):
    chosen = member > 0.5
    largest = jnp.max(jnp.where(chosen, logits, masked), axis=-1, keepdims=True)
    raised = jnp.where(chosen, jnp.exp(jnp.minimum(logits - largest, 0.0)), 0.0)
    return raised / jnp.sum(raised, axis=-1, keepdims=True)


def gated_rows(gates, s, rep, g_low):
    high, low = split(gates)
    up = (s * dot_nt(rep, high).astype(bf16)).astype(bf16)
    down = (s * dot_nt(rep, low).astype(bf16)).astype(bf16)
    return (dot(up, g_low) + dot(down, g_low)).astype(bf16)


def mid_kernel(layer, *refs):
    ob, x_ref, wo_all, gain, r_ref, s_ref, m_ref = refs[:7]
    h1_refs, (mid_ref, h2_ref, gates_ref, pair_ref, buf_ref, wo, sems) = refs[7:-7], refs[-7:]
    copy = Copy(wo_all.at[layer], wo, sems.at[0])
    o_ref = pair_ref.at[:, D:]
    heads_in(ob, o_ref)
    if layer == 0:
        pair_ref[:, :D] = jnp.where(at_axis("section") == 0, h1_refs[0][...], h1_refs[1][...])
    else:
        pair_ref[:, :D] = h1_refs[0][...]
    x = (tok_row(x_ref) if layer == 0 else x_ref[...]).astype(f32)
    copy.wait()
    middle = x + dot(o_ref[...], wo[...])
    mid_ref[...] = middle
    h2 = (norm_parts(middle)[1] * gain[layer]).astype(bf16)
    h2_ref[...] = h2
    pack(buf_ref, [dot(s_ref[...], h2).astype(bf16)])
    gates_ref[...] = gates_from(dot(h2, r_ref[layer]), m_ref[...])


def send_back_kernel(gates, s_ref, cot, buf_ref):
    pack(buf_ref, [gated_rows(gates[...], s_ref[...], slot_table(), tok_row(cot))])


def tok_row(ref):
    return ref[at_axis("section"), 0]


def hidden_of(gu):
    gate, up = gu[:, :F], gu[:, F:]
    sg = jax.nn.sigmoid(gate)
    return gate, up, sg, (gate * sg * up).astype(bf16)


def sorted_out(i, keep, send, at, value):
    cols = slice(at, at + value.shape[1])

    @pl.when(at_axis("section") == i)
    def _():
        keep[:, cols] = value

    @pl.when(at_axis("section") != i)
    def _():
        send[:, cols] = value


def expert_forward_kernel(layer, buf, w_all, ybuf, gu_ref, keep, send, w, sems):
    copies = [Copy(w_all.at[layer, i], w.at[i], sems.at[i]) for i in range(2)]
    (x,) = unpack_experts(buf, 1)
    y = []
    for i in range(2):
        copies[i].wait()
        gu = dot(x[i], w[i, :, : 2 * F])
        gu_ref[i] = gu
        y.append(dot_nt(hidden_of(gu)[3], w[i, :, 2 * F :]).astype(bf16))
        sorted_out(i, keep, send, 0, x[i])
    pack_experts(ybuf, [y])


def expert_back(dy, gu, w_in, w_out):
    gate, up, sg, z = hidden_of(gu)
    dz = dot(dy, w_out)
    dgate = dz * up * (sg + gate * sg * (1.0 - sg))
    dup = dz * gate * sg
    dgu = jnp.concatenate([dgate, dup], axis=1).astype(bf16)
    return z, dgu, dot_nt(dgu, w_in).astype(bf16)


def expert_back_kernel(layer, buf, gu_all, w_all, back, keep, send, w, gu, sems):
    copies = []
    for i in range(2):
        copies.append(Copy(w_all.at[layer, i], w.at[i], sems.at[i]))
        copies.append(Copy(gu_all.at[i], gu.at[i], sems.at[2 + i]))
    (dy,) = unpack_experts(buf, 1)
    dx = []
    for i in range(2):
        copies[2 * i].wait()
        copies[2 * i + 1].wait()
        z, dgu, dx_i = expert_back(dy[i], gu[i], w[i, :, : 2 * F], w[i, :, 2 * F :])
        dx.append(dx_i)
        for at, value in ((0, dy[i]), (D, dgu), (D + 2 * F, z)):
            sorted_out(i, keep, send, at, value)
    pack_experts(back, [dx])


def expert_grad_kernel(x_keep, x_got, keep, got, out):
    x = jnp.concatenate([x_keep[...], x_got[...]], axis=0)
    dy = jnp.concatenate([keep[:, :D], got[:, :D]], axis=0)
    dgu = jnp.concatenate([keep[:, D : D + 2 * F], got[:, D : D + 2 * F]], axis=0)
    z = jnp.concatenate([keep[:, D + 2 * F : D + 3 * F], got[:, D + 2 * F : D + 3 * F]], axis=0)
    out[:, : 2 * F] = dot_tn(x, dgu).astype(bf16)
    out[:, 2 * F :] = dot_tn(dy, z).astype(bf16)


def expert_rows_kernel(rows, b0, b1, b2, b3):
    for k, b in enumerate((b0, b1, b2, b3)):
        at = pl.multiple_of(((at_axis("x") + k) & 3) * T, T)
        b[...] = rows[pl.ds(at, T), :]


def expert_sort_kernel(*refs):
    keep, send = refs[8:]
    for layer in range(2):
        for k in range(4):
            block = refs[4 * layer + k]
            place = (at_axis("x") - k) & 3

            @pl.when(at_axis("section") == layer)
            def _():
                keep[place] = block[...]

            @pl.when(at_axis("section") != layer)
            def _():
                send[place] = block[...]


def expert_final_kernel(keep, got, out_in, out_out):
    for x in range(4):
        for ref, j in ((keep, at_axis("section")), (got, 1 - at_axis("section"))):
            out_in[0, 2 * x + j] = ref[x, :, : 2 * F].astype(f32)
            out_out[0, 2 * x + j] = ref[x, :, 2 * F :].astype(f32)


def place_kernel(keep, got, out):
    out[0, at_axis("section"), 0] = keep[...]
    out[0, 1 - at_axis("section"), 0] = got[...]


def by_section(v_0, v_1, keep, send):
    keep[...] = jnp.where(at_axis("section") == 0, v_0, v_1)
    send[...] = jnp.where(at_axis("section") == 0, v_1, v_0)


def combine(middle, gates, st, rep, y):
    high, low = split(gates)
    up = (st * dot_nt(high, rep).astype(bf16)).astype(bf16)
    down = (st * dot_nt(low, rep).astype(bf16)).astype(bf16)
    return middle + (dot(up, y) + dot(down, y))


def micro_rows(ref):
    return ref[pl.ds(pl.multiple_of(at_axis("section") * T, T), T), :]


def next_kernel(
    yb, mid, gates, st, cos, sin, gain, q_own, q_sent, kv_own, kv_sent, out_ref, h1_ref, saved, buf_ref, q_w, kv_w, sems,
):
    saved[...] = yb[...]
    q_copy = Chosen(1, q_own.at[0], q_sent.at[0], q_w, sems.at[0])
    kv_copy = Chosen(1, kv_own.at[0], kv_sent.at[0], kv_w, sems.at[1])
    (y,) = unpack(yb, 1)
    out = combine(mid[...], gates[...], st[...], slot_table(), y).astype(bf16)
    out_ref[...] = out
    h1 = (norm_parts(out.astype(f32))[1] * gain[1]).astype(bf16)
    h1_ref[...] = h1
    q_copy.wait()
    q = dot(h1, q_w[...])
    kv_copy.wait()
    kv = dot(h1, kv_w[...])
    qkv_pack(q, kv, micro_rows(cos), micro_rows(sin), jnp.zeros((T, 1), f32), buf_ref)


def route_back_kernel(layer, *refs):
    yb, gates_ref, st_ref, r_ref, g_ref = refs[:5]
    dlog_ref, dh2_ref = refs[-2:]
    rep, st, gates = slot_table(), st_ref[...], gates_ref[...]
    (y,) = unpack(yb, 1)
    if layer == 1:
        mid, out_0, keep, send = refs[5:9]
        g_low = tok_row(g_ref)
        by_section(out_0[...], combine(mid[...], gates, st, rep, y).astype(bf16), keep, send)
    else:
        g_low = g_ref[...]
    d_slot = dot_nt(g_low, y) * st.astype(f32)
    high, low = split(d_slot)
    d_gates = dot(high, rep) + dot(low, rep)
    d_chosen = gates * (d_gates - jnp.sum(gates * d_gates, axis=-1, keepdims=True))
    d_log = d_chosen.astype(bf16)
    dlog_ref[...] = d_log
    dh2_ref[...] = dot_nt(d_log, r_ref[layer])


def turn_kernel(layer, *refs):
    dxb, st, dh2, mid, gain, g_ref, wo_all, dmid_ref, dhn_ref, dobuf, wo, sems = refs
    copy = Copy(wo_all.at[layer], wo, sems.at[0])
    (dx,) = unpack(dxb, 1)
    g_low = tok_row(g_ref) if layer == 1 else g_ref[...]
    d_h2 = dot(st[...], dx) + dh2[...]
    d_v, d_hn = norm_back(mid[...], gain[layer], d_h2)
    d_mid = g_low.astype(f32) + d_v
    d_a = d_mid.astype(bf16)
    heads_out(d_a, dobuf, T // 2)
    copy.wait()
    heads_out(dot_nt(d_a, wo[...]).astype(bf16), dobuf, 0)
    dmid_ref[...] = d_mid
    dhn_ref[...] = d_hn.astype(bf16)


def attend_back_kernel(buf_ref, dobuf, pos_ref, out_ref, saved, da_saved, dk_ref, dv_ref):
    q, k, v = attention_parts(buf_ref[...])
    pos = pos_ref[...]
    da_saved[...] = dobuf[:, T // 2 :, :]
    packed = dobuf[:, : T // 2, :]
    do = halves(packed)
    scale = HW**-0.5
    dq = []
    for start in reversed(range(0, SEQ, ROWS)):
        keys = start + ROWS
        probs = block_probs(q, k, pos, start, ROWS)
        do_rows = do[start:keys]
        d_probs = dot_nt(do_rows, v[:keys])
        inner = jnp.sum(probs * d_probs, axis=-1, keepdims=True)
        d_scores = (probs * (d_probs - inner)).astype(bf16)
        dq.append((dot(d_scores, k[:keys]) * scale).astype(bf16))
        d_k = dot_tn(d_scores, q[start:keys]) * scale
        d_v = dot_tn(probs.astype(bf16), do_rows)
        if keys == SEQ:
            dk_ref[...] = d_k
            dv_ref[...] = d_v
        else:
            dk_ref[0:keys] = dk_ref[0:keys] + d_k
            dv_ref[0:keys] = dv_ref[0:keys] + d_v
    d_q = jnp.concatenate(dq[::-1], axis=0)
    d_k = dk_ref[...].astype(bf16)
    d_v = dv_ref[...].astype(bf16)
    out_ref[:, 0:T, :] = jnp.concatenate([d_q, d_k], axis=1).reshape(N_CTX, T, 128)
    d_v = d_v.reshape(N_CTX, T, HW)
    out_ref[:, T:, :] = jnp.concatenate([d_v[:, : T // 2], d_v[:, T // 2 :]], axis=2)
    saved[...] = out_ref[...]


def back_kernel(layer, *refs):
    refs = list(refs)
    buf, x_ref, dmid, cos_ref, sin_ref, gain, q_own, q_sent, kv_own, kv_sent = refs[:10]
    refs = refs[10:]
    if layer == 1:
        s_ref, gates_ref = refs[:2]
        refs = refs[2:]
    if layer == 0:
        grad_1 = refs.pop(0)
        keep, send = refs[:2]
        refs = refs[2:]
    else:
        grad_ref = refs.pop(0)
    if layer == 1:
        g_ref, dybuf = refs[:2]
        refs = refs[2:]
    q_w, kv_w, dq_ref, dkv_ref, sems = refs
    q_copy = Chosen(layer, q_own.at[0], q_sent.at[0], q_w, sems.at[0])
    kv_copy = Chosen(layer, kv_own.at[0], kv_sent.at[0], kv_w, sems.at[1])
    cos, sin = micro_rows(cos_ref), -micro_rows(sin_ref)
    half = T // 2
    k_parts, v_parts = [], []
    for g in range(8):
        a, b = buf[2 * g], buf[2 * g + 1]
        q_two = jnp.concatenate([a[:T, :64], b[:T, :64]], axis=1).astype(f32)
        dq_ref[:, g * 128 : (g + 1) * 128] = rotate(q_two, cos, sin).astype(bf16)
        k_parts.append(a[:T, 64:].astype(f32) + b[:T, 64:].astype(f32))
        v_sum = a[T:].astype(f32) + b[T:].astype(f32)
        v_parts.append(jnp.concatenate([v_sum[:, :64], v_sum[:, 64:]], axis=0))
    for p in range(4):
        k_two = jnp.concatenate([k_parts[2 * p], k_parts[2 * p + 1]], axis=1)
        v_two = jnp.concatenate([v_parts[2 * p], v_parts[2 * p + 1]], axis=1)
        dkv_ref[:, p * 128 : (p + 1) * 128] = rotate(k_two, cos, sin).astype(bf16)
        dkv_ref[:, 512 + p * 128 : 512 + (p + 1) * 128] = v_two.astype(bf16)
    q_copy.wait()
    kv_copy.wait()
    d_h1 = dot_nt(dq_ref[...], q_w[...]) + dot_nt(dkv_ref[...], kv_w[...])
    x = (tok_row(x_ref) if layer == 0 else x_ref[...]).astype(f32)
    d_x, _ = norm_back(x, gain[layer], d_h1)
    grad = dmid[...] + d_x
    if layer == 0:
        by_section(grad, grad_1[...], keep, send)
    else:
        grad_ref[...] = grad
        g_low = grad.astype(bf16)
        g_ref[...] = g_low
        pack(dybuf, [gated_rows(gates_ref[...], s_ref[...], slot_table(), g_low)])


def head_grad_kernel(layer, back, da, cos_ref, sin_ref, pairs, h2, dlog, dhn2, *refs):
    out = refs[-1]
    if layer == 0:
        out[:, WIDE:] = refs[0][...]
    cos, sin = cos_ref[...], -sin_ref[...]
    both = rotate(back[:, :T, :].reshape(SEQ, 2 * HW).astype(f32), cos, sin).astype(bf16)
    lane = iota((T, HW), 1)
    logs = jnp.concatenate([dlog[...], jnp.zeros((T, HW - E), bf16)], axis=1)
    extra = dot_tn(logs, h2[...]) + dot_tn(one_hot(lane == E), dhn2[...])
    h1_all = pairs[:, :D]
    out[:, : 2 * HW] = dot_tn(both, h1_all).T.astype(bf16)
    rest = [dot_tn(halves(back[:, T:, :]), h1_all), dot_tn(halves(da[...]), pairs[:, D:]), extra]
    out[:, 2 * HW : WIDE] = jnp.concatenate(rest, axis=0).T.astype(bf16)


def halves(packed):
    return jnp.concatenate([packed[:, :, :HW], packed[:, :, HW:]], axis=1).reshape(SEQ, HW)


def head_sums(got, layer):
    v = []
    cols = slice(WIDE * layer, WIDE * (layer + 1))
    for c in range(N_CTX):
        v.append(sum(got[4 * c + k, :, cols].astype(f32) for k in range(1, 4)) + got[4 * c, :, cols].astype(f32))
    pair = [v[2 * g] + v[2 * g + 1] for g in range(NK)]
    parts = []
    for blocks, at in ((v, 3 * HW), (v, 0), (pair, HW), (pair, 2 * HW)):
        for a, b in zip(blocks[::2], blocks[1::2]):
            parts.append(jnp.concatenate([a[:, at : at + HW], b[:, at : at + HW]], axis=1))
    total = sum(pair[1:]) + pair[0]
    parts.append(total[:, 3 * HW :])
    return jnp.concatenate(parts, axis=1)


def halves_kernel(got, keep, send):
    by_section(head_sums(got, 0), head_sums(got, 1), keep, send)


def final_kernel(keep, got, q_own, kv_own, gain, gq, gkv, go, gr, g1, g2, q_rows, kv_rows, sems):
    first = 16 * at_axis(ALL)
    rows = pl.ds(pl.multiple_of(first, 16), 16)
    copies = [Copy(q_own.at[0, rows], q_rows, sems.at[0]), Copy(kv_own.at[0, rows], kv_rows, sems.at[1])]
    mine = keep[...] + got[...]
    grad_q, grad_kv, rest = mine[:, D : 2 * D], mine[:, 2 * D : 3 * D], mine[:, 3 * D :]
    go[0] = mine[:, :D]
    gq[0] = grad_q
    gkv[0] = grad_kv
    gr[0] = rest[:, HW : HW + E]
    eye = iota((16, 16), 0) == iota((16, 16), 1)
    as_row = lambda column: jnp.sum(jnp.where(eye, column, 0.0), axis=0, keepdims=True)
    g2[...] = as_row(rest[:, HW + E : HW + E + 1])
    here = iota((16, D), 1) == iota((16, D), 0) + first
    gains = jnp.sum(jnp.where(here, gain[...], 0.0), axis=1, keepdims=True)
    for copy in copies:
        copy.wait()
    both = grad_q * q_rows[...].astype(f32) + grad_kv * kv_rows[...].astype(f32)
    g1[...] = as_row(jnp.sum(both, axis=-1, keepdims=True) / gains)


def swap(v):
    return lax.ppermute(v, "section", [(0, 1), (1, 0)])


def either_order(first, mine, other):
    return jnp.where(first, mine, other), jnp.where(first, other, mine)


def all_to_all(v, axes):
    return lax.all_to_all(v, axes, 0, 0, tiled=True)


def local(
    tokens, positions, expert_ids, cotangent, first_gain, query_weight, key_value_matrix,
    output_weight, second_gain, router_weight, expert_in, expert_out,
):
    s, y_at, x_at, z_at = (lax.axis_index(a) for a in ("section", "y", "x", "expert"))
    first = s == 0
    vm = lambda *arrays: [(VMEM, a) for a in arrays]
    pin = lambda *arrays: [(PIN, a) for a in arrays]
    sems = lambda n: pltpu.SemaphoreType.DMA((n,))
    tied = lambda v, *after: lax.optimization_barrier((v,) + after)[0]

    def with_(v, others):
        v, *others = lax.optimization_barrier((v, *others))
        return v, others

    def gather(v, axis):
        return lax.all_gather(v, axis, axis=0, tiled=True)

    def both(v):
        return lax.all_gather(v, "section", axis=0, tiled=True)

    def round_trip(blocks, axis):
        route = lambda k: [(i, (i + k) % 4) for i in range(4)]
        return [blocks[0]] + [lax.ppermute(blocks[k], axis, route(k)) for k in range(1, 4)]

    w_dd = pltpu.VMEM((D, D), bf16)
    ex_scratch = [pltpu.VMEM((2, D, 3 * F), bf16), sems(2)]
    qkv_shape = pinned((N_CTX, 2 * T, 128), bf16)
    o_shape = pinned((N_CTX, T // 2, 128), bf16)
    qkv_half = pinned((N_CTX, T, 128), bf16)
    back_shape = pinned((N_CTX, T + T // 2, 128), bf16)
    rows_shape = pinned((GROUP_SIZE, 272, 128), bf16)
    row_low, row_full = sds((T, D), bf16), sds((T, D), f32)
    gates_shape, log_shape = sds((T, E), f32), sds((T, E), bf16)
    o_saved, back_saved = sds(o_shape.shape, bf16), sds(back_shape.shape, bf16)
    qkv_saved, rows_saved = sds(qkv_shape.shape, bf16), sds(rows_shape.shape, bf16)
    kv_scratch = [pltpu.VMEM((SEQ, HW), f32), pltpu.VMEM((SEQ, HW), f32)]
    dqkv_scratch = [w_dd, w_dd, pltpu.VMEM((T, D), bf16), pltpu.VMEM((T, D), bf16), sems(2)]

    table = sds((2 * T, 128), f32)
    h1_a, h1_b, buf_a, buf_b, cos, sin = call(
        first_kernel, [row_low, row_low, qkv_shape, qkv_shape, table, table],
        vm(tokens, positions, first_gain) + [(ANY, query_weight), (ANY, key_value_matrix)],
        [w_dd, w_dd, sems(2)], flops=6e8,
    )
    down = lambda v: lax.ppermute(v, "section", [(0, 1)])
    buf = jnp.where(first, buf_a, down(buf_b))
    h1_b = down(h1_b)

    late = lambda v: tied(v, buf_a)
    wo_all = both(late(output_weight))
    g1, g2 = (jnp.stack(either_order(first, v, swap(late(v)))) for v in (first_gain, second_gain))
    router = jnp.concatenate(either_order(first, router_weight, swap(late(router_weight))), axis=0)
    ids_sent = swap(late(lax.dynamic_slice(expert_ids, (0, 1 - s, 0, 0, 0), (1, 1, 1, T, 8)))).reshape(T, 8)
    (pair,) = call(
        pair_kernel, [sds((1, 2, D, 3 * F), bf16)], [(ANY, tied(v, buf)) for v in (expert_in, expert_out)],
        [pltpu.VMEM((2, D, 3 * F), bf16), sems(8)], out_spec=ANY,
    )
    route = [sds((SLOTS, T), bf16), sds((T, SLOTS), bf16), sds((T, E), f32)]

    qkv_0, (pair, g1, g2, router, ids_sent) = with_(all_to_all(buf, CTX), (pair, g1, g2, router, ids_sent))
    ex_w = [(ANY, both(pair))]
    s0, st0, m0, s1, st1, m1 = call(
        prep_kernel, route + route, vm(expert_ids, ids_sent), flops=1e7
    )
    buf, qkv_0, pos_all = call(
        functools.partial(attend_kernel, 0), [o_shape, qkv_saved, sds((SEQ, 1), f32)], pin(qkv_0), flops=4e8
    )
    o_in, (s0, st0, m0, s1, st1, m1, router) = with_(
        all_to_all(buf, CTX), (s0, st0, m0, s1, st1, m1, router)
    )
    q_sent, kv_sent = swap(tied(query_weight, o_in)), swap(tied(key_value_matrix, o_in))
    cos_all, sin_all = call(table_kernel, [sds((SEQ, 128), f32)] * 2, vm(pos_all))

    def middle(layer, o_in, x, s_l, m_l, *h1):
        return call(
            functools.partial(mid_kernel, layer),
            [row_full, row_low, gates_shape, sds((T, 2 * D), bf16), rows_shape],
            pin(o_in) + vm(x) + [(ANY, wo_all)] + vm(g2, router, s_l, m_l, *h1), [w_dd, sems(1)], flops=2e8,
        )

    row_block = sds((ROWS_OF, D), bf16)
    narrow = sds((ROWS_OF, D + 3 * F), bf16)

    def experts_forward(layer, rows):
        return call(
            functools.partial(expert_forward_kernel, layer),
            [rows_shape, sds((2, ROWS_OF, 2 * F), f32), row_block, row_block],
            pin(rows) + ex_w, ex_scratch, flops=2e9,
        )

    def experts_back(layer, rows, gu):
        return call(
            functools.partial(expert_back_kernel, layer), [rows_shape, narrow, narrow],
            pin(rows) + [(ANY, gu)] + ex_w,
            [ex_scratch[0], pltpu.VMEM((2, ROWS_OF, 2 * F), f32), sems(4)], flops=2e9,
        )

    def expert_grad(x_keep, x_got, keep, send):
        return call(
            expert_grad_kernel, [sds((D, 3 * F), bf16)], vm(x_keep) + pin(x_got) + vm(keep) + pin(swap(send)), flops=2e9
        )[0]

    mid_0, h2_0, gates_0, pair_0, buf = middle(0, o_in, tokens, s0, m0, h1_a, h1_b)
    x_rows, (cos_all, sin_all, q_sent, kv_sent) = with_(
        all_to_all(buf, GROUP), (cos_all, sin_all, q_sent, kv_sent)
    )
    qkv_w = [(ANY, v) for v in (query_weight, q_sent, key_value_matrix, kv_sent)]
    buf, gu_0, x_keep_0, x_send = experts_forward(0, x_rows)
    row_0 = gather(pair_0, "x")
    buf, (row_0,) = with_(buf, (row_0,))
    all_0 = gather(row_0, "y")
    y_0 = all_to_all(buf, GROUP)
    x_got_0 = swap(x_send)

    out_0, h1_1, y_0, buf = call(
        next_kernel, [row_low, row_low, rows_saved, qkv_shape],
        pin(y_0) + vm(mid_0, gates_0, st0, cos, sin, g1) + qkv_w,
        [w_dd, w_dd, sems(2)], flops=5e8,
    )
    qkv_1 = all_to_all(buf, CTX)
    buf, qkv_1 = call(
        functools.partial(attend_kernel, 1), [o_shape, qkv_saved], pin(qkv_1) + vm(pos_all), flops=4e8
    )
    mid_1, h2_1, gates_1, pair_1, buf = middle(1, all_to_all(buf, CTX), out_0, s1, m1, h1_1)

    (dy_buf,) = call(send_back_kernel, [rows_shape], vm(gates_1, s1, cotangent), flops=2e8)
    row_1 = gather(tied(pair_1, all_0), "x")
    x_rows, (dy_buf,) = with_(all_to_all(buf, GROUP), (dy_buf,))
    dy_rows = all_to_all(dy_buf, GROUP)
    buf, gu_1, x_keep, x_send = experts_forward(1, x_rows)
    dy_rows, (buf, gu_1) = with_(dy_rows, (buf, gu_1))
    buf, (row_1,) = with_(buf, (row_1,))
    all_1 = gather(row_1, "y")
    y_1 = all_to_all(buf, GROUP)
    x_got = swap(x_send)
    buf, keep, send = experts_back(1, dy_rows, gu_1)
    y_1, (buf,) = with_(y_1, (buf,))
    dx_1 = all_to_all(buf, GROUP)
    out_keep, out_send, dlog_1, dh2 = call(
        functools.partial(route_back_kernel, 1), [row_low, row_low, log_shape, row_full],
        pin(y_1) + vm(gates_1, st1, router, cotangent, mid_1, out_0), flops=5e8,
    )
    part = expert_grad(x_keep, x_got, keep, send)
    dx_1, (part, dh2) = with_(dx_1, (part, dh2))

    def sum_y(part):
        return lax.psum_scatter(part, "y", scatter_dimension=0, tiled=True)

    def turn(layer, dx, st, dh2, mid, g):
        return call(
            functools.partial(turn_kernel, layer), [row_full, row_low, qkv_half],
            pin(dx) + vm(st, dh2, mid, g2, g) + [(ANY, wo_all)], [w_dd, sems(1)], flops=5e8,
        )

    def attend_back(qkv, do):
        return call(
            attend_back_kernel, [back_shape, back_saved, o_saved], vm(qkv) + pin(do) + vm(pos_all), kv_scratch, flops=1e9
        )

    def heads(layer, back, da, pairs, h2, dlog, dhn2, *other):
        return call(
            functools.partial(head_grad_kernel, layer),
            [sds((D, WIDE), bf16) if layer else pinned((D, 2 * WIDE), bf16)],
            vm(back, da, cos_all, sin_all, pairs, h2, dlog, dhn2, *other), flops=8e8,
        )[0]

    def expert_rows(rows):
        return call(expert_rows_kernel, [sds((T, 3 * F), bf16)] * 4, vm(rows))

    def placed(keep, send):
        return call(place_kernel, [sds((1, 2, 1, T, D), keep.dtype)], vm(keep) + pin(swap(send)))[0]

    dmid_1, dhn2_1, buf = turn(1, dx_1, st1, dh2, mid_1, cotangent)
    do_in, (part, all_1) = with_(all_to_all(buf, CTX), (part, all_1))
    ex_1 = sum_y(part)
    buf, back_1, da_1 = attend_back(qkv_1, do_in)
    dqkv = all_to_all(buf, CTX)
    head_part_1 = heads(1, back_1, da_1, all_1, h2_1, dlog_1, dhn2_1)
    layer_out = placed(out_keep, out_send)
    grad_1, g_0, buf = call(
        functools.partial(back_kernel, 1), [row_full, row_low, rows_shape],
        pin(dqkv) + vm(out_0, dmid_1, cos, sin, g1) + qkv_w + vm(s0, gates_0),
        dqkv_scratch, flops=4e8,
    )

    dy_rows, (layer_out, head_part_1) = with_(all_to_all(buf, GROUP), (layer_out, head_part_1))
    buf, keep, send = experts_back(0, dy_rows, gu_0)
    dx_0 = all_to_all(buf, GROUP)
    dlog_0, dh2 = call(
        functools.partial(route_back_kernel, 0), [log_shape, row_full],
        vm(y_0, gates_0, st0, router, g_0), flops=3e8,
    )
    part = expert_grad(x_keep_0, x_got_0, keep, send)
    dx_0, (part, dh2, ex_1) = with_(dx_0, (part, dh2, ex_1))
    ex_0 = sum_y(part)
    ex_1_sent = round_trip(expert_rows(ex_1), "x")
    dmid_0, dhn2_0, buf = turn(0, dx_0, st0, dh2, mid_0, g_0)
    do_in = all_to_all(buf, CTX)
    buf, back_0, da_0 = attend_back(qkv_0, do_in)
    buf, ex_1 = with_(buf, ex_1_sent)
    dqkv = all_to_all(buf, CTX)
    rows_0 = expert_rows(ex_0)
    head_part = heads(0, back_0, da_0, all_0, h2_0, dlog_0, dhn2_0, head_part_1)
    full = all_to_all(head_part.reshape(64, 16, 2 * WIDE), ALL)
    grad_keep, grad_send = call(
        functools.partial(back_kernel, 0), [row_full, row_full],
        pin(tied(dqkv, *rows_0)) + vm(tokens, dmid_0, cos, sin, g1) + qkv_w + vm(grad_1), dqkv_scratch, flops=3e8,
    )

    ex_0 = round_trip(rows_0, "x")
    input_grad = placed(grad_keep, grad_send)
    sums = sds((16, 3 * D + 128), f32)
    keep, send = call(halves_kernel, [sums, sums], pin(full))
    (*ex_0, input_grad, keep, send) = lax.optimization_barrier((*ex_0, input_grad, keep, send))
    four = sds((4, T, 3 * F), bf16)
    ex_keep, ex_send = call(expert_sort_kernel, [four, four], vm(ex_0[0]) + pin(*ex_0[1:]) + vm(*ex_1))
    ex_in, ex_out = call(
        expert_final_kernel, [sds((1, 8, T, 2 * F), f32), sds((1, 8, T, F), f32)],
        vm(ex_keep) + pin(swap(ex_send)),
    )
    mat = sds((1, 16, D), f32)
    row = sds((1, 16), f32)
    grad_q, grad_kv, grad_o, router_grad, first_grad, second_grad = call(
        final_kernel, [mat, mat, mat, sds((1, 16, E), f32), row, row],
        vm(keep) + pin(swap(send)) + [(ANY, query_weight), (ANY, key_value_matrix)] + vm(first_gain),
        [pltpu.VMEM((16, D), bf16), pltpu.VMEM((16, D), bf16), sems(2)],
    )
    return (
        layer_out, input_grad, first_grad, grad_q, grad_kv, grad_o, second_grad, router_grad, ex_in, ex_out,
    )


def solution(mesh):
    grid = Mesh(mesh.devices.reshape(2, 4, 4, 4), ("section", "y", "x", "expert"))
    ctx = ("y", "x")
    every = ("y", "x", "expert")
    placed = (
        P(None, "expert", ctx, None),
        P(None, "expert", ctx),
        P("section", None, "expert", ctx, None),
        P(None, "expert", ctx, None),
        P("section", None),
        P("section", None, None),
        P("section", None, None),
        P("section", None, None),
        P("section", None),
        P("section", None, None),
        P("section", "expert", None, None),
        P("section", "expert", None, None),
    )
    return jax.shard_map(
        local,
        mesh=grid,
        in_specs=placed,
        out_specs=(
            P("section", None, "expert", ctx, None),
            P("section", None, "expert", ctx, None),
            P("section", every),
            P("section", every, None),
            P("section", every, None),
            P("section", every, None),
            P("section", every),
            P("section", every, None),
            P("section", "expert", ctx, None),
            P("section", "expert", ctx, None),
        ),
        check_vma=False,
    )
```

```python
import functools
import math

import jax
import jax.numpy as jnp
from jax import lax
from jax.experimental import pallas as pl
from jax.experimental.pallas import tpu as pltpu
from jax.sharding import Mesh
from jax.sharding import PartitionSpec as P

T = 64
D = 1024
HW = 64
WIDE = 5 * HW
NQ = 16
NK = 8
F = 512
E = 32
CAP = 17
MAIN = E * 16
SLOTS = E * CAP
GROUP_SIZE = 16
ROWS_OF = GROUP_SIZE * CAP
N_CTX = 16
SEQ = N_CTX * T

eps = 1e-06
rope_base = 10000.0
masked = -1e30
f32 = jnp.float32
bf16 = jnp.bfloat16

VMEM = pl.BlockSpec(memory_space=pltpu.VMEM)
SMEM = pl.BlockSpec(memory_space=pltpu.SMEM)
ANY = pl.BlockSpec(memory_space=pl.ANY)
PIN = "pinned"
GROUP = ("x", "expert")
CTX = ("y", "x")
ALL = ("y", "x", "expert")


def sds(shape, dtype):
    return jax.ShapeDtypeStruct(shape, dtype)


def pinned(shape, dtype):
    return pltpu.VMEM(shape, dtype)


class Later:
    def __init__(self, source, place, sem):
        self.place = place
        self.copy = pltpu.make_async_copy(source, place, sem)
        self.copy.start()

    def wait(self):
        if self.copy is not None:
            self.copy.wait()
            self.copy = None

    def __getitem__(self, index):
        self.wait()
        return self.place[index]


def call(body, outs, ins, scratch=(), flops=0, limit=36, out_spec=VMEM, lazy=True):
    late = [i for i, (k, _) in enumerate(ins) if k is VMEM]
    count, own = len(ins) + len(outs), len(scratch)

    def kernel(*refs):
        places, sems = refs[count + own : -1], refs[-1]
        args = list(refs[: len(ins)])
        for n, i in enumerate(late):
            args[i] = Later(args[i], places[n], sems.at[n])
        moving = [args[i] for i in late]
        if not lazy:
            for v in moving:
                v.wait()
        body(*args, *refs[len(ins) : count + own])
        for v in moving:
            v.wait()

    place = lambda k, a: a if k is SMEM else pltpu.with_memory_space_constraint(a, pltpu.VMEM if k is PIN else pltpu.HBM)
    outs = [o if isinstance(o, jax.ShapeDtypeStruct) is False else pltpu.HBM(o.shape, o.dtype) for o in outs]
    read = sum(a.size * a.dtype.itemsize for k, a in ins if k is VMEM)
    written = sum(math.prod(o.shape) * jnp.dtype(o.dtype).itemsize for o in outs)
    return pl.pallas_call(
        kernel,
        out_shape=list(outs),
        in_specs=[VMEM if k is PIN else ANY for k, _ in ins],
        out_specs=[out_spec] * len(outs),
        scratch_shapes=[
            *scratch,
            *[pltpu.VMEM(ins[i][1].shape, ins[i][1].dtype) for i in late],
            pltpu.SemaphoreType.DMA((max(1, len(late)),)),
        ],
        compiler_params=pltpu.CompilerParams(vmem_limit_bytes=limit * 1024 * 1024),
        cost_estimate=pl.CostEstimate(
            flops=int(flops), bytes_accessed=int(read + written), transcendentals=0
        ),
    )(*[place(k, a) for k, a in ins])


def dot(a, b):
    return lax.dot_general(a, b, (((1,), (0,)), ((), ())), preferred_element_type=f32)


def dot_nt(a, b):
    return lax.dot_general(a, b, (((1,), (1,)), ((), ())), preferred_element_type=f32)


def dot_tn(a, b):
    return lax.dot_general(a, b, (((0,), (0,)), ((), ())), preferred_element_type=f32)


def split(v):
    high = v.astype(bf16)
    return high, (v - high.astype(f32)).astype(bf16)


def iota(shape, dim):
    return lax.broadcasted_iota(jnp.int32, shape, dim)


def one_hot(cond):
    return jnp.where(cond, 1.0, 0.0).astype(bf16)


def expert_of(k):
    return 8 * ((k >> 1) & 3) + 2 * (k >> 3) + (k & 1)


def slot_table():
    row, col = iota((SLOTS, E), 0), iota((SLOTS, E), 1)
    return one_hot(expert_of(jnp.where(row < MAIN, row >> 4, row - MAIN)) == col)


def moved_rows(index, q, order):
    bits = q.bit_length() - 1
    if order == "block":
        return index >> (bits + 1), (index >> 1) & (q - 1), index & 1
    if order == "token":
        return (index >> 1) & 15, index >> 5, index & 1
    return index & 15, (index >> 4) & (q - 1), index >> (bits + 4)


def shuffle(q, to, order):
    n = 32 * q
    d, p, i = moved_rows(iota((n, n), 0), q, to)
    at = iota((n, n), 1)
    if order == "block":
        return one_hot(at == d * (2 * q) + p * 2 + i)
    if order == "token":
        return one_hot(at == p * 32 + d * 2 + i)
    return one_hot(at == (i * q + p) * 16 + d)


def pack(buf_ref, parts):
    n = len(parts)
    extra = []
    for k, rows in enumerate(parts):
        for c in range(8):
            piece = rows[:, c * 128 : (c + 1) * 128]
            buf_ref[:, k * 256 + c * 32 : k * 256 + (c + 1) * 32, :] = piece[:MAIN].reshape(16, 32, 128)
            extra.append(piece[MAIN:])
    moved = dot(shuffle(8 * n, "block", "token"), jnp.concatenate(extra, axis=0)).astype(bf16)
    buf_ref[:, 256 * n :, :] = moved.reshape(16, 16 * n, 128)


def unpack(buf_ref, n):
    rest = buf_ref[:, 256 * n :, :].reshape(256 * n, 128)
    moved = dot(shuffle(8 * n, "token", "block"), rest).astype(bf16)
    parts = []
    for k in range(n):
        pieces = []
        for c in range(8):
            head = buf_ref[:, k * 256 + c * 32 : k * 256 + (c + 1) * 32, :].reshape(MAIN, 128)
            at = (k * 8 + c) * E
            pieces.append(jnp.concatenate([head, moved[at : at + E]], axis=0))
        parts.append(jnp.concatenate(pieces, axis=1))
    return parts


def pack_experts(buf_ref, parts):
    n = len(parts)
    extra = []
    for i in range(2):
        for k in range(n):
            for c in range(8):
                piece = parts[k][i][:, c * 128 : (c + 1) * 128]
                at = k * 256 + c * 32 + i * 16
                buf_ref[:, at : at + 16, :] = piece[:256].reshape(16, 16, 128)
                extra.append(piece[256:])
    moved = dot(shuffle(8 * n, "block", "expert"), jnp.concatenate(extra, axis=0)).astype(bf16)
    buf_ref[:, 256 * n :, :] = moved.reshape(16, 16 * n, 128)


def unpack_experts(buf_ref, n):
    rest = buf_ref[:, 256 * n :, :].reshape(256 * n, 128)
    moved = dot(shuffle(8 * n, "expert", "block"), rest).astype(bf16)
    parts = []
    for k in range(n):
        both = []
        for i in range(2):
            pieces = []
            for c in range(8):
                at = k * 256 + c * 32 + i * 16
                head = buf_ref[:, at : at + 16, :].reshape(256, 128)
                at = (i * 8 * n + k * 8 + c) * 16
                pieces.append(jnp.concatenate([head, moved[at : at + 16]], axis=0))
            both.append(jnp.concatenate(pieces, axis=1))
        parts.append(both)
    return parts


def norm_parts(v):
    r = lax.rsqrt(jnp.mean(v * v, axis=-1, keepdims=True) + eps)
    return r, v * r


def norm_back(v, gain, dh):
    r, n = norm_parts(v)
    a = gain * dh
    return r * (a - n * jnp.mean(n * a, axis=-1, keepdims=True)), dh * n


def rotate(chunk, cos, sin):
    lane = iota(chunk.shape, 1) & 63
    other = jnp.where(lane < 32, pltpu.roll(chunk, 96, 1), pltpu.roll(chunk, 32, 1))
    return chunk * cos + other * sin


class Copy:
    def __init__(self, ref, place, sem):
        self.copy = pltpu.make_async_copy(ref, place, sem)
        self.copy.start()

    def wait(self):
        self.copy.wait()


def at_axis(axis):
    return lax.axis_index(axis)


class Chosen(Copy):
    def __init__(self, layer, own, sent, place, sem):
        self.copy = pltpu.make_async_copy(own, place, sem)
        mine = at_axis("section") == layer

        @pl.when(mine)
        def _():
            self.copy.start()

        @pl.when(jnp.logical_not(mine))
        def _():
            pltpu.make_async_copy(sent, place, sem).start()


def either(layer, own, sent):
    return jnp.where(at_axis("section") == layer, own, sent)


def prep_kernel(ids_own, ids_sent, r_own, r_sent, s0, st0, m0, s1, st1, m1, router):
    for layer in range(2):
        router[layer] = either(layer, r_own[0], r_sent[0])
    rep = slot_table()
    own = ids_own[0, at_axis("section"), 0]
    sent = ids_sent[...]
    for layer, (s_ref, st_ref, m_ref) in enumerate(((s0, st0, m0), (s1, st1, m1))):
        ids = either(layer, own, sent)
        col = iota((T, E), 1)
        member = jnp.zeros((T, E), f32)
        for k in range(8):
            member = member + jnp.where(ids[:, k : k + 1] == col, 1.0, 0.0)
        m_ref[...] = member
        low = member.astype(bf16)
        row64, col64 = iota((T, T), 0), iota((T, T), 1)
        rank = dot(one_hot(col64 < row64), low)
        rank = jnp.where(member > 0.5, rank, -1.0).astype(bf16)
        at = dot_nt(rank, rep)
        slot = iota((T, SLOTS), 1)
        place = jnp.where(slot < MAIN, slot & 15, 16).astype(f32)
        st_ref[...] = one_hot(at == place)
        eye = one_hot(iota((E, E), 0) == iota((E, E), 1))
        member_t = dot_nt(eye, low)
        rank_t = dot(member_t.astype(bf16), one_hot(row64 < col64))
        rank_t = jnp.where(member_t > 0.5, rank_t, -1.0).astype(bf16)
        at_t = dot(rep, rank_t)
        slot_t = iota((SLOTS, T), 0)
        place_t = jnp.where(slot_t < MAIN, slot_t & 15, 16).astype(f32)
        s_ref[...] = one_hot(at_t == place_t)


def pair_kernel(in_own, out_own, experts, at, sems):
    moves = []

    def move(source, place, target):
        n = len(moves)
        first = pltpu.make_async_copy(source, place, sems.at[2 * n])
        moves.append((first, pltpu.make_async_copy(place, target, sems.at[2 * n + 1])))
        first.start()

    for i in range(2):
        e = 2 * at_axis("x") + i
        move(in_own.at[0, e], at.at[i, :, : 2 * F], experts.at[0, i, :, : 2 * F])
        move(out_own.at[0, e], at.at[i, :, 2 * F :], experts.at[0, i, :, 2 * F :])
    for first, second in moves:
        first.wait()
        second.start()
    for _, second in moves:
        second.wait()


def qkv_pack(q, kv, cos, sin, pos, buf_ref):
    hi = jnp.floor(pos * (1.0 / 32.0))
    lo = pos - hi * 32.0
    lane = iota((T, 64), 1)
    where_am_i = jnp.where(lane == 0, hi, jnp.where(lane == 1, lo, 0.0)).astype(bf16)
    for pair in range(4):
        k_two = rotate(kv[:, pair * 128 : (pair + 1) * 128], cos, sin).astype(bf16)
        v_two = kv[:, 512 + pair * 128 : 512 + (pair + 1) * 128].astype(bf16)
        for g in range(2):
            k_one = k_two[:, g * 64 : (g + 1) * 64]
            v_one = v_two[:, g * 64 : (g + 1) * 64]
            group = pair * 2 + g
            q_two = rotate(q[:, group * 128 : (group + 1) * 128], cos, sin).astype(bf16)
            low_half = jnp.concatenate([v_one, where_am_i], axis=1)
            for j in range(2):
                top = jnp.concatenate([q_two[:, j * 64 : (j + 1) * 64], k_one], axis=1)
                buf_ref[2 * group + j, 0:T, :] = top
                buf_ref[2 * group + j, T : 2 * T, :] = low_half


def rotary(pos):
    rows = pos.shape[0]
    lane = iota((rows, 128), 1)
    frequency = jnp.exp((lane & 31).astype(f32) * (-2.0 * math.log(rope_base) / HW))
    angles = pos * frequency
    sin = jnp.sin(angles)
    return jnp.cos(angles), jnp.where((lane & 63) < 32, -sin, sin)


def table_kernel(pos, cos, sin):
    for start in range(0, SEQ, 256):
        at = slice(start, start + 256)
        cos[at], sin[at] = rotary(pos[at])


def first_kernel(tok, places, gain, q_own, kv_own, h1_a, h1_b, buf_a, buf_b, cos_ref, sin_ref, q_w, kv_w, sems):
    q_copy = pltpu.make_async_copy(q_own.at[0], q_w, sems.at[0])
    kv_copy = pltpu.make_async_copy(kv_own.at[0], kv_w, sems.at[1])
    q_copy.start()
    kv_copy.start()
    x = jnp.concatenate([tok[0, 0], tok[1, 0]], axis=0).astype(f32)
    h1 = (norm_parts(x)[1] * gain[...]).astype(bf16)
    h1_a[...] = h1[:T]
    h1_b[...] = h1[T:]
    eye = iota((T, T), 0) == iota((T, T), 1)
    columns = [
        jnp.sum(jnp.where(eye, places[m].astype(f32), 0.0), axis=1, keepdims=True) for m in range(2)
    ]
    pos = jnp.concatenate(columns, axis=0)
    cos, sin = rotary(pos)
    cos_ref[...] = cos
    sin_ref[...] = sin
    q_copy.wait()
    q = dot(h1, q_w[...])
    kv_copy.wait()
    kv = dot(h1, kv_w[...])
    for m, buf_ref in enumerate((buf_a, buf_b)):
        at = slice(m * T, (m + 1) * T)
        qkv_pack(q[at], kv[at], cos[at], sin[at], pos[at], buf_ref)


def attention_parts(buf):
    q = buf[:, 0:T, 0:HW].reshape(SEQ, HW)
    k = buf[:, 0:T, HW : 2 * HW].reshape(SEQ, HW)
    v = buf[:, T : 2 * T, 0:HW].reshape(SEQ, HW)
    return q, k, v


def sent_positions(buf):
    hi = buf[:, T : 2 * T, HW : HW + 1].reshape(SEQ, 1).astype(f32)
    lo = buf[:, T : 2 * T, HW + 1 : HW + 2].reshape(SEQ, 1).astype(f32)
    return hi * 32.0 + lo


def block_probs(q, k, pos, start, rows):
    keys = start + rows
    scores = dot_nt(q[start : start + rows], k[:keys]) * (HW**-0.5)
    at = (iota((rows, keys), 0) + start).astype(f32)
    key = iota((rows, keys), 1).astype(f32)
    begin = at[:, 0:1] - pos[start : start + rows]
    scores = jnp.where((key <= at) & (key >= begin), scores, masked)
    raised = jnp.exp(scores - jnp.max(scores, axis=-1, keepdims=True))
    return raised / jnp.sum(raised, axis=-1, keepdims=True)


ROWS = 256


def attend_kernel(layer, buf_ref, *refs):
    q, k, v = attention_parts(buf_ref[...])
    if layer == 0:
        out_ref, kept, pos_ref = refs
        pos = sent_positions(buf_ref[...])
        pos_ref[...] = pos
    else:
        pos_ref, out_ref, kept = refs
        pos = pos_ref[...]
    kept[...] = buf_ref[...]
    for start in range(0, SEQ, ROWS):
        probs = block_probs(q, k, pos, start, ROWS)
        o = dot(probs.astype(bf16), v[: start + ROWS]).astype(bf16)
        for b in range(ROWS // T):
            piece = o[b * T : (b + 1) * T]
            out_ref[start // T + b] = jnp.concatenate([piece[: T // 2], piece[T // 2 :]], axis=1)


def heads_in(buf_ref, o_ref):
    for g in range(8):
        a, b = buf_ref[2 * g], buf_ref[2 * g + 1]
        o_ref[0 : T // 2, g * 128 : (g + 1) * 128] = jnp.concatenate([a[:, :64], b[:, :64]], axis=1)
        o_ref[T // 2 : T, g * 128 : (g + 1) * 128] = jnp.concatenate([a[:, 64:], b[:, 64:]], axis=1)


def heads_out(do, buf_ref, start):
    for g in range(8):
        two = do[:, g * 128 : (g + 1) * 128]
        for j in range(2):
            one = two[:, j * 64 : (j + 1) * 64]
            block = jnp.concatenate([one[: T // 2], one[T // 2 :]], axis=1)
            buf_ref[2 * g + j, start : start + T // 2, :] = block


def gates_from(logits, member):
    chosen = member > 0.5
    largest = jnp.max(jnp.where(chosen, logits, masked), axis=-1, keepdims=True)
    raised = jnp.where(chosen, jnp.exp(jnp.minimum(logits - largest, 0.0)), 0.0)
    return raised / jnp.sum(raised, axis=-1, keepdims=True)


def gated_rows(gates, s, rep, g_low):
    high, low = split(gates)
    up = (s * dot_nt(rep, high).astype(bf16)).astype(bf16)
    down = (s * dot_nt(rep, low).astype(bf16)).astype(bf16)
    return (dot(up, g_low) + dot(down, g_low)).astype(bf16)


def mid_kernel(layer, *refs):
    ob, x_ref, wo_all, gain, r_ref, s_ref, m_ref = refs[:7]
    h1_refs, (mid_ref, h2_ref, gates_ref, pair_ref, buf_ref, wo, sems) = refs[7:-7], refs[-7:]
    copy = Copy(wo_all.at[layer], wo, sems.at[0])
    o_ref = pair_ref.at[:, D:]
    heads_in(ob, o_ref)
    if layer == 0:
        pair_ref[:, :D] = jnp.where(at_axis("section") == 0, h1_refs[0][...], h1_refs[1][...])
    else:
        pair_ref[:, :D] = h1_refs[0][...]
    x = (tok_row(x_ref) if layer == 0 else x_ref[...]).astype(f32)
    copy.wait()
    middle = x + dot(o_ref[...], wo[...])
    mid_ref[...] = middle
    h2 = (norm_parts(middle)[1] * gain[layer]).astype(bf16)
    h2_ref[...] = h2
    pack(buf_ref, [dot(s_ref[...], h2).astype(bf16)])
    gates_ref[...] = gates_from(dot(h2, r_ref[layer]), m_ref[...])


def send_back_kernel(gates, s_ref, cot, buf_ref):
    pack(buf_ref, [gated_rows(gates[...], s_ref[...], slot_table(), tok_row(cot))])


def tok_row(ref):
    return ref[at_axis("section"), 0]


def hidden_of(gu):
    gate, up = gu[:, :F], gu[:, F:]
    sg = jax.nn.sigmoid(gate)
    return gate, up, sg, (gate * sg * up).astype(bf16)


def sorted_out(i, keep, send, at, value):
    cols = slice(at, at + value.shape[1])

    @pl.when(at_axis("section") == i)
    def _():
        keep[:, cols] = value

    @pl.when(at_axis("section") != i)
    def _():
        send[:, cols] = value


def expert_forward_kernel(layer, buf, w_all, ybuf, gu_ref, keep, send, w, sems):
    copies = [Copy(w_all.at[layer, i], w.at[i], sems.at[i]) for i in range(2)]
    (x,) = unpack_experts(buf, 1)
    y = []
    for i in range(2):
        copies[i].wait()
        gu = dot(x[i], w[i, :, : 2 * F])
        gu_ref[i] = gu
        y.append(dot_nt(hidden_of(gu)[3], w[i, :, 2 * F :]).astype(bf16))
        sorted_out(i, keep, send, 0, x[i])
    pack_experts(ybuf, [y])


def expert_back(dy, gu, w_in, w_out):
    gate, up, sg, z = hidden_of(gu)
    dz = dot(dy, w_out)
    dgate = dz * up * (sg + gate * sg * (1.0 - sg))
    dup = dz * gate * sg
    dgu = jnp.concatenate([dgate, dup], axis=1).astype(bf16)
    return z, dgu, dot_nt(dgu, w_in).astype(bf16)


def expert_back_kernel(layer, buf, gu_all, w_all, back, keep, send, w, gu, sems):
    copies = []
    for i in range(2):
        copies.append(Copy(w_all.at[layer, i], w.at[i], sems.at[i]))
        copies.append(Copy(gu_all.at[i], gu.at[i], sems.at[2 + i]))
    (dy,) = unpack_experts(buf, 1)
    dx = []
    for i in range(2):
        copies[2 * i].wait()
        copies[2 * i + 1].wait()
        z, dgu, dx_i = expert_back(dy[i], gu[i], w[i, :, : 2 * F], w[i, :, 2 * F :])
        dx.append(dx_i)
        for at, value in ((0, dy[i]), (D, dgu), (D + 2 * F, z)):
            sorted_out(i, keep, send, at, value)
    pack_experts(back, [dx])


def expert_grad_kernel(x_keep, x_got, keep, got, out):
    x = jnp.concatenate([x_keep[...], x_got[...]], axis=0)
    dy = jnp.concatenate([keep[:, :D], got[:, :D]], axis=0)
    dgu = jnp.concatenate([keep[:, D : D + 2 * F], got[:, D : D + 2 * F]], axis=0)
    z = jnp.concatenate([keep[:, D + 2 * F : D + 3 * F], got[:, D + 2 * F : D + 3 * F]], axis=0)
    out[:, : 2 * F] = dot_tn(x, dgu).astype(bf16)
    out[:, 2 * F :] = dot_tn(dy, z).astype(bf16)


def expert_rows_kernel(rows, b0, b1, b2, b3):
    for k, b in enumerate((b0, b1, b2, b3)):
        at = pl.multiple_of(((at_axis("x") + k) & 3) * T, T)
        b[...] = rows[pl.ds(at, T), :]


def expert_sort_kernel(*refs):
    keep, send = refs[8:]
    for layer in range(2):
        for k in range(4):
            block = refs[4 * layer + k]
            place = (at_axis("x") - k) & 3

            @pl.when(at_axis("section") == layer)
            def _():
                keep[place] = block[...]

            @pl.when(at_axis("section") != layer)
            def _():
                send[place] = block[...]


def expert_final_kernel(keep, got, out_in, out_out):
    for x in range(4):
        for ref, j in ((keep, at_axis("section")), (got, 1 - at_axis("section"))):
            out_in[0, 2 * x + j] = ref[x, :, : 2 * F].astype(f32)
            out_out[0, 2 * x + j] = ref[x, :, 2 * F :].astype(f32)


def place_kernel(keep, got, out):
    out[0, at_axis("section"), 0] = keep[...]
    out[0, 1 - at_axis("section"), 0] = got[...]


def by_section(v_0, v_1, keep, send):
    keep[...] = jnp.where(at_axis("section") == 0, v_0, v_1)
    send[...] = jnp.where(at_axis("section") == 0, v_1, v_0)


def combine(middle, gates, st, rep, y):
    high, low = split(gates)
    up = (st * dot_nt(high, rep).astype(bf16)).astype(bf16)
    down = (st * dot_nt(low, rep).astype(bf16)).astype(bf16)
    return middle + (dot(up, y) + dot(down, y))


def micro_rows(ref):
    return ref[pl.ds(pl.multiple_of(at_axis("section") * T, T), T), :]


def next_kernel(
    yb, mid, gates, st, cos, sin, gain, q_own, q_sent, kv_own, kv_sent, out_ref, h1_ref, saved, buf_ref, q_w, kv_w, sems,
):
    saved[...] = yb[...]
    q_copy = Chosen(1, q_own.at[0], q_sent.at[0], q_w, sems.at[0])
    kv_copy = Chosen(1, kv_own.at[0], kv_sent.at[0], kv_w, sems.at[1])
    (y,) = unpack(yb, 1)
    out = combine(mid[...], gates[...], st[...], slot_table(), y).astype(bf16)
    out_ref[...] = out
    h1 = (norm_parts(out.astype(f32))[1] * gain[1]).astype(bf16)
    h1_ref[...] = h1
    q_copy.wait()
    q = dot(h1, q_w[...])
    kv_copy.wait()
    kv = dot(h1, kv_w[...])
    qkv_pack(q, kv, micro_rows(cos), micro_rows(sin), jnp.zeros((T, 1), f32), buf_ref)


def route_back_kernel(layer, *refs):
    yb, gates_ref, st_ref, r_ref, g_ref = refs[:5]
    dlog_ref, dh2_ref = refs[-2:]
    rep, st, gates = slot_table(), st_ref[...], gates_ref[...]
    (y,) = unpack(yb, 1)
    if layer == 1:
        mid, out_0, keep, send = refs[5:9]
        g_low = tok_row(g_ref)
        by_section(out_0[...], combine(mid[...], gates, st, rep, y).astype(bf16), keep, send)
    else:
        g_low = g_ref[...]
    d_slot = dot_nt(g_low, y) * st.astype(f32)
    high, low = split(d_slot)
    d_gates = dot(high, rep) + dot(low, rep)
    d_chosen = gates * (d_gates - jnp.sum(gates * d_gates, axis=-1, keepdims=True))
    d_log = d_chosen.astype(bf16)
    dlog_ref[...] = d_log
    dh2_ref[...] = dot_nt(d_log, r_ref[layer])


def turn_kernel(layer, *refs):
    dxb, st, dh2, mid, gain, g_ref, wo_all, dmid_ref, dhn_ref, dobuf, wo, sems = refs
    copy = Copy(wo_all.at[layer], wo, sems.at[0])
    (dx,) = unpack(dxb, 1)
    g_low = tok_row(g_ref) if layer == 1 else g_ref[...]
    d_h2 = dot(st[...], dx) + dh2[...]
    d_v, d_hn = norm_back(mid[...], gain[layer], d_h2)
    d_mid = g_low.astype(f32) + d_v
    d_a = d_mid.astype(bf16)
    heads_out(d_a, dobuf, T // 2)
    copy.wait()
    heads_out(dot_nt(d_a, wo[...]).astype(bf16), dobuf, 0)
    dmid_ref[...] = d_mid
    dhn_ref[...] = d_hn.astype(bf16)


def attend_back_kernel(buf_ref, dobuf, pos_ref, out_ref, saved, da_saved, dk_ref, dv_ref):
    q, k, v = attention_parts(buf_ref[...])
    pos = pos_ref[...]
    da_saved[...] = dobuf[:, T // 2 :, :]
    packed = dobuf[:, : T // 2, :]
    do = halves(packed)
    scale = HW**-0.5
    dq = []
    for start in reversed(range(0, SEQ, ROWS)):
        keys = start + ROWS
        probs = block_probs(q, k, pos, start, ROWS)
        do_rows = do[start:keys]
        d_probs = dot_nt(do_rows, v[:keys])
        inner = jnp.sum(probs * d_probs, axis=-1, keepdims=True)
        d_scores = (probs * (d_probs - inner)).astype(bf16)
        dq.append((dot(d_scores, k[:keys]) * scale).astype(bf16))
        d_k = dot_tn(d_scores, q[start:keys]) * scale
        d_v = dot_tn(probs.astype(bf16), do_rows)
        if keys == SEQ:
            dk_ref[...] = d_k
            dv_ref[...] = d_v
        else:
            dk_ref[0:keys] = dk_ref[0:keys] + d_k
            dv_ref[0:keys] = dv_ref[0:keys] + d_v
    d_q = jnp.concatenate(dq[::-1], axis=0)
    d_k = dk_ref[...].astype(bf16)
    d_v = dv_ref[...].astype(bf16)
    out_ref[:, 0:T, :] = jnp.concatenate([d_q, d_k], axis=1).reshape(N_CTX, T, 128)
    d_v = d_v.reshape(N_CTX, T, HW)
    out_ref[:, T:, :] = jnp.concatenate([d_v[:, : T // 2], d_v[:, T // 2 :]], axis=2)
    saved[...] = out_ref[...]


def back_kernel(layer, *refs):
    refs = list(refs)
    buf, x_ref, dmid, cos_ref, sin_ref, gain, q_own, q_sent, kv_own, kv_sent = refs[:10]
    refs = refs[10:]
    if layer == 1:
        s_ref, gates_ref = refs[:2]
        refs = refs[2:]
    if layer == 0:
        grad_1 = refs.pop(0)
        keep, send = refs[:2]
        refs = refs[2:]
    else:
        grad_ref = refs.pop(0)
    if layer == 1:
        g_ref, dybuf = refs[:2]
        refs = refs[2:]
    q_w, kv_w, dq_ref, dkv_ref, sems = refs
    q_copy = Chosen(layer, q_own.at[0], q_sent.at[0], q_w, sems.at[0])
    kv_copy = Chosen(layer, kv_own.at[0], kv_sent.at[0], kv_w, sems.at[1])
    cos, sin = micro_rows(cos_ref), -micro_rows(sin_ref)
    half = T // 2
    k_parts, v_parts = [], []
    for g in range(8):
        a, b = buf[2 * g], buf[2 * g + 1]
        q_two = jnp.concatenate([a[:T, :64], b[:T, :64]], axis=1).astype(f32)
        dq_ref[:, g * 128 : (g + 1) * 128] = rotate(q_two, cos, sin).astype(bf16)
        k_parts.append(a[:T, 64:].astype(f32) + b[:T, 64:].astype(f32))
        v_sum = a[T:].astype(f32) + b[T:].astype(f32)
        v_parts.append(jnp.concatenate([v_sum[:, :64], v_sum[:, 64:]], axis=0))
    for p in range(4):
        k_two = jnp.concatenate([k_parts[2 * p], k_parts[2 * p + 1]], axis=1)
        v_two = jnp.concatenate([v_parts[2 * p], v_parts[2 * p + 1]], axis=1)
        dkv_ref[:, p * 128 : (p + 1) * 128] = rotate(k_two, cos, sin).astype(bf16)
        dkv_ref[:, 512 + p * 128 : 512 + (p + 1) * 128] = v_two.astype(bf16)
    q_copy.wait()
    kv_copy.wait()
    d_h1 = dot_nt(dq_ref[...], q_w[...]) + dot_nt(dkv_ref[...], kv_w[...])
    x = (tok_row(x_ref) if layer == 0 else x_ref[...]).astype(f32)
    d_x, _ = norm_back(x, gain[layer], d_h1)
    grad = dmid[...] + d_x
    if layer == 0:
        by_section(grad, grad_1[...], keep, send)
    else:
        grad_ref[...] = grad
        g_low = grad.astype(bf16)
        g_ref[...] = g_low
        pack(dybuf, [gated_rows(gates_ref[...], s_ref[...], slot_table(), g_low)])


def head_grad_kernel(layer, back, da, cos_ref, sin_ref, pairs, h2, dlog, dhn2, *refs):
    out = refs[-1]
    if layer == 0:
        out[:, WIDE:] = refs[0][...]
    cos, sin = cos_ref[...], -sin_ref[...]
    both = rotate(back[:, :T, :].reshape(SEQ, 2 * HW).astype(f32), cos, sin).astype(bf16)
    lane = iota((T, HW), 1)
    logs = jnp.concatenate([dlog[...], jnp.zeros((T, HW - E), bf16)], axis=1)
    extra = dot_tn(logs, h2[...]) + dot_tn(one_hot(lane == E), dhn2[...])
    h1_all = pairs[:, :D]
    out[:, : 2 * HW] = dot_tn(both, h1_all).T.astype(bf16)
    rest = [dot_tn(halves(back[:, T:, :]), h1_all), dot_tn(halves(da[...]), pairs[:, D:]), extra]
    out[:, 2 * HW : WIDE] = jnp.concatenate(rest, axis=0).T.astype(bf16)


def halves(packed):
    return jnp.concatenate([packed[:, :, :HW], packed[:, :, HW:]], axis=1).reshape(SEQ, HW)


def head_sums(got, layer):
    v = []
    cols = slice(WIDE * layer, WIDE * (layer + 1))
    for c in range(N_CTX):
        v.append(sum(got[4 * c + k, :, cols].astype(f32) for k in range(1, 4)) + got[4 * c, :, cols].astype(f32))
    pair = [v[2 * g] + v[2 * g + 1] for g in range(NK)]
    parts = []
    for blocks, at in ((v, 3 * HW), (v, 0), (pair, HW), (pair, 2 * HW)):
        for a, b in zip(blocks[::2], blocks[1::2]):
            parts.append(jnp.concatenate([a[:, at : at + HW], b[:, at : at + HW]], axis=1))
    total = sum(pair[1:]) + pair[0]
    parts.append(total[:, 3 * HW :])
    return jnp.concatenate(parts, axis=1)


def halves_kernel(got, keep, send):
    by_section(head_sums(got, 0), head_sums(got, 1), keep, send)


def final_kernel(keep, got, q_own, kv_own, gain, gq, gkv, go, gr, g1, g2, q_rows, kv_rows, sems):
    first = 16 * at_axis(ALL)
    rows = pl.ds(pl.multiple_of(first, 16), 16)
    copies = [Copy(q_own.at[0, rows], q_rows, sems.at[0]), Copy(kv_own.at[0, rows], kv_rows, sems.at[1])]
    mine = keep[...] + got[...]
    grad_q, grad_kv, rest = mine[:, D : 2 * D], mine[:, 2 * D : 3 * D], mine[:, 3 * D :]
    go[0] = mine[:, :D]
    gq[0] = grad_q
    gkv[0] = grad_kv
    gr[0] = rest[:, HW : HW + E]
    eye = iota((16, 16), 0) == iota((16, 16), 1)
    as_row = lambda column: jnp.sum(jnp.where(eye, column, 0.0), axis=0, keepdims=True)
    g2[...] = as_row(rest[:, HW + E : HW + E + 1])
    here = iota((16, D), 1) == iota((16, D), 0) + first
    gains = jnp.sum(jnp.where(here, gain[...], 0.0), axis=1, keepdims=True)
    for copy in copies:
        copy.wait()
    both = grad_q * q_rows[...].astype(f32) + grad_kv * kv_rows[...].astype(f32)
    g1[...] = as_row(jnp.sum(both, axis=-1, keepdims=True) / gains)


def swap(v):
    return lax.ppermute(v, "section", [(0, 1), (1, 0)])


def either_order(first, mine, other):
    return jnp.where(first, mine, other), jnp.where(first, other, mine)


def all_to_all(v, axes):
    return lax.all_to_all(v, axes, 0, 0, tiled=True)


def local(
    tokens, positions, expert_ids, cotangent, first_gain, query_weight, key_value_matrix,
    output_weight, second_gain, router_weight, expert_in, expert_out,
):
    s, y_at, x_at, z_at = (lax.axis_index(a) for a in ("section", "y", "x", "expert"))
    first = s == 0
    vm = lambda *arrays: [(VMEM, a) for a in arrays]
    pin = lambda *arrays: [(PIN, a) for a in arrays]
    sems = lambda n: pltpu.SemaphoreType.DMA((n,))
    tied = lambda v, *after: lax.optimization_barrier((v,) + after)[0]

    def with_(v, others):
        v, *others = lax.optimization_barrier((v, *others))
        return v, others

    def gather(v, axis):
        return lax.all_gather(v, axis, axis=0, tiled=True)

    def both(v):
        return lax.all_gather(v, "section", axis=0, tiled=True)

    def round_trip(blocks, axis):
        route = lambda k: [(i, (i + k) % 4) for i in range(4)]
        return [blocks[0]] + [lax.ppermute(blocks[k], axis, route(k)) for k in range(1, 4)]

    w_dd = pltpu.VMEM((D, D), bf16)
    ex_scratch = [pltpu.VMEM((2, D, 3 * F), bf16), sems(2)]
    qkv_shape = pinned((N_CTX, 2 * T, 128), bf16)
    o_shape = pinned((N_CTX, T // 2, 128), bf16)
    qkv_half = pinned((N_CTX, T, 128), bf16)
    back_shape = pinned((N_CTX, T + T // 2, 128), bf16)
    rows_shape = pinned((GROUP_SIZE, 272, 128), bf16)
    row_low, row_full = sds((T, D), bf16), sds((T, D), f32)
    gates_shape, log_shape = sds((T, E), f32), sds((T, E), bf16)
    o_saved, back_saved = sds(o_shape.shape, bf16), sds(back_shape.shape, bf16)
    qkv_saved, rows_saved = sds(qkv_shape.shape, bf16), sds(rows_shape.shape, bf16)
    kv_scratch = [pltpu.VMEM((SEQ, HW), f32), pltpu.VMEM((SEQ, HW), f32)]
    dqkv_scratch = [w_dd, w_dd, pltpu.VMEM((T, D), bf16), pltpu.VMEM((T, D), bf16), sems(2)]

    table = sds((2 * T, 128), f32)
    h1_a, h1_b, buf_a, buf_b, cos, sin = call(
        first_kernel, [row_low, row_low, qkv_shape, qkv_shape, table, table],
        vm(tokens, positions, first_gain) + [(ANY, query_weight), (ANY, key_value_matrix)],
        [w_dd, w_dd, sems(2)], flops=6e8,
    )
    down = lambda v: lax.ppermute(v, "section", [(0, 1)])
    buf = jnp.where(first, buf_a, down(buf_b))
    h1_b = down(h1_b)

    late = lambda v: tied(v, buf_a)
    wo_all = both(late(output_weight))
    g1, g2 = (jnp.stack(either_order(first, v, swap(late(v)))) for v in (first_gain, second_gain))
    r_sent = swap(late(router_weight))
    ids_sent = swap(late(lax.dynamic_slice(expert_ids, (0, 1 - s, 0, 0, 0), (1, 1, 1, T, 8)))).reshape(T, 8)
    (pair,) = call(
        pair_kernel, [sds((1, 2, D, 3 * F), bf16)], [(ANY, tied(v, buf)) for v in (expert_in, expert_out)],
        [pltpu.VMEM((2, D, 3 * F), bf16), sems(8)], out_spec=ANY,
    )
    route = [sds((SLOTS, T), bf16), sds((T, SLOTS), bf16), sds((T, E), f32)]

    qkv_0, (pair, g1, g2, r_sent, ids_sent, h1_b) = with_(
        all_to_all(buf, CTX), (pair, g1, g2, r_sent, ids_sent, h1_b)
    )
    ex_w = [(ANY, both(pair))]
    s0, st0, m0, s1, st1, m1, router = call(
        prep_kernel, route + route + [sds((2, D, E), bf16)],
        vm(expert_ids, ids_sent, router_weight, r_sent), flops=1e7,
    )
    buf, qkv_0, pos_all = call(
        functools.partial(attend_kernel, 0), [o_shape, qkv_saved, sds((SEQ, 1), f32)], pin(qkv_0), flops=4e8
    )
    o_in, (s0, st0, m0, s1, st1, m1, router) = with_(
        all_to_all(buf, CTX), (s0, st0, m0, s1, st1, m1, router)
    )
    q_sent, kv_sent = swap(tied(query_weight, o_in)), swap(tied(key_value_matrix, o_in))
    cos_all, sin_all = call(table_kernel, [sds((SEQ, 128), f32)] * 2, vm(pos_all))

    def middle(layer, o_in, x, s_l, m_l, *h1):
        return call(
            functools.partial(mid_kernel, layer),
            [row_full, row_low, gates_shape, sds((T, 2 * D), bf16), rows_shape],
            pin(o_in) + vm(x) + [(ANY, wo_all)] + vm(g2, router, s_l, m_l, *h1), [w_dd, sems(1)], flops=2e8,
        )

    row_block = sds((ROWS_OF, D), bf16)
    narrow = sds((ROWS_OF, D + 3 * F), bf16)

    def experts_forward(layer, rows):
        return call(
            functools.partial(expert_forward_kernel, layer),
            [rows_shape, sds((2, ROWS_OF, 2 * F), f32), row_block, row_block],
            pin(rows) + ex_w, ex_scratch, flops=2e9,
        )

    def experts_back(layer, rows, gu):
        return call(
            functools.partial(expert_back_kernel, layer), [rows_shape, narrow, narrow],
            pin(rows) + [(ANY, gu)] + ex_w,
            [ex_scratch[0], pltpu.VMEM((2, ROWS_OF, 2 * F), f32), sems(4)], flops=2e9,
        )

    def expert_grad(x_keep, x_got, keep, send):
        return call(
            expert_grad_kernel, [sds((D, 3 * F), bf16)], vm(x_keep) + pin(x_got) + vm(keep) + pin(swap(send)), flops=2e9
        )[0]

    mid_0, h2_0, gates_0, pair_0, buf = middle(0, o_in, tokens, s0, m0, h1_a, h1_b)
    x_rows, (cos_all, sin_all, q_sent, kv_sent) = with_(
        all_to_all(buf, GROUP), (cos_all, sin_all, q_sent, kv_sent)
    )
    qkv_w = [(ANY, v) for v in (query_weight, q_sent, key_value_matrix, kv_sent)]
    buf, gu_0, x_keep_0, x_send = experts_forward(0, x_rows)
    row_0 = gather(pair_0, "x")
    buf, (row_0,) = with_(buf, (row_0,))
    all_0 = gather(row_0, "y")
    y_0 = all_to_all(buf, GROUP)
    x_got_0 = swap(x_send)

    out_0, h1_1, y_0, buf = call(
        next_kernel, [row_low, row_low, rows_saved, qkv_shape],
        pin(y_0) + vm(mid_0, gates_0, st0, cos, sin, g1) + qkv_w,
        [w_dd, w_dd, sems(2)], flops=5e8,
    )
    qkv_1 = all_to_all(buf, CTX)
    buf, qkv_1 = call(
        functools.partial(attend_kernel, 1), [o_shape, qkv_saved], pin(qkv_1) + vm(pos_all), flops=4e8
    )
    mid_1, h2_1, gates_1, pair_1, buf = middle(1, all_to_all(buf, CTX), out_0, s1, m1, h1_1)

    (dy_buf,) = call(send_back_kernel, [rows_shape], vm(gates_1, s1, cotangent), flops=2e8)
    row_1 = gather(tied(pair_1, all_0), "x")
    x_rows, (dy_buf,) = with_(all_to_all(buf, GROUP), (dy_buf,))
    dy_rows = all_to_all(dy_buf, GROUP)
    buf, gu_1, x_keep, x_send = experts_forward(1, x_rows)
    dy_rows, (buf, gu_1) = with_(dy_rows, (buf, gu_1))
    buf, (row_1,) = with_(buf, (row_1,))
    all_1 = gather(row_1, "y")
    y_1 = all_to_all(buf, GROUP)
    x_got = swap(x_send)
    buf, keep, send = experts_back(1, dy_rows, gu_1)
    y_1, (buf,) = with_(y_1, (buf,))
    dx_1 = all_to_all(buf, GROUP)
    out_keep, out_send, dlog_1, dh2 = call(
        functools.partial(route_back_kernel, 1), [row_low, row_low, log_shape, row_full],
        pin(y_1) + vm(gates_1, st1, router, cotangent, mid_1, out_0), flops=5e8,
    )
    part = expert_grad(x_keep, x_got, keep, send)
    dx_1, (part, dh2) = with_(dx_1, (part, dh2))

    def sum_y(part):
        return lax.psum_scatter(part, "y", scatter_dimension=0, tiled=True)

    def turn(layer, dx, st, dh2, mid, g):
        return call(
            functools.partial(turn_kernel, layer), [row_full, row_low, qkv_half],
            pin(dx) + vm(st, dh2, mid, g2, g) + [(ANY, wo_all)], [w_dd, sems(1)], flops=5e8,
        )

    def attend_back(qkv, do):
        return call(
            attend_back_kernel, [back_shape, back_saved, o_saved], vm(qkv) + pin(do) + vm(pos_all), kv_scratch, flops=1e9
        )

    def heads(layer, back, da, pairs, h2, dlog, dhn2, *other):
        return call(
            functools.partial(head_grad_kernel, layer),
            [sds((D, WIDE), bf16) if layer else pinned((D, 2 * WIDE), bf16)],
            vm(back, da, cos_all, sin_all, pairs, h2, dlog, dhn2, *other), flops=8e8,
        )[0]

    def expert_rows(rows):
        return call(expert_rows_kernel, [sds((T, 3 * F), bf16)] * 4, vm(rows))

    def placed(keep, send):
        return call(place_kernel, [sds((1, 2, 1, T, D), keep.dtype)], vm(keep) + pin(swap(send)))[0]

    dmid_1, dhn2_1, buf = turn(1, dx_1, st1, dh2, mid_1, cotangent)
    do_in, (part, all_1) = with_(all_to_all(buf, CTX), (part, all_1))
    ex_1 = sum_y(part)
    buf, back_1, da_1 = attend_back(qkv_1, do_in)
    dqkv = all_to_all(buf, CTX)
    head_part_1 = heads(1, back_1, da_1, all_1, h2_1, dlog_1, dhn2_1)
    layer_out = placed(out_keep, out_send)
    grad_1, g_0, buf = call(
        functools.partial(back_kernel, 1), [row_full, row_low, rows_shape],
        pin(dqkv) + vm(out_0, dmid_1, cos, sin, g1) + qkv_w + vm(s0, gates_0),
        dqkv_scratch, flops=4e8,
    )

    dy_rows, (layer_out, head_part_1) = with_(all_to_all(buf, GROUP), (layer_out, head_part_1))
    buf, keep, send = experts_back(0, dy_rows, gu_0)
    dx_0 = all_to_all(buf, GROUP)
    dlog_0, dh2 = call(
        functools.partial(route_back_kernel, 0), [log_shape, row_full],
        vm(y_0, gates_0, st0, router, g_0), flops=3e8,
    )
    part = expert_grad(x_keep_0, x_got_0, keep, send)
    dx_0, (part, dh2, ex_1) = with_(dx_0, (part, dh2, ex_1))
    ex_0 = sum_y(part)
    ex_1_sent = round_trip(expert_rows(ex_1), "x")
    dmid_0, dhn2_0, buf = turn(0, dx_0, st0, dh2, mid_0, g_0)
    do_in = all_to_all(buf, CTX)
    buf, back_0, da_0 = attend_back(qkv_0, do_in)
    buf, ex_1 = with_(buf, ex_1_sent)
    dqkv = all_to_all(buf, CTX)
    rows_0 = expert_rows(ex_0)
    head_part = heads(0, back_0, da_0, all_0, h2_0, dlog_0, dhn2_0, head_part_1)
    full = all_to_all(head_part.reshape(64, 16, 2 * WIDE), ALL)
    grad_keep, grad_send = call(
        functools.partial(back_kernel, 0), [row_full, row_full],
        pin(tied(dqkv, *rows_0)) + vm(tokens, dmid_0, cos, sin, g1) + qkv_w + vm(grad_1), dqkv_scratch, flops=3e8,
    )

    ex_0 = round_trip(rows_0, "x")
    input_grad = placed(grad_keep, grad_send)
    sums = sds((16, 3 * D + 128), f32)
    full, (input_grad,) = with_(full, (input_grad,))
    keep, send = call(halves_kernel, [sums, sums], pin(full))
    (*ex_0, keep, send) = lax.optimization_barrier((*ex_0, keep, send))
    four = sds((4, T, 3 * F), bf16)
    ex_keep, ex_send = call(expert_sort_kernel, [four, four], vm(ex_0[0]) + pin(*ex_0[1:]) + vm(*ex_1), lazy=False)
    ex_in, ex_out = call(
        expert_final_kernel, [sds((1, 8, T, 2 * F), f32), sds((1, 8, T, F), f32)],
        vm(ex_keep) + pin(swap(ex_send)),
    )
    mat = sds((1, 16, D), f32)
    row = sds((1, 16), f32)
    grad_q, grad_kv, grad_o, router_grad, first_grad, second_grad = call(
        final_kernel, [mat, mat, mat, sds((1, 16, E), f32), row, row],
        vm(keep) + pin(swap(send)) + [(ANY, query_weight), (ANY, key_value_matrix)] + vm(first_gain),
        [pltpu.VMEM((16, D), bf16), pltpu.VMEM((16, D), bf16), sems(2)],
    )
    return (
        layer_out, input_grad, first_grad, grad_q, grad_kv, grad_o, second_grad, router_grad, ex_in, ex_out,
    )


def solution(mesh):
    grid = Mesh(mesh.devices.reshape(2, 4, 4, 4), ("section", "y", "x", "expert"))
    ctx = ("y", "x")
    every = ("y", "x", "expert")
    placed = (
        P(None, "expert", ctx, None),
        P(None, "expert", ctx),
        P("section", None, "expert", ctx, None),
        P(None, "expert", ctx, None),
        P("section", None),
        P("section", None, None),
        P("section", None, None),
        P("section", None, None),
        P("section", None),
        P("section", None, None),
        P("section", "expert", None, None),
        P("section", "expert", None, None),
    )
    return jax.shard_map(
        local,
        mesh=grid,
        in_specs=placed,
        out_specs=(
            P("section", None, "expert", ctx, None),
            P("section", None, "expert", ctx, None),
            P("section", every),
            P("section", every, None),
            P("section", every, None),
            P("section", every, None),
            P("section", every),
            P("section", every, None),
            P("section", "expert", ctx, None),
            P("section", "expert", ctx, None),
        ),
        check_vma=False,
    )
```

```python
import functools
import math

import jax
import jax.numpy as jnp
from jax import lax
from jax.experimental import pallas as pl
from jax.experimental.pallas import tpu as pltpu
from jax.sharding import Mesh
from jax.sharding import PartitionSpec as P

T = 64
D = 1024
HW = 64
WIDE = 5 * HW
NQ = 16
NK = 8
F = 512
E = 32
CAP = 17
MAIN = E * 16
SLOTS = E * CAP
GROUP_SIZE = 16
ROWS_OF = GROUP_SIZE * CAP
N_CTX = 16
SEQ = N_CTX * T

eps = 1e-06
rope_base = 10000.0
masked = -1e30
f32 = jnp.float32
bf16 = jnp.bfloat16

VMEM = pl.BlockSpec(memory_space=pltpu.VMEM)
SMEM = pl.BlockSpec(memory_space=pltpu.SMEM)
ANY = pl.BlockSpec(memory_space=pl.ANY)
PIN = "pinned"
GROUP = ("x", "expert")
CTX = ("y", "x")
ALL = ("y", "x", "expert")


def sds(shape, dtype):
    return jax.ShapeDtypeStruct(shape, dtype)


def pinned(shape, dtype):
    return pltpu.VMEM(shape, dtype)


class Later:
    def __init__(self, source, place, sem):
        self.place = place
        self.copy = pltpu.make_async_copy(source, place, sem)
        self.copy.start()

    def wait(self):
        if self.copy is not None:
            self.copy.wait()
            self.copy = None

    def __getitem__(self, index):
        self.wait()
        return self.place[index]


def call(body, outs, ins, scratch=(), flops=0, limit=36, out_spec=VMEM, lazy=True):
    late = [i for i, (k, _) in enumerate(ins) if k is VMEM]
    count, own = len(ins) + len(outs), len(scratch)

    def kernel(*refs):
        places, sems = refs[count + own : -1], refs[-1]
        args = list(refs[: len(ins)])
        for n, i in enumerate(late):
            args[i] = Later(args[i], places[n], sems.at[n])
        moving = [args[i] for i in late]
        if not lazy:
            for v in moving:
                v.wait()
        body(*args, *refs[len(ins) : count + own])
        for v in moving:
            v.wait()

    place = lambda k, a: a if k is SMEM else pltpu.with_memory_space_constraint(a, pltpu.VMEM if k is PIN else pltpu.HBM)
    outs = [o if isinstance(o, jax.ShapeDtypeStruct) is False else pltpu.HBM(o.shape, o.dtype) for o in outs]
    read = sum(a.size * a.dtype.itemsize for k, a in ins if k is VMEM)
    written = sum(math.prod(o.shape) * jnp.dtype(o.dtype).itemsize for o in outs)
    return pl.pallas_call(
        kernel,
        out_shape=list(outs),
        in_specs=[VMEM if k is PIN else ANY for k, _ in ins],
        out_specs=[out_spec] * len(outs),
        scratch_shapes=[
            *scratch,
            *[pltpu.VMEM(ins[i][1].shape, ins[i][1].dtype) for i in late],
            pltpu.SemaphoreType.DMA((max(1, len(late)),)),
        ],
        compiler_params=pltpu.CompilerParams(vmem_limit_bytes=limit * 1024 * 1024),
        cost_estimate=pl.CostEstimate(
            flops=int(flops), bytes_accessed=int(read + written), transcendentals=0
        ),
    )(*[place(k, a) for k, a in ins])


def dot(a, b):
    return lax.dot_general(a, b, (((1,), (0,)), ((), ())), preferred_element_type=f32)


def dot_nt(a, b):
    return lax.dot_general(a, b, (((1,), (1,)), ((), ())), preferred_element_type=f32)


def dot_tn(a, b):
    return lax.dot_general(a, b, (((0,), (0,)), ((), ())), preferred_element_type=f32)


def split(v):
    high = v.astype(bf16)
    return high, (v - high.astype(f32)).astype(bf16)


def iota(shape, dim):
    return lax.broadcasted_iota(jnp.int32, shape, dim)


def one_hot(cond):
    return jnp.where(cond, 1.0, 0.0).astype(bf16)


def expert_of(k):
    return 8 * ((k >> 1) & 3) + 2 * (k >> 3) + (k & 1)


def slot_table():
    row, col = iota((SLOTS, E), 0), iota((SLOTS, E), 1)
    return one_hot(expert_of(jnp.where(row < MAIN, row >> 4, row - MAIN)) == col)


def moved_rows(index, q, order):
    bits = q.bit_length() - 1
    if order == "block":
        return index >> (bits + 1), (index >> 1) & (q - 1), index & 1
    if order == "token":
        return (index >> 1) & 15, index >> 5, index & 1
    return index & 15, (index >> 4) & (q - 1), index >> (bits + 4)


def shuffle(q, to, order):
    n = 32 * q
    d, p, i = moved_rows(iota((n, n), 0), q, to)
    at = iota((n, n), 1)
    if order == "block":
        return one_hot(at == d * (2 * q) + p * 2 + i)
    if order == "token":
        return one_hot(at == p * 32 + d * 2 + i)
    return one_hot(at == (i * q + p) * 16 + d)


def pack(buf_ref, parts):
    n = len(parts)
    extra = []
    for k, rows in enumerate(parts):
        for c in range(8):
            piece = rows[:, c * 128 : (c + 1) * 128]
            buf_ref[:, k * 256 + c * 32 : k * 256 + (c + 1) * 32, :] = piece[:MAIN].reshape(16, 32, 128)
            extra.append(piece[MAIN:])
    moved = dot(shuffle(8 * n, "block", "token"), jnp.concatenate(extra, axis=0)).astype(bf16)
    buf_ref[:, 256 * n :, :] = moved.reshape(16, 16 * n, 128)


def unpack(buf_ref, n):
    rest = buf_ref[:, 256 * n :, :].reshape(256 * n, 128)
    moved = dot(shuffle(8 * n, "token", "block"), rest).astype(bf16)
    parts = []
    for k in range(n):
        pieces = []
        for c in range(8):
            head = buf_ref[:, k * 256 + c * 32 : k * 256 + (c + 1) * 32, :].reshape(MAIN, 128)
            at = (k * 8 + c) * E
            pieces.append(jnp.concatenate([head, moved[at : at + E]], axis=0))
        parts.append(jnp.concatenate(pieces, axis=1))
    return parts


def pack_experts(buf_ref, parts):
    n = len(parts)
    extra = []
    for i in range(2):
        for k in range(n):
            for c in range(8):
                piece = parts[k][i][:, c * 128 : (c + 1) * 128]
                at = k * 256 + c * 32 + i * 16
                buf_ref[:, at : at + 16, :] = piece[:256].reshape(16, 16, 128)
                extra.append(piece[256:])
    moved = dot(shuffle(8 * n, "block", "expert"), jnp.concatenate(extra, axis=0)).astype(bf16)
    buf_ref[:, 256 * n :, :] = moved.reshape(16, 16 * n, 128)


def unpack_experts(buf_ref, n):
    rest = buf_ref[:, 256 * n :, :].reshape(256 * n, 128)
    moved = dot(shuffle(8 * n, "expert", "block"), rest).astype(bf16)
    parts = []
    for k in range(n):
        both = []
        for i in range(2):
            pieces = []
            for c in range(8):
                at = k * 256 + c * 32 + i * 16
                head = buf_ref[:, at : at + 16, :].reshape(256, 128)
                at = (i * 8 * n + k * 8 + c) * 16
                pieces.append(jnp.concatenate([head, moved[at : at + 16]], axis=0))
            both.append(jnp.concatenate(pieces, axis=1))
        parts.append(both)
    return parts


def norm_parts(v):
    r = lax.rsqrt(jnp.mean(v * v, axis=-1, keepdims=True) + eps)
    return r, v * r


def norm_back(v, gain, dh):
    r, n = norm_parts(v)
    a = gain * dh
    return r * (a - n * jnp.mean(n * a, axis=-1, keepdims=True)), dh * n


def rotate(chunk, cos, sin):
    lane = iota(chunk.shape, 1) & 63
    other = jnp.where(lane < 32, pltpu.roll(chunk, 96, 1), pltpu.roll(chunk, 32, 1))
    return chunk * cos + other * sin


class Copy:
    def __init__(self, ref, place, sem):
        self.copy = pltpu.make_async_copy(ref, place, sem)
        self.copy.start()

    def wait(self):
        self.copy.wait()


def at_axis(axis):
    return lax.axis_index(axis)


class Chosen(Copy):
    def __init__(self, layer, own, sent, place, sem):
        self.copy = pltpu.make_async_copy(own, place, sem)
        mine = at_axis("section") == layer

        @pl.when(mine)
        def _():
            self.copy.start()

        @pl.when(jnp.logical_not(mine))
        def _():
            pltpu.make_async_copy(sent, place, sem).start()


def either(layer, own, sent):
    return jnp.where(at_axis("section") == layer, own, sent)


def prep_kernel(ids_own, ids_sent, r_own, r_sent, s0, st0, m0, s1, st1, m1, router):
    for layer in range(2):
        router[layer] = either(layer, r_own[0], r_sent[0])
    rep = slot_table()
    own = ids_own[0, at_axis("section"), 0]
    sent = ids_sent[...]
    for layer, (s_ref, st_ref, m_ref) in enumerate(((s0, st0, m0), (s1, st1, m1))):
        ids = either(layer, own, sent)
        col = iota((T, E), 1)
        member = jnp.zeros((T, E), f32)
        for k in range(8):
            member = member + jnp.where(ids[:, k : k + 1] == col, 1.0, 0.0)
        m_ref[...] = member
        low = member.astype(bf16)
        row64, col64 = iota((T, T), 0), iota((T, T), 1)
        rank = dot(one_hot(col64 < row64), low)
        rank = jnp.where(member > 0.5, rank, -1.0).astype(bf16)
        at = dot_nt(rank, rep)
        slot = iota((T, SLOTS), 1)
        place = jnp.where(slot < MAIN, slot & 15, 16).astype(f32)
        st_ref[...] = one_hot(at == place)
        eye = one_hot(iota((E, E), 0) == iota((E, E), 1))
        member_t = dot_nt(eye, low)
        rank_t = dot(member_t.astype(bf16), one_hot(row64 < col64))
        rank_t = jnp.where(member_t > 0.5, rank_t, -1.0).astype(bf16)
        at_t = dot(rep, rank_t)
        slot_t = iota((SLOTS, T), 0)
        place_t = jnp.where(slot_t < MAIN, slot_t & 15, 16).astype(f32)
        s_ref[...] = one_hot(at_t == place_t)


def pair_kernel(in_own, out_own, experts, at, sems):
    moves = []

    def move(source, place, target):
        n = len(moves)
        first = pltpu.make_async_copy(source, place, sems.at[2 * n])
        moves.append((first, pltpu.make_async_copy(place, target, sems.at[2 * n + 1])))
        first.start()

    for i in range(2):
        e = 2 * at_axis("x") + i
        move(in_own.at[0, e], at.at[i, :, : 2 * F], experts.at[0, i, :, : 2 * F])
        move(out_own.at[0, e], at.at[i, :, 2 * F :], experts.at[0, i, :, 2 * F :])
    for first, second in moves:
        first.wait()
        second.start()
    for _, second in moves:
        second.wait()


def qkv_pack(q, kv, cos, sin, pos, buf_ref):
    hi = jnp.floor(pos * (1.0 / 32.0))
    lo = pos - hi * 32.0
    lane = iota((T, 64), 1)
    where_am_i = jnp.where(lane == 0, hi, jnp.where(lane == 1, lo, 0.0)).astype(bf16)
    for pair in range(4):
        k_two = rotate(kv[:, pair * 128 : (pair + 1) * 128], cos, sin).astype(bf16)
        v_two = kv[:, 512 + pair * 128 : 512 + (pair + 1) * 128].astype(bf16)
        for g in range(2):
            k_one = k_two[:, g * 64 : (g + 1) * 64]
            v_one = v_two[:, g * 64 : (g + 1) * 64]
            group = pair * 2 + g
            q_two = rotate(q[:, group * 128 : (group + 1) * 128], cos, sin).astype(bf16)
            low_half = jnp.concatenate([v_one, where_am_i], axis=1)
            for j in range(2):
                top = jnp.concatenate([q_two[:, j * 64 : (j + 1) * 64], k_one], axis=1)
                buf_ref[2 * group + j, 0:T, :] = top
                buf_ref[2 * group + j, T : 2 * T, :] = low_half


def rotary(pos):
    rows = pos.shape[0]
    lane = iota((rows, 128), 1)
    frequency = jnp.exp((lane & 31).astype(f32) * (-2.0 * math.log(rope_base) / HW))
    angles = pos * frequency
    sin = jnp.sin(angles)
    return jnp.cos(angles), jnp.where((lane & 63) < 32, -sin, sin)


def table_kernel(pos, cos, sin):
    for start in range(0, SEQ, 256):
        at = slice(start, start + 256)
        cos[at], sin[at] = rotary(pos[at])


def first_kernel(tok, places, gain, q_own, kv_own, h1_a, h1_b, buf_a, buf_b, cos_ref, sin_ref, q_w, kv_w, sems):
    q_copy = pltpu.make_async_copy(q_own.at[0], q_w, sems.at[0])
    kv_copy = pltpu.make_async_copy(kv_own.at[0], kv_w, sems.at[1])
    q_copy.start()
    kv_copy.start()
    x = jnp.concatenate([tok[0, 0], tok[1, 0]], axis=0).astype(f32)
    h1 = (norm_parts(x)[1] * gain[...]).astype(bf16)
    h1_a[...] = h1[:T]
    h1_b[...] = h1[T:]
    eye = iota((T, T), 0) == iota((T, T), 1)
    columns = [
        jnp.sum(jnp.where(eye, places[m].astype(f32), 0.0), axis=1, keepdims=True) for m in range(2)
    ]
    pos = jnp.concatenate(columns, axis=0)
    cos, sin = rotary(pos)
    cos_ref[...] = cos
    sin_ref[...] = sin
    q_copy.wait()
    q = dot(h1, q_w[...])
    kv_copy.wait()
    kv = dot(h1, kv_w[...])
    for m, buf_ref in enumerate((buf_a, buf_b)):
        at = slice(m * T, (m + 1) * T)
        qkv_pack(q[at], kv[at], cos[at], sin[at], pos[at], buf_ref)


def attention_parts(buf):
    q = buf[:, 0:T, 0:HW].reshape(SEQ, HW)
    k = buf[:, 0:T, HW : 2 * HW].reshape(SEQ, HW)
    v = buf[:, T : 2 * T, 0:HW].reshape(SEQ, HW)
    return q, k, v


def sent_positions(buf):
    hi = buf[:, T : 2 * T, HW : HW + 1].reshape(SEQ, 1).astype(f32)
    lo = buf[:, T : 2 * T, HW + 1 : HW + 2].reshape(SEQ, 1).astype(f32)
    return hi * 32.0 + lo


def block_probs(q, k, pos, start, rows):
    keys = start + rows
    scores = dot_nt(q[start : start + rows], k[:keys]) * (HW**-0.5)
    at = (iota((rows, keys), 0) + start).astype(f32)
    key = iota((rows, keys), 1).astype(f32)
    begin = at[:, 0:1] - pos[start : start + rows]
    scores = jnp.where((key <= at) & (key >= begin), scores, masked)
    raised = jnp.exp(scores - jnp.max(scores, axis=-1, keepdims=True))
    return raised / jnp.sum(raised, axis=-1, keepdims=True)


ROWS = 256


def attend_kernel(layer, buf_ref, *refs):
    q, k, v = attention_parts(buf_ref[...])
    if layer == 0:
        out_ref, kept, pos_ref = refs
        pos = sent_positions(buf_ref[...])
        pos_ref[...] = pos
    else:
        pos_ref, out_ref, kept = refs
        pos = pos_ref[...]
    kept[...] = buf_ref[...]
    for start in range(0, SEQ, ROWS):
        probs = block_probs(q, k, pos, start, ROWS)
        o = dot(probs.astype(bf16), v[: start + ROWS]).astype(bf16)
        for b in range(ROWS // T):
            piece = o[b * T : (b + 1) * T]
            out_ref[start // T + b] = jnp.concatenate([piece[: T // 2], piece[T // 2 :]], axis=1)


def heads_in(buf_ref, o_ref):
    for g in range(8):
        a, b = buf_ref[2 * g], buf_ref[2 * g + 1]
        o_ref[0 : T // 2, g * 128 : (g + 1) * 128] = jnp.concatenate([a[:, :64], b[:, :64]], axis=1)
        o_ref[T // 2 : T, g * 128 : (g + 1) * 128] = jnp.concatenate([a[:, 64:], b[:, 64:]], axis=1)


def heads_out(do, buf_ref, start):
    for g in range(8):
        two = do[:, g * 128 : (g + 1) * 128]
        for j in range(2):
            one = two[:, j * 64 : (j + 1) * 64]
            block = jnp.concatenate([one[: T // 2], one[T // 2 :]], axis=1)
            buf_ref[2 * g + j, start : start + T // 2, :] = block


def gates_from(logits, member):
    chosen = member > 0.5
    largest = jnp.max(jnp.where(chosen, logits, masked), axis=-1, keepdims=True)
    raised = jnp.where(chosen, jnp.exp(jnp.minimum(logits - largest, 0.0)), 0.0)
    return raised / jnp.sum(raised, axis=-1, keepdims=True)


def gated_rows(gates, s, rep, g_low):
    high, low = split(gates)
    up = (s * dot_nt(rep, high).astype(bf16)).astype(bf16)
    down = (s * dot_nt(rep, low).astype(bf16)).astype(bf16)
    return (dot(up, g_low) + dot(down, g_low)).astype(bf16)


def mid_kernel(layer, *refs):
    ob, x_ref, wo_all, gain, r_ref, s_ref, m_ref = refs[:7]
    h1_refs, (mid_ref, h2_ref, gates_ref, pair_ref, buf_ref, wo, sems) = refs[7:-7], refs[-7:]
    copy = Copy(wo_all.at[layer], wo, sems.at[0])
    o_ref = pair_ref.at[:, D:]
    heads_in(ob, o_ref)
    if layer == 0:
        pair_ref[:, :D] = jnp.where(at_axis("section") == 0, h1_refs[0][...], h1_refs[1][...])
    else:
        pair_ref[:, :D] = h1_refs[0][...]
    x = (tok_row(x_ref) if layer == 0 else x_ref[...]).astype(f32)
    copy.wait()
    middle = x + dot(o_ref[...], wo[...])
    mid_ref[...] = middle
    h2 = (norm_parts(middle)[1] * gain[layer]).astype(bf16)
    h2_ref[...] = h2
    pack(buf_ref, [dot(s_ref[...], h2).astype(bf16)])
    gates_ref[...] = gates_from(dot(h2, r_ref[layer]), m_ref[...])


def send_back_kernel(gates, s_ref, cot, buf_ref):
    pack(buf_ref, [gated_rows(gates[...], s_ref[...], slot_table(), tok_row(cot))])


def tok_row(ref):
    return ref[at_axis("section"), 0]


def hidden_of(gu):
    gate, up = gu[:, :F], gu[:, F:]
    sg = jax.nn.sigmoid(gate)
    return gate, up, sg, (gate * sg * up).astype(bf16)


def sorted_out(i, keep, send, at, value):
    cols = slice(at, at + value.shape[1])

    @pl.when(at_axis("section") == i)
    def _():
        keep[:, cols] = value

    @pl.when(at_axis("section") != i)
    def _():
        send[:, cols] = value


def expert_forward_kernel(layer, buf, w_all, ybuf, gu_ref, keep, send, w, sems):
    copies = [Copy(w_all.at[layer, i], w.at[i], sems.at[i]) for i in range(2)]
    (x,) = unpack_experts(buf, 1)
    y = []
    for i in range(2):
        copies[i].wait()
        gu = dot(x[i], w[i, :, : 2 * F])
        gu_ref[i] = gu
        y.append(dot_nt(hidden_of(gu)[3], w[i, :, 2 * F :]).astype(bf16))
        sorted_out(i, keep, send, 0, x[i])
    pack_experts(ybuf, [y])


def expert_back(dy, gu, w_in, w_out):
    gate, up, sg, z = hidden_of(gu)
    dz = dot(dy, w_out)
    dgate = dz * up * (sg + gate * sg * (1.0 - sg))
    dup = dz * gate * sg
    dgu = jnp.concatenate([dgate, dup], axis=1).astype(bf16)
    return z, dgu, dot_nt(dgu, w_in).astype(bf16)


def expert_back_kernel(layer, buf, gu_all, w_all, back, keep, send, w, gu, sems):
    copies = []
    for i in range(2):
        copies.append(Copy(w_all.at[layer, i], w.at[i], sems.at[i]))
        copies.append(Copy(gu_all.at[i], gu.at[i], sems.at[2 + i]))
    (dy,) = unpack_experts(buf, 1)
    dx = []
    for i in range(2):
        copies[2 * i].wait()
        copies[2 * i + 1].wait()
        z, dgu, dx_i = expert_back(dy[i], gu[i], w[i, :, : 2 * F], w[i, :, 2 * F :])
        dx.append(dx_i)
        for at, value in ((0, dy[i]), (D, dgu), (D + 2 * F, z)):
            sorted_out(i, keep, send, at, value)
    pack_experts(back, [dx])


def expert_grad_kernel(x_keep, x_got, keep, got, out):
    x = jnp.concatenate([x_keep[...], x_got[...]], axis=0)
    dy = jnp.concatenate([keep[:, :D], got[:, :D]], axis=0)
    dgu = jnp.concatenate([keep[:, D : D + 2 * F], got[:, D : D + 2 * F]], axis=0)
    z = jnp.concatenate([keep[:, D + 2 * F : D + 3 * F], got[:, D + 2 * F : D + 3 * F]], axis=0)
    out[:, : 2 * F] = dot_tn(x, dgu).astype(bf16)
    out[:, 2 * F :] = dot_tn(dy, z).astype(bf16)


def expert_rows_kernel(rows, b0, b1, b2, b3):
    for k, b in enumerate((b0, b1, b2, b3)):
        at = pl.multiple_of(((at_axis("x") + k) & 3) * T, T)
        b[...] = rows[pl.ds(at, T), :]


def expert_sort_kernel(*refs):
    keep, send = refs[8:]
    for layer in range(2):
        for k in range(4):
            block = refs[4 * layer + k]
            place = (at_axis("x") - k) & 3

            @pl.when(at_axis("section") == layer)
            def _():
                keep[place] = block[...]

            @pl.when(at_axis("section") != layer)
            def _():
                send[place] = block[...]


def expert_final_kernel(keep, got, out_in, out_out):
    for x in range(4):
        for ref, j in ((keep, at_axis("section")), (got, 1 - at_axis("section"))):
            out_in[0, 2 * x + j] = ref[x, :, : 2 * F].astype(f32)
            out_out[0, 2 * x + j] = ref[x, :, 2 * F :].astype(f32)


def place_kernel(keep, got, out):
    out[0, at_axis("section"), 0] = keep[...]
    out[0, 1 - at_axis("section"), 0] = got[...]


def by_section(v_0, v_1, keep, send):
    keep[...] = jnp.where(at_axis("section") == 0, v_0, v_1)
    send[...] = jnp.where(at_axis("section") == 0, v_1, v_0)


def combine(middle, gates, st, rep, y):
    high, low = split(gates)
    up = (st * dot_nt(high, rep).astype(bf16)).astype(bf16)
    down = (st * dot_nt(low, rep).astype(bf16)).astype(bf16)
    return middle + (dot(up, y) + dot(down, y))


def micro_rows(ref):
    return ref[pl.ds(pl.multiple_of(at_axis("section") * T, T), T), :]


def next_kernel(
    yb, mid, gates, st, cos, sin, gain, q_own, q_sent, kv_own, kv_sent, out_ref, h1_ref, saved, buf_ref, q_w, kv_w, sems,
):
    saved[...] = yb[...]
    q_copy = Chosen(1, q_own.at[0], q_sent.at[0], q_w, sems.at[0])
    kv_copy = Chosen(1, kv_own.at[0], kv_sent.at[0], kv_w, sems.at[1])
    (y,) = unpack(yb, 1)
    out = combine(mid[...], gates[...], st[...], slot_table(), y).astype(bf16)
    out_ref[...] = out
    h1 = (norm_parts(out.astype(f32))[1] * gain[1]).astype(bf16)
    h1_ref[...] = h1
    q_copy.wait()
    q = dot(h1, q_w[...])
    kv_copy.wait()
    kv = dot(h1, kv_w[...])
    qkv_pack(q, kv, micro_rows(cos), micro_rows(sin), jnp.zeros((T, 1), f32), buf_ref)


def route_back_kernel(layer, *refs):
    yb, gates_ref, st_ref, r_ref, g_ref = refs[:5]
    dlog_ref, dh2_ref = refs[-2:]
    rep, st, gates = slot_table(), st_ref[...], gates_ref[...]
    (y,) = unpack(yb, 1)
    if layer == 1:
        mid, out_0, keep, send = refs[5:9]
        g_low = tok_row(g_ref)
        by_section(out_0[...], combine(mid[...], gates, st, rep, y).astype(bf16), keep, send)
    else:
        g_low = g_ref[...]
    d_slot = dot_nt(g_low, y) * st.astype(f32)
    high, low = split(d_slot)
    d_gates = dot(high, rep) + dot(low, rep)
    d_chosen = gates * (d_gates - jnp.sum(gates * d_gates, axis=-1, keepdims=True))
    d_log = d_chosen.astype(bf16)
    dlog_ref[...] = d_log
    dh2_ref[...] = dot_nt(d_log, r_ref[layer])


def turn_kernel(layer, *refs):
    dxb, st, dh2, mid, gain, g_ref, wo_all, dmid_ref, dhn_ref, dobuf, wo, sems = refs
    copy = Copy(wo_all.at[layer], wo, sems.at[0])
    (dx,) = unpack(dxb, 1)
    g_low = tok_row(g_ref) if layer == 1 else g_ref[...]
    d_h2 = dot(st[...], dx) + dh2[...]
    d_v, d_hn = norm_back(mid[...], gain[layer], d_h2)
    d_mid = g_low.astype(f32) + d_v
    d_a = d_mid.astype(bf16)
    heads_out(d_a, dobuf, T // 2)
    copy.wait()
    heads_out(dot_nt(d_a, wo[...]).astype(bf16), dobuf, 0)
    dmid_ref[...] = d_mid
    dhn_ref[...] = d_hn.astype(bf16)


def attend_back_kernel(buf_ref, dobuf, pos_ref, out_ref, saved, da_saved, dk_ref, dv_ref):
    q, k, v = attention_parts(buf_ref[...])
    pos = pos_ref[...]
    da_saved[...] = dobuf[:, T // 2 :, :]
    packed = dobuf[:, : T // 2, :]
    do = halves(packed)
    scale = HW**-0.5
    dq = []
    for start in reversed(range(0, SEQ, ROWS)):
        keys = start + ROWS
        probs = block_probs(q, k, pos, start, ROWS)
        do_rows = do[start:keys]
        d_probs = dot_nt(do_rows, v[:keys])
        inner = jnp.sum(probs * d_probs, axis=-1, keepdims=True)
        d_scores = (probs * (d_probs - inner)).astype(bf16)
        dq.append((dot(d_scores, k[:keys]) * scale).astype(bf16))
        d_k = dot_tn(d_scores, q[start:keys]) * scale
        d_v = dot_tn(probs.astype(bf16), do_rows)
        if keys == SEQ:
            dk_ref[...] = d_k
            dv_ref[...] = d_v
        else:
            dk_ref[0:keys] = dk_ref[0:keys] + d_k
            dv_ref[0:keys] = dv_ref[0:keys] + d_v
    d_q = jnp.concatenate(dq[::-1], axis=0)
    d_k = dk_ref[...].astype(bf16)
    d_v = dv_ref[...].astype(bf16)
    out_ref[:, 0:T, :] = jnp.concatenate([d_q, d_k], axis=1).reshape(N_CTX, T, 128)
    d_v = d_v.reshape(N_CTX, T, HW)
    out_ref[:, T:, :] = jnp.concatenate([d_v[:, : T // 2], d_v[:, T // 2 :]], axis=2)
    saved[...] = out_ref[...]


def back_kernel(layer, *refs):
    refs = list(refs)
    buf, x_ref, dmid, cos_ref, sin_ref, gain, q_own, q_sent, kv_own, kv_sent = refs[:10]
    refs = refs[10:]
    if layer == 1:
        s_ref, gates_ref = refs[:2]
        refs = refs[2:]
    if layer == 0:
        grad_1 = refs.pop(0)
        keep, send = refs[:2]
        refs = refs[2:]
    else:
        grad_ref = refs.pop(0)
    if layer == 1:
        g_ref, dybuf = refs[:2]
        refs = refs[2:]
    q_w, kv_w, dq_ref, dkv_ref, sems = refs
    q_copy = Chosen(layer, q_own.at[0], q_sent.at[0], q_w, sems.at[0])
    kv_copy = Chosen(layer, kv_own.at[0], kv_sent.at[0], kv_w, sems.at[1])
    cos, sin = micro_rows(cos_ref), -micro_rows(sin_ref)
    half = T // 2
    k_parts, v_parts = [], []
    for g in range(8):
        a, b = buf[2 * g], buf[2 * g + 1]
        q_two = jnp.concatenate([a[:T, :64], b[:T, :64]], axis=1).astype(f32)
        dq_ref[:, g * 128 : (g + 1) * 128] = rotate(q_two, cos, sin).astype(bf16)
        k_parts.append(a[:T, 64:].astype(f32) + b[:T, 64:].astype(f32))
        v_sum = a[T:].astype(f32) + b[T:].astype(f32)
        v_parts.append(jnp.concatenate([v_sum[:, :64], v_sum[:, 64:]], axis=0))
    for p in range(4):
        k_two = jnp.concatenate([k_parts[2 * p], k_parts[2 * p + 1]], axis=1)
        v_two = jnp.concatenate([v_parts[2 * p], v_parts[2 * p + 1]], axis=1)
        dkv_ref[:, p * 128 : (p + 1) * 128] = rotate(k_two, cos, sin).astype(bf16)
        dkv_ref[:, 512 + p * 128 : 512 + (p + 1) * 128] = v_two.astype(bf16)
    q_copy.wait()
    kv_copy.wait()
    d_h1 = dot_nt(dq_ref[...], q_w[...]) + dot_nt(dkv_ref[...], kv_w[...])
    x = (tok_row(x_ref) if layer == 0 else x_ref[...]).astype(f32)
    d_x, _ = norm_back(x, gain[layer], d_h1)
    grad = dmid[...] + d_x
    if layer == 0:
        by_section(grad, grad_1[...], keep, send)
    else:
        grad_ref[...] = grad
        g_low = grad.astype(bf16)
        g_ref[...] = g_low
        pack(dybuf, [gated_rows(gates_ref[...], s_ref[...], slot_table(), g_low)])


def head_grad_kernel(layer, back, da, cos_ref, sin_ref, pairs, h2, dlog, dhn2, *refs):
    out = refs[-1]
    if layer == 0:
        out[:, WIDE:] = refs[0][...]
    cos, sin = cos_ref[...], -sin_ref[...]
    both = rotate(back[:, :T, :].reshape(SEQ, 2 * HW).astype(f32), cos, sin).astype(bf16)
    lane = iota((T, HW), 1)
    logs = jnp.concatenate([dlog[...], jnp.zeros((T, HW - E), bf16)], axis=1)
    extra = dot_tn(logs, h2[...]) + dot_tn(one_hot(lane == E), dhn2[...])
    h1_all = pairs[:, :D]
    out[:, : 2 * HW] = dot_tn(both, h1_all).T.astype(bf16)
    rest = [dot_tn(halves(back[:, T:, :]), h1_all), dot_tn(halves(da[...]), pairs[:, D:]), extra]
    out[:, 2 * HW : WIDE] = jnp.concatenate(rest, axis=0).T.astype(bf16)


def halves(packed):
    return jnp.concatenate([packed[:, :, :HW], packed[:, :, HW:]], axis=1).reshape(SEQ, HW)


def head_sums(got, layer):
    v = []
    cols = slice(WIDE * layer, WIDE * (layer + 1))
    for c in range(N_CTX):
        v.append(sum(got[4 * c + k, :, cols].astype(f32) for k in range(1, 4)) + got[4 * c, :, cols].astype(f32))
    pair = [v[2 * g] + v[2 * g + 1] for g in range(NK)]
    parts = []
    for blocks, at in ((v, 3 * HW), (v, 0), (pair, HW), (pair, 2 * HW)):
        for a, b in zip(blocks[::2], blocks[1::2]):
            parts.append(jnp.concatenate([a[:, at : at + HW], b[:, at : at + HW]], axis=1))
    total = sum(pair[1:]) + pair[0]
    parts.append(total[:, 3 * HW :])
    return jnp.concatenate(parts, axis=1)


def halves_kernel(got, keep, send):
    by_section(head_sums(got, 0), head_sums(got, 1), keep, send)


def final_kernel(keep, got, q_own, kv_own, gain, gq, gkv, go, gr, g1, g2, q_rows, kv_rows, sems):
    first = 16 * at_axis(ALL)
    rows = pl.ds(pl.multiple_of(first, 16), 16)
    copies = [Copy(q_own.at[0, rows], q_rows, sems.at[0]), Copy(kv_own.at[0, rows], kv_rows, sems.at[1])]
    mine = keep[...] + got[...]
    grad_q, grad_kv, rest = mine[:, D : 2 * D], mine[:, 2 * D : 3 * D], mine[:, 3 * D :]
    go[0] = mine[:, :D]
    gq[0] = grad_q
    gkv[0] = grad_kv
    gr[0] = rest[:, HW : HW + E]
    eye = iota((16, 16), 0) == iota((16, 16), 1)
    as_row = lambda column: jnp.sum(jnp.where(eye, column, 0.0), axis=0, keepdims=True)
    g2[...] = as_row(rest[:, HW + E : HW + E + 1])
    here = iota((16, D), 1) == iota((16, D), 0) + first
    gains = jnp.sum(jnp.where(here, gain[...], 0.0), axis=1, keepdims=True)
    for copy in copies:
        copy.wait()
    both = grad_q * q_rows[...].astype(f32) + grad_kv * kv_rows[...].astype(f32)
    g1[...] = as_row(jnp.sum(both, axis=-1, keepdims=True) / gains)


def swap(v):
    return lax.ppermute(v, "section", [(0, 1), (1, 0)])


def either_order(first, mine, other):
    return jnp.where(first, mine, other), jnp.where(first, other, mine)


def all_to_all(v, axes):
    return lax.all_to_all(v, axes, 0, 0, tiled=True)


def local(
    tokens, positions, expert_ids, cotangent, first_gain, query_weight, key_value_matrix,
    output_weight, second_gain, router_weight, expert_in, expert_out,
):
    s, y_at, x_at, z_at = (lax.axis_index(a) for a in ("section", "y", "x", "expert"))
    first = s == 0
    vm = lambda *arrays: [(VMEM, a) for a in arrays]
    pin = lambda *arrays: [(PIN, a) for a in arrays]
    sems = lambda n: pltpu.SemaphoreType.DMA((n,))
    tied = lambda v, *after: lax.optimization_barrier((v,) + after)[0]

    def with_(v, others):
        v, *others = lax.optimization_barrier((v, *others))
        return v, others

    def gather(v, axis):
        return lax.all_gather(v, axis, axis=0, tiled=True)

    def both(v):
        return lax.all_gather(v, "section", axis=0, tiled=True)

    def round_trip(blocks, axis):
        route = lambda k: [(i, (i + k) % 4) for i in range(4)]
        return [blocks[0]] + [lax.ppermute(blocks[k], axis, route(k)) for k in range(1, 4)]

    w_dd = pltpu.VMEM((D, D), bf16)
    ex_scratch = [pltpu.VMEM((2, D, 3 * F), bf16), sems(2)]
    qkv_shape = pinned((N_CTX, 2 * T, 128), bf16)
    o_shape = pinned((N_CTX, T // 2, 128), bf16)
    qkv_half = pinned((N_CTX, T, 128), bf16)
    back_shape = pinned((N_CTX, T + T // 2, 128), bf16)
    rows_shape = pinned((GROUP_SIZE, 272, 128), bf16)
    row_low, row_full = sds((T, D), bf16), sds((T, D), f32)
    gates_shape, log_shape = sds((T, E), f32), sds((T, E), bf16)
    o_saved, back_saved = sds(o_shape.shape, bf16), sds(back_shape.shape, bf16)
    qkv_saved, rows_saved = sds(qkv_shape.shape, bf16), sds(rows_shape.shape, bf16)
    kv_scratch = [pltpu.VMEM((SEQ, HW), f32), pltpu.VMEM((SEQ, HW), f32)]
    dqkv_scratch = [w_dd, w_dd, pltpu.VMEM((T, D), bf16), pltpu.VMEM((T, D), bf16), sems(2)]

    table = sds((2 * T, 128), f32)
    h1_a, h1_b, buf_a, buf_b, cos, sin = call(
        first_kernel, [row_low, row_low, qkv_shape, qkv_shape, table, table],
        vm(tokens, positions, first_gain) + [(ANY, query_weight), (ANY, key_value_matrix)],
        [w_dd, w_dd, sems(2)], flops=6e8,
    )
    down = lambda v: lax.ppermute(v, "section", [(0, 1)])
    buf = jnp.where(first, buf_a, down(buf_b))
    h1_b = down(h1_b)

    late = lambda v: tied(v, buf_a)
    wo_all = both(late(output_weight))
    g1, g2 = (jnp.stack(either_order(first, v, swap(late(v)))) for v in (first_gain, second_gain))
    r_sent = swap(late(router_weight))
    ids_sent = swap(late(lax.dynamic_slice(expert_ids, (0, 1 - s, 0, 0, 0), (1, 1, 1, T, 8)))).reshape(T, 8)
    (pair,) = call(
        pair_kernel, [sds((1, 2, D, 3 * F), bf16)], [(ANY, tied(v, buf)) for v in (expert_in, expert_out)],
        [pltpu.VMEM((2, D, 3 * F), bf16), sems(8)], out_spec=ANY,
    )
    route = [sds((SLOTS, T), bf16), sds((T, SLOTS), bf16), sds((T, E), f32)]

    qkv_0, (pair, g1, g2, r_sent, ids_sent, h1_b) = with_(
        all_to_all(buf, CTX), (pair, g1, g2, r_sent, ids_sent, h1_b)
    )
    ex_w = [(ANY, both(pair))]
    s0, st0, m0, s1, st1, m1, router = call(
        prep_kernel, route + route + [sds((2, D, E), bf16)],
        vm(expert_ids, ids_sent, router_weight, r_sent), flops=1e7,
    )
    buf, qkv_0, pos_all = call(
        functools.partial(attend_kernel, 0), [o_shape, qkv_saved, sds((SEQ, 1), f32)], pin(qkv_0), flops=4e8
    )
    o_in, (s0, st0, m0, s1, st1, m1, router) = with_(
        all_to_all(buf, CTX), (s0, st0, m0, s1, st1, m1, router)
    )
    q_sent, kv_sent = swap(tied(query_weight, o_in)), swap(tied(key_value_matrix, o_in))
    cos_all, sin_all = call(table_kernel, [sds((SEQ, 128), f32)] * 2, vm(pos_all))

    def middle(layer, o_in, x, s_l, m_l, *h1):
        return call(
            functools.partial(mid_kernel, layer),
            [row_full, row_low, gates_shape, sds((T, 2 * D), bf16), rows_shape],
            pin(o_in) + vm(x) + [(ANY, wo_all)] + vm(g2, router, s_l, m_l, *h1), [w_dd, sems(1)], flops=2e8,
        )

    row_block = sds((ROWS_OF, D), bf16)
    narrow = sds((ROWS_OF, D + 3 * F), bf16)

    def experts_forward(layer, rows):
        return call(
            functools.partial(expert_forward_kernel, layer),
            [rows_shape, sds((2, ROWS_OF, 2 * F), f32), row_block, row_block],
            pin(rows) + ex_w, ex_scratch, flops=2e9,
        )

    def experts_back(layer, rows, gu):
        return call(
            functools.partial(expert_back_kernel, layer), [rows_shape, narrow, narrow],
            pin(rows) + [(ANY, gu)] + ex_w,
            [ex_scratch[0], pltpu.VMEM((2, ROWS_OF, 2 * F), f32), sems(4)], flops=2e9,
        )

    def expert_grad(x_keep, x_got, keep, send):
        return call(
            expert_grad_kernel, [sds((D, 3 * F), bf16)], vm(x_keep) + pin(x_got) + vm(keep) + pin(swap(send)), flops=2e9
        )[0]

    mid_0, h2_0, gates_0, pair_0, buf = middle(0, o_in, tokens, s0, m0, h1_a, h1_b)
    x_rows, (cos_all, sin_all, q_sent, kv_sent) = with_(
        all_to_all(buf, GROUP), (cos_all, sin_all, q_sent, kv_sent)
    )
    qkv_w = [(ANY, v) for v in (query_weight, q_sent, key_value_matrix, kv_sent)]
    buf, gu_0, x_keep_0, x_send = experts_forward(0, x_rows)
    row_0 = gather(pair_0, "x")
    y_0, (row_0,) = with_(all_to_all(buf, GROUP), (row_0,))
    all_0 = gather(row_0, "y")
    x_got_0 = swap(x_send)

    out_0, h1_1, y_0, buf = call(
        next_kernel, [row_low, row_low, rows_saved, qkv_shape],
        pin(y_0) + vm(mid_0, gates_0, st0, cos, sin, g1) + qkv_w,
        [w_dd, w_dd, sems(2)], flops=5e8,
    )
    qkv_1 = all_to_all(buf, CTX)
    buf, qkv_1 = call(
        functools.partial(attend_kernel, 1), [o_shape, qkv_saved], pin(qkv_1) + vm(pos_all), flops=4e8
    )
    mid_1, h2_1, gates_1, pair_1, buf = middle(1, all_to_all(buf, CTX), out_0, s1, m1, h1_1)

    (dy_buf,) = call(send_back_kernel, [rows_shape], vm(gates_1, s1, cotangent), flops=2e8)
    x_rows, (dy_buf, pair_1, all_0) = with_(all_to_all(buf, GROUP), (dy_buf, pair_1, all_0))
    row_1 = gather(pair_1, "x")
    dy_rows = all_to_all(dy_buf, GROUP)
    buf, gu_1, x_keep, x_send = experts_forward(1, x_rows)
    dy_rows, (buf, gu_1) = with_(dy_rows, (buf, gu_1))
    y_1 = all_to_all(buf, GROUP)
    x_got = swap(x_send)
    buf, keep, send = experts_back(1, dy_rows, gu_1)
    y_1, (buf, row_1) = with_(y_1, (buf, row_1))
    all_1 = gather(row_1, "y")
    dx_1 = all_to_all(buf, GROUP)
    out_keep, out_send, dlog_1, dh2 = call(
        functools.partial(route_back_kernel, 1), [row_low, row_low, log_shape, row_full],
        pin(y_1) + vm(gates_1, st1, router, cotangent, mid_1, out_0), flops=5e8,
    )
    part = expert_grad(x_keep, x_got, keep, send)
    dx_1, (part, dh2) = with_(dx_1, (part, dh2))

    def sum_y(part):
        return lax.psum_scatter(part, "y", scatter_dimension=0, tiled=True)

    def turn(layer, dx, st, dh2, mid, g):
        return call(
            functools.partial(turn_kernel, layer), [row_full, row_low, qkv_half],
            pin(dx) + vm(st, dh2, mid, g2, g) + [(ANY, wo_all)], [w_dd, sems(1)], flops=5e8,
        )

    def attend_back(qkv, do):
        return call(
            attend_back_kernel, [back_shape, back_saved, o_saved], vm(qkv) + pin(do) + vm(pos_all), kv_scratch, flops=1e9
        )

    def heads(layer, back, da, pairs, h2, dlog, dhn2, *other):
        return call(
            functools.partial(head_grad_kernel, layer),
            [sds((D, WIDE), bf16) if layer else pinned((D, 2 * WIDE), bf16)],
            vm(back, da, cos_all, sin_all, pairs, h2, dlog, dhn2, *other), flops=8e8,
        )[0]

    def expert_rows(rows):
        return call(expert_rows_kernel, [sds((T, 3 * F), bf16)] * 4, vm(rows))

    def placed(keep, send):
        return call(place_kernel, [sds((1, 2, 1, T, D), keep.dtype)], vm(keep) + pin(swap(send)))[0]

    dmid_1, dhn2_1, buf = turn(1, dx_1, st1, dh2, mid_1, cotangent)
    buf, back_1, da_1 = attend_back(qkv_1, all_to_all(buf, CTX))
    dqkv, (part, all_1) = with_(all_to_all(buf, CTX), (part, all_1))
    ex_1 = sum_y(part)
    head_part_1 = heads(1, back_1, da_1, all_1, h2_1, dlog_1, dhn2_1)
    layer_out = placed(out_keep, out_send)
    grad_1, g_0, buf = call(
        functools.partial(back_kernel, 1), [row_full, row_low, rows_shape],
        pin(dqkv) + vm(out_0, dmid_1, cos, sin, g1) + qkv_w + vm(s0, gates_0),
        dqkv_scratch, flops=4e8,
    )

    dy_rows, (layer_out, head_part_1) = with_(all_to_all(buf, GROUP), (layer_out, head_part_1))
    buf, keep, send = experts_back(0, dy_rows, gu_0)
    dx_0 = all_to_all(buf, GROUP)
    dlog_0, dh2 = call(
        functools.partial(route_back_kernel, 0), [log_shape, row_full],
        vm(y_0, gates_0, st0, router, g_0), flops=3e8,
    )
    part = expert_grad(x_keep_0, x_got_0, keep, send)
    dx_0, (part, dh2, ex_1) = with_(dx_0, (part, dh2, ex_1))
    ex_0 = sum_y(part)
    ex_1_sent = round_trip(expert_rows(ex_1), "x")
    dmid_0, dhn2_0, buf = turn(0, dx_0, st0, dh2, mid_0, g_0)
    do_in = all_to_all(buf, CTX)
    buf, back_0, da_0 = attend_back(qkv_0, do_in)
    buf, ex_1 = with_(buf, ex_1_sent)
    dqkv = all_to_all(buf, CTX)
    rows_0 = expert_rows(ex_0)
    head_part = heads(0, back_0, da_0, all_0, h2_0, dlog_0, dhn2_0, head_part_1)
    full = all_to_all(head_part.reshape(64, 16, 2 * WIDE), ALL)
    grad_keep, grad_send = call(
        functools.partial(back_kernel, 0), [row_full, row_full],
        pin(tied(dqkv, *rows_0)) + vm(tokens, dmid_0, cos, sin, g1) + qkv_w + vm(grad_1), dqkv_scratch, flops=3e8,
    )

    ex_0 = round_trip(rows_0, "x")
    input_grad = placed(grad_keep, grad_send)
    sums = sds((16, 3 * D + 128), f32)
    full, (input_grad,) = with_(full, (input_grad,))
    keep, send = call(halves_kernel, [sums, sums], pin(full))
    (*ex_0, keep, send) = lax.optimization_barrier((*ex_0, keep, send))
    four = sds((4, T, 3 * F), bf16)
    ex_keep, ex_send = call(expert_sort_kernel, [four, four], vm(ex_0[0]) + pin(*ex_0[1:]) + vm(*ex_1), lazy=False)
    ex_in, ex_out = call(
        expert_final_kernel, [sds((1, 8, T, 2 * F), f32), sds((1, 8, T, F), f32)],
        vm(ex_keep) + pin(swap(ex_send)),
    )
    mat = sds((1, 16, D), f32)
    row = sds((1, 16), f32)
    grad_q, grad_kv, grad_o, router_grad, first_grad, second_grad = call(
        final_kernel, [mat, mat, mat, sds((1, 16, E), f32), row, row],
        vm(keep) + pin(swap(send)) + [(ANY, query_weight), (ANY, key_value_matrix)] + vm(first_gain),
        [pltpu.VMEM((16, D), bf16), pltpu.VMEM((16, D), bf16), sems(2)],
    )
    return (
        layer_out, input_grad, first_grad, grad_q, grad_kv, grad_o, second_grad, router_grad, ex_in, ex_out,
    )


def solution(mesh):
    grid = Mesh(mesh.devices.reshape(2, 4, 4, 4), ("section", "y", "x", "expert"))
    ctx = ("y", "x")
    every = ("y", "x", "expert")
    placed = (
        P(None, "expert", ctx, None),
        P(None, "expert", ctx),
        P("section", None, "expert", ctx, None),
        P(None, "expert", ctx, None),
        P("section", None),
        P("section", None, None),
        P("section", None, None),
        P("section", None, None),
        P("section", None),
        P("section", None, None),
        P("section", "expert", None, None),
        P("section", "expert", None, None),
    )
    return jax.shard_map(
        local,
        mesh=grid,
        in_specs=placed,
        out_specs=(
            P("section", None, "expert", ctx, None),
            P("section", None, "expert", ctx, None),
            P("section", every),
            P("section", every, None),
            P("section", every, None),
            P("section", every, None),
            P("section", every),
            P("section", every, None),
            P("section", "expert", ctx, None),
            P("section", "expert", ctx, None),
        ),
        check_vma=False,
    )
```

```python
import functools
import math

import jax
import jax.numpy as jnp
from jax import lax
from jax.experimental import pallas as pl
from jax.experimental.pallas import tpu as pltpu
from jax.sharding import Mesh
from jax.sharding import PartitionSpec as P

T = 64
D = 1024
HW = 64
WIDE = 5 * HW
NQ = 16
NK = 8
F = 512
E = 32
CAP = 17
MAIN = E * 16
SLOTS = E * CAP
GROUP_SIZE = 16
ROWS_OF = GROUP_SIZE * CAP
N_CTX = 16
SEQ = N_CTX * T

eps = 1e-06
rope_base = 10000.0
masked = -1e30
f32 = jnp.float32
bf16 = jnp.bfloat16

VMEM = pl.BlockSpec(memory_space=pltpu.VMEM)
SMEM = pl.BlockSpec(memory_space=pltpu.SMEM)
ANY = pl.BlockSpec(memory_space=pl.ANY)
PIN = "pinned"
GROUP = ("x", "expert")
CTX = ("y", "x")
ALL = ("y", "x", "expert")


def sds(shape, dtype):
    return jax.ShapeDtypeStruct(shape, dtype)


def pinned(shape, dtype):
    return pltpu.VMEM(shape, dtype)


class Later:
    def __init__(self, source, place, sem):
        self.place = place
        self.copy = pltpu.make_async_copy(source, place, sem)
        self.copy.start()

    def wait(self):
        if self.copy is not None:
            self.copy.wait()
            self.copy = None

    def __getitem__(self, index):
        self.wait()
        return self.place[index]


def call(body, outs, ins, scratch=(), flops=0, limit=36, out_spec=VMEM, lazy=True):
    late = [i for i, (k, _) in enumerate(ins) if k is VMEM]
    count, own = len(ins) + len(outs), len(scratch)

    def kernel(*refs):
        places, sems = refs[count + own : -1], refs[-1]
        args = list(refs[: len(ins)])
        for n, i in enumerate(late):
            args[i] = Later(args[i], places[n], sems.at[n])
        moving = [args[i] for i in late]
        if not lazy:
            for v in moving:
                v.wait()
        body(*args, *refs[len(ins) : count + own])
        for v in moving:
            v.wait()

    place = lambda k, a: a if k is SMEM else pltpu.with_memory_space_constraint(a, pltpu.VMEM if k is PIN else pltpu.HBM)
    outs = [o if isinstance(o, jax.ShapeDtypeStruct) is False else pltpu.HBM(o.shape, o.dtype) for o in outs]
    read = sum(a.size * a.dtype.itemsize for k, a in ins if k is VMEM)
    written = sum(math.prod(o.shape) * jnp.dtype(o.dtype).itemsize for o in outs)
    return pl.pallas_call(
        kernel,
        out_shape=list(outs),
        in_specs=[VMEM if k is PIN else ANY for k, _ in ins],
        out_specs=[out_spec] * len(outs),
        scratch_shapes=[
            *scratch,
            *[pltpu.VMEM(ins[i][1].shape, ins[i][1].dtype) for i in late],
            pltpu.SemaphoreType.DMA((max(1, len(late)),)),
        ],
        compiler_params=pltpu.CompilerParams(vmem_limit_bytes=limit * 1024 * 1024),
        cost_estimate=pl.CostEstimate(
            flops=int(flops), bytes_accessed=int(read + written), transcendentals=0
        ),
    )(*[place(k, a) for k, a in ins])


def dot(a, b):
    return lax.dot_general(a, b, (((1,), (0,)), ((), ())), preferred_element_type=f32)


def dot_nt(a, b):
    return lax.dot_general(a, b, (((1,), (1,)), ((), ())), preferred_element_type=f32)


def dot_tn(a, b):
    return lax.dot_general(a, b, (((0,), (0,)), ((), ())), preferred_element_type=f32)


def split(v):
    high = v.astype(bf16)
    return high, (v - high.astype(f32)).astype(bf16)


def iota(shape, dim):
    return lax.broadcasted_iota(jnp.int32, shape, dim)


def one_hot(cond):
    return jnp.where(cond, 1.0, 0.0).astype(bf16)


def expert_of(k):
    return 8 * ((k >> 1) & 3) + 2 * (k >> 3) + (k & 1)


def slot_table():
    row, col = iota((SLOTS, E), 0), iota((SLOTS, E), 1)
    return one_hot(expert_of(jnp.where(row < MAIN, row >> 4, row - MAIN)) == col)


def moved_rows(index, q, order):
    bits = q.bit_length() - 1
    if order == "block":
        return index >> (bits + 1), (index >> 1) & (q - 1), index & 1
    if order == "token":
        return (index >> 1) & 15, index >> 5, index & 1
    return index & 15, (index >> 4) & (q - 1), index >> (bits + 4)


def shuffle(q, to, order):
    n = 32 * q
    d, p, i = moved_rows(iota((n, n), 0), q, to)
    at = iota((n, n), 1)
    if order == "block":
        return one_hot(at == d * (2 * q) + p * 2 + i)
    if order == "token":
        return one_hot(at == p * 32 + d * 2 + i)
    return one_hot(at == (i * q + p) * 16 + d)


def pack(buf_ref, parts):
    n = len(parts)
    extra = []
    for k, rows in enumerate(parts):
        for c in range(8):
            piece = rows[:, c * 128 : (c + 1) * 128]
            buf_ref[:, k * 256 + c * 32 : k * 256 + (c + 1) * 32, :] = piece[:MAIN].reshape(16, 32, 128)
            extra.append(piece[MAIN:])
    moved = dot(shuffle(8 * n, "block", "token"), jnp.concatenate(extra, axis=0)).astype(bf16)
    buf_ref[:, 256 * n :, :] = moved.reshape(16, 16 * n, 128)


def unpack(buf_ref, n):
    rest = buf_ref[:, 256 * n :, :].reshape(256 * n, 128)
    moved = dot(shuffle(8 * n, "token", "block"), rest).astype(bf16)
    parts = []
    for k in range(n):
        pieces = []
        for c in range(8):
            head = buf_ref[:, k * 256 + c * 32 : k * 256 + (c + 1) * 32, :].reshape(MAIN, 128)
            at = (k * 8 + c) * E
            pieces.append(jnp.concatenate([head, moved[at : at + E]], axis=0))
        parts.append(jnp.concatenate(pieces, axis=1))
    return parts


def pack_experts(buf_ref, parts):
    n = len(parts)
    extra = []
    for i in range(2):
        for k in range(n):
            for c in range(8):
                piece = parts[k][i][:, c * 128 : (c + 1) * 128]
                at = k * 256 + c * 32 + i * 16
                buf_ref[:, at : at + 16, :] = piece[:256].reshape(16, 16, 128)
                extra.append(piece[256:])
    moved = dot(shuffle(8 * n, "block", "expert"), jnp.concatenate(extra, axis=0)).astype(bf16)
    buf_ref[:, 256 * n :, :] = moved.reshape(16, 16 * n, 128)


def unpack_experts(buf_ref, n):
    rest = buf_ref[:, 256 * n :, :].reshape(256 * n, 128)
    moved = dot(shuffle(8 * n, "expert", "block"), rest).astype(bf16)
    parts = []
    for k in range(n):
        both = []
        for i in range(2):
            pieces = []
            for c in range(8):
                at = k * 256 + c * 32 + i * 16
                head = buf_ref[:, at : at + 16, :].reshape(256, 128)
                at = (i * 8 * n + k * 8 + c) * 16
                pieces.append(jnp.concatenate([head, moved[at : at + 16]], axis=0))
            both.append(jnp.concatenate(pieces, axis=1))
        parts.append(both)
    return parts


def norm_parts(v):
    r = lax.rsqrt(jnp.mean(v * v, axis=-1, keepdims=True) + eps)
    return r, v * r


def norm_back(v, gain, dh):
    r, n = norm_parts(v)
    a = gain * dh
    return r * (a - n * jnp.mean(n * a, axis=-1, keepdims=True)), dh * n


def rotate(chunk, cos, sin):
    lane = iota(chunk.shape, 1) & 63
    other = jnp.where(lane < 32, pltpu.roll(chunk, 96, 1), pltpu.roll(chunk, 32, 1))
    return chunk * cos + other * sin


class Copy:
    def __init__(self, ref, place, sem):
        self.copy = pltpu.make_async_copy(ref, place, sem)
        self.copy.start()

    def wait(self):
        self.copy.wait()


def at_axis(axis):
    return lax.axis_index(axis)


class Chosen(Copy):
    def __init__(self, layer, own, sent, place, sem):
        self.copy = pltpu.make_async_copy(own, place, sem)
        mine = at_axis("section") == layer

        @pl.when(mine)
        def _():
            self.copy.start()

        @pl.when(jnp.logical_not(mine))
        def _():
            pltpu.make_async_copy(sent, place, sem).start()


def either(layer, own, sent):
    return jnp.where(at_axis("section") == layer, own, sent)


def prep_kernel(ids_own, ids_sent, r_own, r_sent, s0, st0, m0, s1, st1, m1, router):
    for layer in range(2):
        router[layer] = either(layer, r_own[0], r_sent[0])
    rep = slot_table()
    own = ids_own[0, at_axis("section"), 0]
    sent = ids_sent[...]
    for layer, (s_ref, st_ref, m_ref) in enumerate(((s0, st0, m0), (s1, st1, m1))):
        ids = either(layer, own, sent)
        col = iota((T, E), 1)
        member = jnp.zeros((T, E), f32)
        for k in range(8):
            member = member + jnp.where(ids[:, k : k + 1] == col, 1.0, 0.0)
        m_ref[...] = member
        low = member.astype(bf16)
        row64, col64 = iota((T, T), 0), iota((T, T), 1)
        rank = dot(one_hot(col64 < row64), low)
        rank = jnp.where(member > 0.5, rank, -1.0).astype(bf16)
        at = dot_nt(rank, rep)
        slot = iota((T, SLOTS), 1)
        place = jnp.where(slot < MAIN, slot & 15, 16).astype(f32)
        st_ref[...] = one_hot(at == place)
        eye = one_hot(iota((E, E), 0) == iota((E, E), 1))
        member_t = dot_nt(eye, low)
        rank_t = dot(member_t.astype(bf16), one_hot(row64 < col64))
        rank_t = jnp.where(member_t > 0.5, rank_t, -1.0).astype(bf16)
        at_t = dot(rep, rank_t)
        slot_t = iota((SLOTS, T), 0)
        place_t = jnp.where(slot_t < MAIN, slot_t & 15, 16).astype(f32)
        s_ref[...] = one_hot(at_t == place_t)


def pair_kernel(in_own, out_own, experts, at, sems):
    moves = []

    def move(source, place, target):
        n = len(moves)
        first = pltpu.make_async_copy(source, place, sems.at[2 * n])
        moves.append((first, pltpu.make_async_copy(place, target, sems.at[2 * n + 1])))
        first.start()

    for i in range(2):
        e = 2 * at_axis("x") + i
        move(in_own.at[0, e], at.at[i, :, : 2 * F], experts.at[0, i, :, : 2 * F])
        move(out_own.at[0, e], at.at[i, :, 2 * F :], experts.at[0, i, :, 2 * F :])
    for first, second in moves:
        first.wait()
        second.start()
    for _, second in moves:
        second.wait()


def qkv_pack(q, kv, cos, sin, pos, buf_ref):
    hi = jnp.floor(pos * (1.0 / 32.0))
    lo = pos - hi * 32.0
    lane = iota((T, 64), 1)
    where_am_i = jnp.where(lane == 0, hi, jnp.where(lane == 1, lo, 0.0)).astype(bf16)
    for pair in range(4):
        k_two = rotate(kv[:, pair * 128 : (pair + 1) * 128], cos, sin).astype(bf16)
        v_two = kv[:, 512 + pair * 128 : 512 + (pair + 1) * 128].astype(bf16)
        for g in range(2):
            k_one = k_two[:, g * 64 : (g + 1) * 64]
            v_one = v_two[:, g * 64 : (g + 1) * 64]
            group = pair * 2 + g
            q_two = rotate(q[:, group * 128 : (group + 1) * 128], cos, sin).astype(bf16)
            low_half = jnp.concatenate([v_one, where_am_i], axis=1)
            for j in range(2):
                top = jnp.concatenate([q_two[:, j * 64 : (j + 1) * 64], k_one], axis=1)
                buf_ref[2 * group + j, 0:T, :] = top
                buf_ref[2 * group + j, T : 2 * T, :] = low_half


def rotary(pos):
    rows = pos.shape[0]
    lane = iota((rows, 128), 1)
    frequency = jnp.exp((lane & 31).astype(f32) * (-2.0 * math.log(rope_base) / HW))
    angles = pos * frequency
    sin = jnp.sin(angles)
    return jnp.cos(angles), jnp.where((lane & 63) < 32, -sin, sin)


def table_kernel(pos, cos, sin):
    for start in range(0, SEQ, 256):
        at = slice(start, start + 256)
        cos[at], sin[at] = rotary(pos[at])


def first_kernel(tok, places, gain, q_own, kv_own, h1_a, h1_b, buf_a, buf_b, cos_ref, sin_ref, q_w, kv_w, sems):
    q_copy = pltpu.make_async_copy(q_own.at[0], q_w, sems.at[0])
    kv_copy = pltpu.make_async_copy(kv_own.at[0], kv_w, sems.at[1])
    q_copy.start()
    kv_copy.start()
    x = jnp.concatenate([tok[0, 0], tok[1, 0]], axis=0).astype(f32)
    h1 = (norm_parts(x)[1] * gain[...]).astype(bf16)
    h1_a[...] = h1[:T]
    h1_b[...] = h1[T:]
    eye = iota((T, T), 0) == iota((T, T), 1)
    columns = [
        jnp.sum(jnp.where(eye, places[m].astype(f32), 0.0), axis=1, keepdims=True) for m in range(2)
    ]
    pos = jnp.concatenate(columns, axis=0)
    cos, sin = rotary(pos)
    cos_ref[...] = cos
    sin_ref[...] = sin
    q_copy.wait()
    q = dot(h1, q_w[...])
    kv_copy.wait()
    kv = dot(h1, kv_w[...])
    for m, buf_ref in enumerate((buf_a, buf_b)):
        at = slice(m * T, (m + 1) * T)
        qkv_pack(q[at], kv[at], cos[at], sin[at], pos[at], buf_ref)


def attention_parts(buf):
    q = buf[:, 0:T, 0:HW].reshape(SEQ, HW)
    k = buf[:, 0:T, HW : 2 * HW].reshape(SEQ, HW)
    v = buf[:, T : 2 * T, 0:HW].reshape(SEQ, HW)
    return q, k, v


def sent_positions(buf):
    hi = buf[:, T : 2 * T, HW : HW + 1].reshape(SEQ, 1).astype(f32)
    lo = buf[:, T : 2 * T, HW + 1 : HW + 2].reshape(SEQ, 1).astype(f32)
    return hi * 32.0 + lo


def block_probs(q, k, pos, start, rows):
    keys = start + rows
    scores = dot_nt(q[start : start + rows], k[:keys]) * (HW**-0.5)
    at = (iota((rows, keys), 0) + start).astype(f32)
    key = iota((rows, keys), 1).astype(f32)
    begin = at[:, 0:1] - pos[start : start + rows]
    scores = jnp.where((key <= at) & (key >= begin), scores, masked)
    raised = jnp.exp(scores - jnp.max(scores, axis=-1, keepdims=True))
    return raised / jnp.sum(raised, axis=-1, keepdims=True)


ROWS = 256


def attend_kernel(layer, buf_ref, *refs):
    q, k, v = attention_parts(buf_ref[...])
    if layer == 0:
        out_ref, kept, pos_ref = refs
        pos = sent_positions(buf_ref[...])
        pos_ref[...] = pos
    else:
        pos_ref, out_ref, kept = refs
        pos = pos_ref[...]
    kept[...] = buf_ref[...]
    for start in range(0, SEQ, ROWS):
        probs = block_probs(q, k, pos, start, ROWS)
        o = dot(probs.astype(bf16), v[: start + ROWS]).astype(bf16)
        for b in range(ROWS // T):
            piece = o[b * T : (b + 1) * T]
            out_ref[start // T + b] = jnp.concatenate([piece[: T // 2], piece[T // 2 :]], axis=1)


def heads_in(buf_ref, o_ref):
    for g in range(8):
        a, b = buf_ref[2 * g], buf_ref[2 * g + 1]
        o_ref[0 : T // 2, g * 128 : (g + 1) * 128] = jnp.concatenate([a[:, :64], b[:, :64]], axis=1)
        o_ref[T // 2 : T, g * 128 : (g + 1) * 128] = jnp.concatenate([a[:, 64:], b[:, 64:]], axis=1)


def heads_out(do, buf_ref, start):
    for g in range(8):
        two = do[:, g * 128 : (g + 1) * 128]
        for j in range(2):
            one = two[:, j * 64 : (j + 1) * 64]
            block = jnp.concatenate([one[: T // 2], one[T // 2 :]], axis=1)
            buf_ref[2 * g + j, start : start + T // 2, :] = block


def gates_from(logits, member):
    chosen = member > 0.5
    largest = jnp.max(jnp.where(chosen, logits, masked), axis=-1, keepdims=True)
    raised = jnp.where(chosen, jnp.exp(jnp.minimum(logits - largest, 0.0)), 0.0)
    return raised / jnp.sum(raised, axis=-1, keepdims=True)


def gated_rows(gates, s, rep, g_low):
    high, low = split(gates)
    up = (s * dot_nt(rep, high).astype(bf16)).astype(bf16)
    down = (s * dot_nt(rep, low).astype(bf16)).astype(bf16)
    return (dot(up, g_low) + dot(down, g_low)).astype(bf16)


def mid_kernel(layer, *refs):
    ob, x_ref, wo_all, gain, r_ref, s_ref, m_ref = refs[:7]
    h1_refs, (mid_ref, h2_ref, gates_ref, pair_ref, buf_ref, wo, sems) = refs[7:-7], refs[-7:]
    copy = Copy(wo_all.at[layer], wo, sems.at[0])
    o_ref = pair_ref.at[:, D:]
    heads_in(ob, o_ref)
    if layer == 0:
        pair_ref[:, :D] = jnp.where(at_axis("section") == 0, h1_refs[0][...], h1_refs[1][...])
    else:
        pair_ref[:, :D] = h1_refs[0][...]
    x = (tok_row(x_ref) if layer == 0 else x_ref[...]).astype(f32)
    copy.wait()
    middle = x + dot(o_ref[...], wo[...])
    mid_ref[...] = middle
    h2 = (norm_parts(middle)[1] * gain[layer]).astype(bf16)
    h2_ref[...] = h2
    pack(buf_ref, [dot(s_ref[...], h2).astype(bf16)])
    gates_ref[...] = gates_from(dot(h2, r_ref[layer]), m_ref[...])


def send_back_kernel(gates, s_ref, cot, buf_ref):
    pack(buf_ref, [gated_rows(gates[...], s_ref[...], slot_table(), tok_row(cot))])


def tok_row(ref):
    return ref[at_axis("section"), 0]


def hidden_of(gu):
    gate, up = gu[:, :F], gu[:, F:]
    sg = jax.nn.sigmoid(gate)
    return gate, up, sg, (gate * sg * up).astype(bf16)


def sorted_out(i, keep, send, at, value):
    cols = slice(at, at + value.shape[1])

    @pl.when(at_axis("section") == i)
    def _():
        keep[:, cols] = value

    @pl.when(at_axis("section") != i)
    def _():
        send[:, cols] = value


def expert_forward_kernel(layer, buf, w_all, ybuf, gu_ref, keep, send, w, sems):
    copies = [Copy(w_all.at[layer, i], w.at[i], sems.at[i]) for i in range(2)]
    (x,) = unpack_experts(buf, 1)
    y = []
    for i in range(2):
        copies[i].wait()
        gu = dot(x[i], w[i, :, : 2 * F])
        gu_ref[i] = gu
        y.append(dot_nt(hidden_of(gu)[3], w[i, :, 2 * F :]).astype(bf16))
        sorted_out(i, keep, send, 0, x[i])
    pack_experts(ybuf, [y])


def expert_back(dy, gu, w_in, w_out):
    gate, up, sg, z = hidden_of(gu)
    dz = dot(dy, w_out)
    dgate = dz * up * (sg + gate * sg * (1.0 - sg))
    dup = dz * gate * sg
    dgu = jnp.concatenate([dgate, dup], axis=1).astype(bf16)
    return z, dgu, dot_nt(dgu, w_in).astype(bf16)


def expert_back_kernel(layer, buf, gu_all, w_all, back, keep, send, w, gu, sems):
    copies = []
    for i in range(2):
        copies.append(Copy(w_all.at[layer, i], w.at[i], sems.at[i]))
        copies.append(Copy(gu_all.at[i], gu.at[i], sems.at[2 + i]))
    (dy,) = unpack_experts(buf, 1)
    dx = []
    for i in range(2):
        copies[2 * i].wait()
        copies[2 * i + 1].wait()
        z, dgu, dx_i = expert_back(dy[i], gu[i], w[i, :, : 2 * F], w[i, :, 2 * F :])
        dx.append(dx_i)
        for at, value in ((0, dy[i]), (D, dgu), (D + 2 * F, z)):
            sorted_out(i, keep, send, at, value)
    pack_experts(back, [dx])


def expert_grad_kernel(x_keep, x_got, keep, got, out):
    x = jnp.concatenate([x_keep[...], x_got[...]], axis=0)
    dy = jnp.concatenate([keep[:, :D], got[:, :D]], axis=0)
    dgu = jnp.concatenate([keep[:, D : D + 2 * F], got[:, D : D + 2 * F]], axis=0)
    z = jnp.concatenate([keep[:, D + 2 * F : D + 3 * F], got[:, D + 2 * F : D + 3 * F]], axis=0)
    out[:, : 2 * F] = dot_tn(x, dgu).astype(bf16)
    out[:, 2 * F :] = dot_tn(dy, z).astype(bf16)


def expert_rows_kernel(rows, b0, b1, b2, b3):
    for k, b in enumerate((b0, b1, b2, b3)):
        at = pl.multiple_of(((at_axis("x") + k) & 3) * T, T)
        b[...] = rows[pl.ds(at, T), :]


def expert_sort_kernel(*refs):
    keep, send = refs[8:]
    for layer in range(2):
        for k in range(4):
            block = refs[4 * layer + k]
            place = (at_axis("x") - k) & 3

            @pl.when(at_axis("section") == layer)
            def _():
                keep[place] = block[...]

            @pl.when(at_axis("section") != layer)
            def _():
                send[place] = block[...]


def expert_final_kernel(keep, got, out_in, out_out):
    for x in range(4):
        for ref, j in ((keep, at_axis("section")), (got, 1 - at_axis("section"))):
            out_in[0, 2 * x + j] = ref[x, :, : 2 * F].astype(f32)
            out_out[0, 2 * x + j] = ref[x, :, 2 * F :].astype(f32)


def place_kernel(keep, got, out):
    out[0, at_axis("section"), 0] = keep[...]
    out[0, 1 - at_axis("section"), 0] = got[...]


def by_section(v_0, v_1, keep, send):
    keep[...] = jnp.where(at_axis("section") == 0, v_0, v_1)
    send[...] = jnp.where(at_axis("section") == 0, v_1, v_0)


def combine(middle, gates, st, rep, y):
    high, low = split(gates)
    up = (st * dot_nt(high, rep).astype(bf16)).astype(bf16)
    down = (st * dot_nt(low, rep).astype(bf16)).astype(bf16)
    return middle + (dot(up, y) + dot(down, y))


def micro_rows(ref):
    return ref[pl.ds(pl.multiple_of(at_axis("section") * T, T), T), :]


def next_kernel(
    yb, mid, gates, st, cos, sin, gain, q_own, q_sent, kv_own, kv_sent, out_ref, h1_ref, saved, buf_ref, q_w, kv_w, sems,
):
    saved[...] = yb[...]
    q_copy = Chosen(1, q_own.at[0], q_sent.at[0], q_w, sems.at[0])
    kv_copy = Chosen(1, kv_own.at[0], kv_sent.at[0], kv_w, sems.at[1])
    (y,) = unpack(yb, 1)
    out = combine(mid[...], gates[...], st[...], slot_table(), y).astype(bf16)
    out_ref[...] = out
    h1 = (norm_parts(out.astype(f32))[1] * gain[1]).astype(bf16)
    h1_ref[...] = h1
    q_copy.wait()
    q = dot(h1, q_w[...])
    kv_copy.wait()
    kv = dot(h1, kv_w[...])
    qkv_pack(q, kv, micro_rows(cos), micro_rows(sin), jnp.zeros((T, 1), f32), buf_ref)


def route_back_kernel(layer, *refs):
    yb, gates_ref, st_ref, r_ref, g_ref = refs[:5]
    dlog_ref, dh2_ref = refs[-2:]
    rep, st, gates = slot_table(), st_ref[...], gates_ref[...]
    (y,) = unpack(yb, 1)
    if layer == 1:
        mid, out_0, keep, send = refs[5:9]
        g_low = tok_row(g_ref)
        by_section(out_0[...], combine(mid[...], gates, st, rep, y).astype(bf16), keep, send)
    else:
        g_low = g_ref[...]
    d_slot = dot_nt(g_low, y) * st.astype(f32)
    high, low = split(d_slot)
    d_gates = dot(high, rep) + dot(low, rep)
    d_chosen = gates * (d_gates - jnp.sum(gates * d_gates, axis=-1, keepdims=True))
    d_log = d_chosen.astype(bf16)
    dlog_ref[...] = d_log
    dh2_ref[...] = dot_nt(d_log, r_ref[layer])


def turn_kernel(layer, *refs):
    dxb, st, dh2, mid, gain, g_ref, wo_all, dmid_ref, dhn_ref, dobuf, wo, sems = refs
    copy = Copy(wo_all.at[layer], wo, sems.at[0])
    (dx,) = unpack(dxb, 1)
    g_low = tok_row(g_ref) if layer == 1 else g_ref[...]
    d_h2 = dot(st[...], dx) + dh2[...]
    d_v, d_hn = norm_back(mid[...], gain[layer], d_h2)
    d_mid = g_low.astype(f32) + d_v
    d_a = d_mid.astype(bf16)
    heads_out(d_a, dobuf, T // 2)
    copy.wait()
    heads_out(dot_nt(d_a, wo[...]).astype(bf16), dobuf, 0)
    dmid_ref[...] = d_mid
    dhn_ref[...] = d_hn.astype(bf16)


def attend_back_kernel(buf_ref, dobuf, pos_ref, out_ref, saved, da_saved, dk_ref, dv_ref):
    q, k, v = attention_parts(buf_ref[...])
    pos = pos_ref[...]
    da_saved[...] = dobuf[:, T // 2 :, :]
    packed = dobuf[:, : T // 2, :]
    do = halves(packed)
    scale = HW**-0.5
    dq = []
    for start in reversed(range(0, SEQ, ROWS)):
        keys = start + ROWS
        probs = block_probs(q, k, pos, start, ROWS)
        do_rows = do[start:keys]
        d_probs = dot_nt(do_rows, v[:keys])
        inner = jnp.sum(probs * d_probs, axis=-1, keepdims=True)
        d_scores = (probs * (d_probs - inner)).astype(bf16)
        dq.append((dot(d_scores, k[:keys]) * scale).astype(bf16))
        d_k = dot_tn(d_scores, q[start:keys]) * scale
        d_v = dot_tn(probs.astype(bf16), do_rows)
        if keys == SEQ:
            dk_ref[...] = d_k
            dv_ref[...] = d_v
        else:
            dk_ref[0:keys] = dk_ref[0:keys] + d_k
            dv_ref[0:keys] = dv_ref[0:keys] + d_v
    d_q = jnp.concatenate(dq[::-1], axis=0)
    d_k = dk_ref[...].astype(bf16)
    d_v = dv_ref[...].astype(bf16)
    out_ref[:, 0:T, :] = jnp.concatenate([d_q, d_k], axis=1).reshape(N_CTX, T, 128)
    d_v = d_v.reshape(N_CTX, T, HW)
    out_ref[:, T:, :] = jnp.concatenate([d_v[:, : T // 2], d_v[:, T // 2 :]], axis=2)
    saved[...] = out_ref[...]


def back_kernel(layer, *refs):
    refs = list(refs)
    buf, x_ref, dmid, cos_ref, sin_ref, gain, q_own, q_sent, kv_own, kv_sent = refs[:10]
    refs = refs[10:]
    if layer == 1:
        s_ref, gates_ref = refs[:2]
        refs = refs[2:]
    if layer == 0:
        grad_1 = refs.pop(0)
        keep, send = refs[:2]
        refs = refs[2:]
    else:
        grad_ref = refs.pop(0)
    if layer == 1:
        g_ref, dybuf = refs[:2]
        refs = refs[2:]
    q_w, kv_w, dq_ref, dkv_ref, sems = refs
    q_copy = Chosen(layer, q_own.at[0], q_sent.at[0], q_w, sems.at[0])
    kv_copy = Chosen(layer, kv_own.at[0], kv_sent.at[0], kv_w, sems.at[1])
    cos, sin = micro_rows(cos_ref), -micro_rows(sin_ref)
    half = T // 2
    k_parts, v_parts = [], []
    for g in range(8):
        a, b = buf[2 * g], buf[2 * g + 1]
        q_two = jnp.concatenate([a[:T, :64], b[:T, :64]], axis=1).astype(f32)
        dq_ref[:, g * 128 : (g + 1) * 128] = rotate(q_two, cos, sin).astype(bf16)
        k_parts.append(a[:T, 64:].astype(f32) + b[:T, 64:].astype(f32))
        v_sum = a[T:].astype(f32) + b[T:].astype(f32)
        v_parts.append(jnp.concatenate([v_sum[:, :64], v_sum[:, 64:]], axis=0))
    for p in range(4):
        k_two = jnp.concatenate([k_parts[2 * p], k_parts[2 * p + 1]], axis=1)
        v_two = jnp.concatenate([v_parts[2 * p], v_parts[2 * p + 1]], axis=1)
        dkv_ref[:, p * 128 : (p + 1) * 128] = rotate(k_two, cos, sin).astype(bf16)
        dkv_ref[:, 512 + p * 128 : 512 + (p + 1) * 128] = v_two.astype(bf16)
    q_copy.wait()
    kv_copy.wait()
    d_h1 = dot_nt(dq_ref[...], q_w[...]) + dot_nt(dkv_ref[...], kv_w[...])
    x = (tok_row(x_ref) if layer == 0 else x_ref[...]).astype(f32)
    d_x, _ = norm_back(x, gain[layer], d_h1)
    grad = dmid[...] + d_x
    if layer == 0:
        by_section(grad, grad_1[...], keep, send)
    else:
        grad_ref[...] = grad
        g_low = grad.astype(bf16)
        g_ref[...] = g_low
        pack(dybuf, [gated_rows(gates_ref[...], s_ref[...], slot_table(), g_low)])


def head_grad_kernel(layer, back, da, cos_ref, sin_ref, pairs, h2, dlog, dhn2, *refs):
    out = refs[-1]
    if layer == 0:
        out[:, WIDE:] = refs[0][...]
    cos, sin = cos_ref[...], -sin_ref[...]
    both = rotate(back[:, :T, :].reshape(SEQ, 2 * HW).astype(f32), cos, sin).astype(bf16)
    lane = iota((T, HW), 1)
    logs = jnp.concatenate([dlog[...], jnp.zeros((T, HW - E), bf16)], axis=1)
    extra = dot_tn(logs, h2[...]) + dot_tn(one_hot(lane == E), dhn2[...])
    h1_all = pairs[:, :D]
    out[:, : 2 * HW] = dot_tn(both, h1_all).T.astype(bf16)
    rest = [dot_tn(halves(back[:, T:, :]), h1_all), dot_tn(halves(da[...]), pairs[:, D:]), extra]
    out[:, 2 * HW : WIDE] = jnp.concatenate(rest, axis=0).T.astype(bf16)


def halves(packed):
    return jnp.concatenate([packed[:, :, :HW], packed[:, :, HW:]], axis=1).reshape(SEQ, HW)


def head_sums(got, layer):
    v = []
    cols = slice(WIDE * layer, WIDE * (layer + 1))
    for c in range(N_CTX):
        v.append(sum(got[4 * c + k, :, cols].astype(f32) for k in range(1, 4)) + got[4 * c, :, cols].astype(f32))
    pair = [v[2 * g] + v[2 * g + 1] for g in range(NK)]
    parts = []
    for blocks, at in ((v, 3 * HW), (v, 0), (pair, HW), (pair, 2 * HW)):
        for a, b in zip(blocks[::2], blocks[1::2]):
            parts.append(jnp.concatenate([a[:, at : at + HW], b[:, at : at + HW]], axis=1))
    total = sum(pair[1:]) + pair[0]
    parts.append(total[:, 3 * HW :])
    return jnp.concatenate(parts, axis=1)


def halves_kernel(got, keep, send):
    by_section(head_sums(got, 0), head_sums(got, 1), keep, send)


def final_kernel(keep, got, q_own, kv_own, gain, gq, gkv, go, gr, g1, g2, q_rows, kv_rows, sems):
    first = 16 * at_axis(ALL)
    rows = pl.ds(pl.multiple_of(first, 16), 16)
    copies = [Copy(q_own.at[0, rows], q_rows, sems.at[0]), Copy(kv_own.at[0, rows], kv_rows, sems.at[1])]
    mine = keep[...] + got[...]
    grad_q, grad_kv, rest = mine[:, D : 2 * D], mine[:, 2 * D : 3 * D], mine[:, 3 * D :]
    go[0] = mine[:, :D]
    gq[0] = grad_q
    gkv[0] = grad_kv
    gr[0] = rest[:, HW : HW + E]
    eye = iota((16, 16), 0) == iota((16, 16), 1)
    as_row = lambda column: jnp.sum(jnp.where(eye, column, 0.0), axis=0, keepdims=True)
    g2[...] = as_row(rest[:, HW + E : HW + E + 1])
    here = iota((16, D), 1) == iota((16, D), 0) + first
    gains = jnp.sum(jnp.where(here, gain[...], 0.0), axis=1, keepdims=True)
    for copy in copies:
        copy.wait()
    both = grad_q * q_rows[...].astype(f32) + grad_kv * kv_rows[...].astype(f32)
    g1[...] = as_row(jnp.sum(both, axis=-1, keepdims=True) / gains)


def swap(v):
    return lax.ppermute(v, "section", [(0, 1), (1, 0)])


def either_order(first, mine, other):
    return jnp.where(first, mine, other), jnp.where(first, other, mine)


def all_to_all(v, axes):
    return lax.all_to_all(v, axes, 0, 0, tiled=True)


def local(
    tokens, positions, expert_ids, cotangent, first_gain, query_weight, key_value_matrix,
    output_weight, second_gain, router_weight, expert_in, expert_out,
):
    s, y_at, x_at, z_at = (lax.axis_index(a) for a in ("section", "y", "x", "expert"))
    first = s == 0
    vm = lambda *arrays: [(VMEM, a) for a in arrays]
    pin = lambda *arrays: [(PIN, a) for a in arrays]
    sems = lambda n: pltpu.SemaphoreType.DMA((n,))
    tied = lambda v, *after: lax.optimization_barrier((v,) + after)[0]

    def with_(v, others):
        v, *others = lax.optimization_barrier((v, *others))
        return v, others

    def gather(v, axis):
        return lax.all_gather(v, axis, axis=0, tiled=True)

    def both(v):
        return lax.all_gather(v, "section", axis=0, tiled=True)

    def round_trip(blocks, axis):
        route = lambda k: [(i, (i + k) % 4) for i in range(4)]
        return [blocks[0]] + [lax.ppermute(blocks[k], axis, route(k)) for k in range(1, 4)]

    w_dd = pltpu.VMEM((D, D), bf16)
    ex_scratch = [pltpu.VMEM((2, D, 3 * F), bf16), sems(2)]
    qkv_shape = pinned((N_CTX, 2 * T, 128), bf16)
    o_shape = pinned((N_CTX, T // 2, 128), bf16)
    qkv_half = pinned((N_CTX, T, 128), bf16)
    back_shape = pinned((N_CTX, T + T // 2, 128), bf16)
    rows_shape = pinned((GROUP_SIZE, 272, 128), bf16)
    row_low, row_full = sds((T, D), bf16), sds((T, D), f32)
    gates_shape, log_shape = sds((T, E), f32), sds((T, E), bf16)
    o_saved, back_saved = sds(o_shape.shape, bf16), sds(back_shape.shape, bf16)
    qkv_saved, rows_saved = sds(qkv_shape.shape, bf16), sds(rows_shape.shape, bf16)
    kv_scratch = [pltpu.VMEM((SEQ, HW), f32), pltpu.VMEM((SEQ, HW), f32)]
    dqkv_scratch = [w_dd, w_dd, pltpu.VMEM((T, D), bf16), pltpu.VMEM((T, D), bf16), sems(2)]

    table = sds((2 * T, 128), f32)
    h1_a, h1_b, buf_a, buf_b, cos, sin = call(
        first_kernel, [row_low, row_low, qkv_shape, qkv_shape, table, table],
        vm(tokens, positions, first_gain) + [(ANY, query_weight), (ANY, key_value_matrix)],
        [w_dd, w_dd, sems(2)], flops=6e8,
    )
    down = lambda v: lax.ppermute(v, "section", [(0, 1)])
    buf = jnp.where(first, buf_a, down(buf_b))
    h1_b = down(h1_b)

    late = lambda v: tied(v, buf_a)
    wo_all = both(late(output_weight))
    g1, g2 = (jnp.stack(either_order(first, v, swap(late(v)))) for v in (first_gain, second_gain))
    r_sent = swap(late(router_weight))
    ids_sent = swap(late(lax.dynamic_slice(expert_ids, (0, 1 - s, 0, 0, 0), (1, 1, 1, T, 8)))).reshape(T, 8)
    (pair,) = call(
        pair_kernel, [sds((1, 2, D, 3 * F), bf16)], [(ANY, tied(v, buf)) for v in (expert_in, expert_out)],
        [pltpu.VMEM((2, D, 3 * F), bf16), sems(8)], out_spec=ANY,
    )
    route = [sds((SLOTS, T), bf16), sds((T, SLOTS), bf16), sds((T, E), f32)]

    qkv_0, (pair, g1, g2, r_sent, ids_sent, h1_b) = with_(
        all_to_all(buf, CTX), (pair, g1, g2, r_sent, ids_sent, h1_b)
    )
    ex_w = [(ANY, both(pair))]
    s0, st0, m0, s1, st1, m1, router = call(
        prep_kernel, route + route + [sds((2, D, E), bf16)],
        vm(expert_ids, ids_sent, router_weight, r_sent), flops=1e7,
    )
    buf, qkv_0, pos_all = call(
        functools.partial(attend_kernel, 0), [o_shape, qkv_saved, sds((SEQ, 1), f32)], pin(qkv_0), flops=4e8
    )
    o_in, (s0, st0, m0, s1, st1, m1, router) = with_(
        all_to_all(buf, CTX), (s0, st0, m0, s1, st1, m1, router)
    )
    q_sent, kv_sent = swap(tied(query_weight, o_in)), swap(tied(key_value_matrix, o_in))
    cos_all, sin_all = call(table_kernel, [sds((SEQ, 128), f32)] * 2, vm(pos_all))

    def middle(layer, o_in, x, s_l, m_l, *h1):
        return call(
            functools.partial(mid_kernel, layer),
            [row_full, row_low, gates_shape, sds((T, 2 * D), bf16), rows_shape],
            pin(o_in) + vm(x) + [(ANY, wo_all)] + vm(g2, router, s_l, m_l, *h1), [w_dd, sems(1)], flops=2e8,
        )

    row_block = sds((ROWS_OF, D), bf16)
    narrow = sds((ROWS_OF, D + 3 * F), bf16)

    def experts_forward(layer, rows):
        return call(
            functools.partial(expert_forward_kernel, layer),
            [rows_shape, sds((2, ROWS_OF, 2 * F), f32), row_block, row_block],
            pin(rows) + ex_w, ex_scratch, flops=2e9,
        )

    def experts_back(layer, rows, gu):
        return call(
            functools.partial(expert_back_kernel, layer), [rows_shape, narrow, narrow],
            pin(rows) + [(ANY, gu)] + ex_w,
            [ex_scratch[0], pltpu.VMEM((2, ROWS_OF, 2 * F), f32), sems(4)], flops=2e9,
        )

    def expert_grad(x_keep, x_got, keep, send):
        return call(
            expert_grad_kernel, [sds((D, 3 * F), bf16)], vm(x_keep) + pin(x_got) + vm(keep) + pin(swap(send)), flops=2e9
        )[0]

    mid_0, h2_0, gates_0, pair_0, buf = middle(0, o_in, tokens, s0, m0, h1_a, h1_b)
    x_rows, (cos_all, sin_all, q_sent, kv_sent) = with_(
        all_to_all(buf, GROUP), (cos_all, sin_all, q_sent, kv_sent)
    )
    qkv_w = [(ANY, v) for v in (query_weight, q_sent, key_value_matrix, kv_sent)]
    buf, gu_0, x_keep_0, x_send = experts_forward(0, x_rows)
    row_0 = gather(pair_0, "x")
    y_0, (row_0,) = with_(all_to_all(buf, GROUP), (row_0,))
    all_0 = gather(row_0, "y")
    x_send_0 = x_send

    out_0, h1_1, y_0, buf = call(
        next_kernel, [row_low, row_low, rows_saved, qkv_shape],
        pin(y_0) + vm(mid_0, gates_0, st0, cos, sin, g1) + qkv_w,
        [w_dd, w_dd, sems(2)], flops=5e8,
    )
    qkv_1 = all_to_all(buf, CTX)
    x_got_0 = swap(tied(x_send_0, qkv_1))
    buf, qkv_1 = call(
        functools.partial(attend_kernel, 1), [o_shape, qkv_saved], pin(qkv_1) + vm(pos_all), flops=4e8
    )
    mid_1, h2_1, gates_1, pair_1, buf = middle(1, all_to_all(buf, CTX), out_0, s1, m1, h1_1)

    (dy_buf,) = call(send_back_kernel, [rows_shape], vm(gates_1, s1, cotangent), flops=2e8)
    x_rows, (dy_buf, pair_1, all_0) = with_(all_to_all(buf, GROUP), (dy_buf, pair_1, all_0))
    row_1 = gather(pair_1, "x")
    dy_rows = all_to_all(dy_buf, GROUP)
    buf, gu_1, x_keep, x_send = experts_forward(1, x_rows)
    dy_rows, (buf, gu_1) = with_(dy_rows, (buf, gu_1))
    y_1 = all_to_all(buf, GROUP)
    buf, keep, send = experts_back(1, dy_rows, gu_1)
    y_1, (buf, row_1) = with_(y_1, (buf, row_1))
    all_1 = gather(row_1, "y")
    dx_1 = all_to_all(buf, GROUP)
    out_keep, out_send, dlog_1, dh2 = call(
        functools.partial(route_back_kernel, 1), [row_low, row_low, log_shape, row_full],
        pin(y_1) + vm(gates_1, st1, router, cotangent, mid_1, out_0), flops=5e8,
    )
    dx_1, (dh2, x_send, send) = with_(dx_1, (dh2, x_send, send))
    part = expert_grad(x_keep, swap(x_send), keep, send)

    def sum_y(part):
        return lax.psum_scatter(part, "y", scatter_dimension=0, tiled=True)

    def turn(layer, dx, st, dh2, mid, g):
        return call(
            functools.partial(turn_kernel, layer), [row_full, row_low, qkv_half],
            pin(dx) + vm(st, dh2, mid, g2, g) + [(ANY, wo_all)], [w_dd, sems(1)], flops=5e8,
        )

    def attend_back(qkv, do):
        return call(
            attend_back_kernel, [back_shape, back_saved, o_saved], vm(qkv) + pin(do) + vm(pos_all), kv_scratch, flops=1e9
        )

    def heads(layer, back, da, pairs, h2, dlog, dhn2, *other):
        return call(
            functools.partial(head_grad_kernel, layer),
            [sds((D, WIDE), bf16) if layer else pinned((D, 2 * WIDE), bf16)],
            vm(back, da, cos_all, sin_all, pairs, h2, dlog, dhn2, *other), flops=8e8,
        )[0]

    def expert_rows(rows):
        return call(expert_rows_kernel, [sds((T, 3 * F), bf16)] * 4, vm(rows))

    def placed(keep, send):
        return call(place_kernel, [sds((1, 2, 1, T, D), keep.dtype)], vm(keep) + pin(swap(send)))[0]

    dmid_1, dhn2_1, buf = turn(1, dx_1, st1, dh2, mid_1, cotangent)
    do_in, (part,) = with_(all_to_all(buf, CTX), (part,))
    buf, back_1, da_1 = attend_back(qkv_1, do_in)
    dqkv, (part, all_1) = with_(all_to_all(buf, CTX), (part, all_1))
    ex_1 = sum_y(part)
    head_part_1 = heads(1, back_1, da_1, all_1, h2_1, dlog_1, dhn2_1)
    layer_out = placed(out_keep, out_send)
    grad_1, g_0, buf = call(
        functools.partial(back_kernel, 1), [row_full, row_low, rows_shape],
        pin(dqkv) + vm(out_0, dmid_1, cos, sin, g1) + qkv_w + vm(s0, gates_0),
        dqkv_scratch, flops=4e8,
    )

    dy_rows, (layer_out, head_part_1) = with_(all_to_all(buf, GROUP), (layer_out, head_part_1))
    buf, keep, send = experts_back(0, dy_rows, gu_0)
    dx_0 = all_to_all(buf, GROUP)
    dlog_0, dh2 = call(
        functools.partial(route_back_kernel, 0), [log_shape, row_full],
        vm(y_0, gates_0, st0, router, g_0), flops=3e8,
    )
    part = expert_grad(x_keep_0, x_got_0, keep, send)
    dx_0, (part, dh2, ex_1) = with_(dx_0, (part, dh2, ex_1))
    ex_0 = sum_y(part)
    ex_1_sent = round_trip(expert_rows(ex_1), "x")
    dmid_0, dhn2_0, buf = turn(0, dx_0, st0, dh2, mid_0, g_0)
    do_in = all_to_all(buf, CTX)
    buf, back_0, da_0 = attend_back(qkv_0, do_in)
    buf, ex_1 = with_(buf, ex_1_sent)
    dqkv = all_to_all(buf, CTX)
    rows_0 = expert_rows(ex_0)
    head_part = heads(0, back_0, da_0, all_0, h2_0, dlog_0, dhn2_0, head_part_1)
    full = all_to_all(head_part.reshape(64, 16, 2 * WIDE), ALL)
    grad_keep, grad_send = call(
        functools.partial(back_kernel, 0), [row_full, row_full],
        pin(tied(dqkv, *rows_0)) + vm(tokens, dmid_0, cos, sin, g1) + qkv_w + vm(grad_1), dqkv_scratch, flops=3e8,
    )

    ex_0 = round_trip(rows_0, "x")
    input_grad = placed(grad_keep, grad_send)
    sums = sds((16, 3 * D + 128), f32)
    full, (input_grad,) = with_(full, (input_grad,))
    keep, send = call(halves_kernel, [sums, sums], pin(full))
    (*ex_0, keep, send) = lax.optimization_barrier((*ex_0, keep, send))
    four = sds((4, T, 3 * F), bf16)
    ex_keep, ex_send = call(expert_sort_kernel, [four, four], vm(ex_0[0]) + pin(*ex_0[1:]) + vm(*ex_1), lazy=False)
    ex_in, ex_out = call(
        expert_final_kernel, [sds((1, 8, T, 2 * F), f32), sds((1, 8, T, F), f32)],
        vm(ex_keep) + pin(swap(ex_send)),
    )
    mat = sds((1, 16, D), f32)
    row = sds((1, 16), f32)
    grad_q, grad_kv, grad_o, router_grad, first_grad, second_grad = call(
        final_kernel, [mat, mat, mat, sds((1, 16, E), f32), row, row],
        vm(keep) + pin(swap(send)) + [(ANY, query_weight), (ANY, key_value_matrix)] + vm(first_gain),
        [pltpu.VMEM((16, D), bf16), pltpu.VMEM((16, D), bf16), sems(2)],
    )
    return (
        layer_out, input_grad, first_grad, grad_q, grad_kv, grad_o, second_grad, router_grad, ex_in, ex_out,
    )


def solution(mesh):
    grid = Mesh(mesh.devices.reshape(2, 4, 4, 4), ("section", "y", "x", "expert"))
    ctx = ("y", "x")
    every = ("y", "x", "expert")
    placed = (
        P(None, "expert", ctx, None),
        P(None, "expert", ctx),
        P("section", None, "expert", ctx, None),
        P(None, "expert", ctx, None),
        P("section", None),
        P("section", None, None),
        P("section", None, None),
        P("section", None, None),
        P("section", None),
        P("section", None, None),
        P("section", "expert", None, None),
        P("section", "expert", None, None),
    )
    return jax.shard_map(
        local,
        mesh=grid,
        in_specs=placed,
        out_specs=(
            P("section", None, "expert", ctx, None),
            P("section", None, "expert", ctx, None),
            P("section", every),
            P("section", every, None),
            P("section", every, None),
            P("section", every, None),
            P("section", every),
            P("section", every, None),
            P("section", "expert", ctx, None),
            P("section", "expert", ctx, None),
        ),
        check_vma=False,
    )
```
